512 devices in a mesh: dp: 16 (over z), bal: 32 (over y, x, core).
Axes of the slice: x: 4, y: 4, z: 16, core: 2. Of those that a mesh axis runs over, the one named last changes fastest.
Arguments:
- pixels: bfloat16 [163840, 588], P(('dp', 'bal'))
- latent: bfloat16 [1792, 588], replicated
- quant_scale: float32 [1792], replicated, as said below
- embed_bias: float32 [1792], replicated, may hold values from -6 to 6
- ln_gain: float32 [1792], replicated, may hold values from 0.5 to 1.5
- ln_bias: float32 [1792], replicated, may hold values from -3 to 3
- qkv_weight: bfloat16 [1792, 2688], P(None, 'dp'), may hold values from -0.1875 to 0.1875
- cotangent: bfloat16 [131072, 896], P(('dp', 'bal')), may hold values from -6 to 6
- image_length: int32 [16, 128], P('dp'), may hold values from 0 to 192, as said below
- image_source: int32 [16, 128], P('dp'), may hold values from 0 to 31, as said below
- image_target: int32 [16, 128], P('dp'), may hold values from 0 to 31
Outputs:
- attended: bfloat16 [131072, 896], P(('dp', 'bal'))
- grad_latent: float32 [1792, 588], P('bal')
- grad_scale: float32 [1792], P('bal')
The draws below stay inside these ranges and needn't reach their ends.
Inputs may be any that keep to these rules, and one draw needn't show every extreme that they name: `image_length`: entries of a group come in no fixed order; each length is a multiple of 64; 0 marks an unused entry. The entries bound for one device total at most 256 patches, and those held by one device at most 320; both are reached on some device of every group. Every device of a group sends exactly one image, of at most 128 patches, to one other device and receives exactly one image from one other device; all other entries have image_source equal to image_target. 128 is reached in every group. `quant_scale`: positive.
All inputs are finite; a program needn't handle non-finite values.
Results may differ from the reference program's by a relative error of at most 0.04.
Values may be sent and summed in bfloat16 or wider, within the bound.
A program may use at most 128 MiB of HBM per device.

```python
import math
import jax
import jax.numpy as jnp
from jax import lax

D = 1792
HEAD = 112
PIX = 588
HEADS = 8
BLK = 64
ENTRIES = 4
HD = 896
OUT_ROWS = 256
IN_ROWS = 320
MOVE_ROWS = 128
ROWS = 131072
SOURCE_ROWS = 163840
N_DP = 16
N_BAL = 32


pattern_table = [[1, 1, 1, 1], [1, 3, 0, 0], [2, 1, 1, 0], [1, 2, 1, 0], [2, 0, 1, 1], [1, 1, 2, 0], [2, 2, 0, 0], [1, 0, 2, 1], [2, 1, 0, 0], [1, 1, 1, 0], [2, 0, 0, 1], [1, 0, 0, 2]]


def one_group(key):
    key_cycle, key_pattern, key_order, key_fullest = jax.random.split(key, 4)
    devices = jnp.arange(N_BAL, dtype=jnp.int32)
    cycle_order = jax.random.permutation(key_cycle, N_BAL).astype(jnp.int32)
    cycle_place = jnp.zeros((N_BAL,), jnp.int32).at[cycle_order].set(devices)
    sender = cycle_order[(cycle_place + 1) % N_BAL]
    fullest = jax.random.randint(key_fullest, (), 0, N_BAL).astype(jnp.int32)
    receiver_of_fullest = cycle_order[(cycle_place[fullest] + N_BAL - 1) % N_BAL]
    sender_of_fullest = sender[fullest]
    pattern_pick = jax.random.randint(key_pattern, (N_BAL,), 0, len(pattern_table)).astype(jnp.int32)
    pattern_pick = jnp.where(devices == fullest, 0, pattern_pick)
    pattern_pick = jnp.where(devices == receiver_of_fullest, 2, pattern_pick)
    pattern_pick = jnp.where(devices == sender_of_fullest, 1, pattern_pick)
    blocks = jnp.array(pattern_table, jnp.int32)[pattern_pick]
    length = blocks * BLK
    target = jnp.broadcast_to(devices[:, None], (N_BAL, ENTRIES))
    source = target.at[:, 0].set(sender)
    shuffle = jax.random.permutation(key_order, N_BAL * ENTRIES).astype(jnp.int32)
    return (length.reshape(-1)[shuffle], source.reshape(-1)[shuffle], target.reshape(-1)[shuffle])


def placement(key):
    keys = jax.random.split(key, N_DP)
    return jax.vmap(one_group)(keys)


def quant_pair(key):
    key_scale, key_level, key_fraction = jax.random.split(key, 3)
    step_sizes = jnp.exp(jax.random.uniform(key_scale, (D,), jnp.float32, math.log(0.002), math.log(0.02)))
    levels_int = jax.random.randint(key_level, (D, PIX), -10, 10).astype(jnp.float32)
    fraction = jax.random.uniform(key_fraction, (D, PIX), jnp.float32, -0.4, 0.4)
    return (step_sizes, (levels_int + fraction) * step_sizes[:, None])


def draw_image_length(key, part):
    shared = placement(key)
    return shared[0]


def draw_image_source(key, part):
    shared = placement(key)
    return shared[1]


def draw_image_target(key, part):
    shared = placement(key)
    return shared[2]


def draw_quant_scale(key, part):
    shared = quant_pair(key)
    return shared[0]


def draw_latent(key, part):
    shared = quant_pair(key)
    return shared[1].astype(jnp.bfloat16)


def draw_pixels(key, part):
    key = jax.random.fold_in(key, 6)
    key_base, key_row, key_column = jax.random.split(key, 3)
    base_values = jax.random.normal(key_base, (SOURCE_ROWS, PIX), jnp.float32)
    row_scale = jnp.exp(jax.random.uniform(key_row, (SOURCE_ROWS,), jnp.float32, math.log(0.3), math.log(3.0)))
    column_scale = jnp.exp(jax.random.uniform(key_column, (PIX,), jnp.float32, math.log(0.5), math.log(2.0)))
    return (base_values * row_scale[:, None] * column_scale[None, :]).astype(jnp.bfloat16)


def shard_levels(own_key, dims, shards, low, largest):
    gain = 1.0
    for dim, blocks in shards:
        steps = jax.random.uniform(jax.random.fold_in(jax.random.fold_in(own_key, 6), dim), (blocks,), jnp.float32, low / len(shards), largest / len(shards))
        gain = gain * jnp.repeat(jnp.exp(steps), dims[dim] // blocks).reshape((-1,) + (1,) * (len(dims) - 1 - dim))
    return gain


def centred(stream_key, extent, spread, bound, cuts=(), kind=jnp.bfloat16):
    values = jax.random.normal(stream_key, extent, jnp.float32) * spread
    if len(cuts) > 0:
        values = shard_levels(stream_key, extent, cuts, -0.22, 0.18) * values
    return jnp.clip(values, min=-bound, max=bound).astype(kind)


def setup_inputs(seed: int = 0) -> dict:
    splits = jax.random.split(jax.random.key(seed), 12)
    pixels = draw_pixels(jax.random.fold_in(splits[11], 71), 0)
    latent = draw_latent(jax.random.fold_in(splits[11], 71), 0)
    quant_scale = draw_quant_scale(jax.random.fold_in(splits[11], 71), 0)
    embed_bias = centred(splits[3], (D,), 1.0, 6.0, (), jnp.float32)
    ln_gain = jnp.clip(jax.random.uniform(splits[4], (D,), jnp.float32, 0.5, 1.5), 0.5, 1.5)
    ln_bias = centred(splits[5], (D,), 0.5, 3.0, (), jnp.float32)
    qkv_weight = centred(splits[6], (D, 3 * HD), (D // 2) ** -0.5, 0.1875, ((1, 16),))
    cotangent = centred(splits[7], (ROWS, HD), 1.0, 6.0, ((0, 512),))
    image_length = draw_image_length(jax.random.fold_in(splits[11], 71), 0)
    image_source = draw_image_source(jax.random.fold_in(splits[11], 71), 0)
    image_target = draw_image_target(jax.random.fold_in(splits[11], 71), 0)
    return {"pixels": pixels, "latent": latent, "quant_scale": quant_scale, "embed_bias": embed_bias, "ln_gain": ln_gain, "ln_bias": ln_bias, "qkv_weight": qkv_weight, "cotangent": cotangent, "image_length": image_length, "image_source": image_source, "image_target": image_target}


EPSILON = 1e-06

def quantize(latent, quant_scale):
    ratio = latent.astype(jnp.float32) / quant_scale[:, None]
    level = jnp.floor(ratio + 0.5)
    inside = (level >= -8.0) & (level <= 7.0)
    clipped = jnp.clip(level, -8.0, 7.0)
    quant_weight = (clipped * quant_scale[:, None]).astype(jnp.bfloat16)
    scale_slope = jnp.where(inside, level - ratio, clipped)
    return (quant_weight, inside, scale_slope)

def arrange(length, source, target, member, out_rows, move_rows):
    entries = length.shape[0]
    entry_index = jnp.arange(entries, dtype=jnp.int32)
    before = entry_index[:, None] > entry_index[None, :]
    moving = target != source

    def earlier_total(owner, amounts):
        matching = before & (owner[:, None] == owner[None, :])
        return lax.optimization_barrier(jnp.sum(jnp.where(matching, amounts[None, :], 0), axis=1)).astype(jnp.int32)
    target_start = earlier_total(target, length)
    source_start = earlier_total(source, length)
    outbox_start = earlier_total(source, jnp.where(moving, length, 0).astype(jnp.int32))
    row_index = jnp.arange(out_rows, dtype=jnp.int32)[:, None]
    covers = (target[None, :] == member) & (row_index >= target_start[None, :]) & (row_index < (target_start + length)[None, :])

    def select_rows(values):
        return lax.optimization_barrier(jnp.sum(jnp.where(covers, values[None, :], 0), axis=1)).astype(jnp.int32)
    active = jnp.any(covers, axis=1)
    image_id = select_rows(entry_index)
    within = (row_index[:, 0] - select_rows(target_start)).astype(jnp.int32)
    from_device = select_rows(source)
    from_row = (select_rows(source_start) + within).astype(jnp.int32)
    outbox_row = (select_rows(outbox_start) + within).astype(jnp.int32)
    slot_index = jnp.arange(move_rows, dtype=jnp.int32)[:, None]
    leaving = (source[None, :] == member) & moving[None, :] & (slot_index >= outbox_start[None, :]) & (slot_index < (outbox_start + length)[None, :])
    leaving_row = (lax.optimization_barrier(jnp.sum(jnp.where(leaving, (source_start - outbox_start)[None, :], 0), axis=1)) + slot_index[:, 0]).astype(jnp.int32)
    leaving_active = jnp.any(leaving, axis=1)
    return (active, image_id, from_device, from_row, outbox_row, leaving_active, leaving_row)

def forward_backward(target_pixels, active, same_image, quant_weight, embed_bias, ln_gain, ln_bias, qkv_weight, cot_rows, grad_factor):
    proj_width = HEADS * HEAD
    score_scale = HEAD ** (-0.5)
    embedded = (jnp.dot(target_pixels, quant_weight.T, preferred_element_type=jnp.float32) + embed_bias).astype(jnp.bfloat16)
    values_row = embedded.astype(jnp.float32)
    row_mean = lax.optimization_barrier(jnp.mean(values_row, axis=1, keepdims=True))
    centered = values_row - row_mean
    variance = lax.optimization_barrier(jnp.mean(centered * centered, axis=1, keepdims=True))
    inverse_std = lax.rsqrt(variance + EPSILON)
    centered_scaled = centered * inverse_std
    normed = (centered_scaled * ln_gain + ln_bias).astype(jnp.bfloat16)
    projected = jnp.dot(normed, qkv_weight, preferred_element_type=jnp.float32).astype(jnp.bfloat16)
    row_count = projected.shape[0]
    queries = projected[:, :proj_width].reshape(row_count, HEADS, HEAD).astype(jnp.float32)
    key_rows = projected[:, proj_width:2 * proj_width].reshape(row_count, HEADS, HEAD).astype(jnp.float32)
    value_rows = projected[:, 2 * proj_width:].reshape(row_count, HEADS, HEAD).astype(jnp.float32)
    scores = jnp.einsum('qhd,khd->hqk', queries, key_rows) * score_scale
    exponent = jnp.where(same_image[None], jnp.exp(scores), 0.0)
    denominator = lax.optimization_barrier(jnp.sum(exponent, axis=2, keepdims=True))
    denominator = jnp.where(active[None, :, None], denominator, 1.0)
    attention = exponent / denominator
    attention_soft = attention.astype(jnp.bfloat16).astype(jnp.float32)
    attended = jnp.einsum('hqk,khd->qhd', attention_soft, value_rows).reshape(row_count, proj_width)
    attended = jnp.where(active[:, None], attended, 0.0).astype(jnp.bfloat16)
    grad_out = jnp.where(active[:, None], cot_rows.astype(jnp.float32) * grad_factor, 0.0).astype(jnp.bfloat16)
    grad_out = grad_out.reshape(row_count, HEADS, HEAD).astype(jnp.float32)
    grad_values = jnp.einsum('hqk,qhd->khd', attention_soft, grad_out).astype(jnp.bfloat16)
    grad_attention = jnp.einsum('qhd,khd->hqk', grad_out, value_rows)
    row_inner = lax.optimization_barrier(jnp.sum(attention * grad_attention, axis=2, keepdims=True))
    grad_score = (attention * (grad_attention - row_inner) * score_scale).astype(jnp.bfloat16).astype(jnp.float32)
    grad_queries = jnp.einsum('hqk,khd->qhd', grad_score, key_rows).astype(jnp.bfloat16)
    grad_keys = jnp.einsum('hqk,qhd->khd', grad_score, queries).astype(jnp.bfloat16)
    grad_projected = jnp.concatenate([grad_queries.reshape(row_count, proj_width), grad_keys.reshape(row_count, proj_width), grad_values.reshape(row_count, proj_width)], axis=1)
    grad_normed = jnp.dot(grad_projected, qkv_weight.T, preferred_element_type=jnp.float32)
    gained = grad_normed * ln_gain
    grad_rows = inverse_std * (gained - lax.optimization_barrier(jnp.mean(gained, axis=1, keepdims=True)) - centered_scaled * lax.optimization_barrier(jnp.mean(gained * centered_scaled, axis=1, keepdims=True)))
    grad_embedded = jnp.where(active[:, None], grad_rows, 0.0).astype(jnp.bfloat16)
    return (attended, grad_embedded)

def reference(pixels, latent, quant_scale, embed_bias, ln_gain, ln_bias, qkv_weight, cotangent, image_length, image_source, image_target):
    quant_weight, inside, scale_slope = quantize(latent, quant_scale)
    grad_factor = 1.0 / math.sqrt(ROWS)
    lsq_factor = 1.0 / math.sqrt(PIX * 7.0)

    def device_step(summed, device_id):
        group_id = (device_id // N_BAL).astype(jnp.int32)
        member = (device_id % N_BAL).astype(jnp.int32)
        length = lax.dynamic_index_in_dim(image_length, group_id, 0, keepdims=False)
        source = lax.dynamic_index_in_dim(image_source, group_id, 0, keepdims=False)
        target = lax.dynamic_index_in_dim(image_target, group_id, 0, keepdims=False)
        active, image_id, from_device, from_row, outbox_row, leaving_active, leaving_row = arrange(length, source, target, member, OUT_ROWS, MOVE_ROWS)
        global_row = ((group_id * N_BAL + from_device) * IN_ROWS + from_row).astype(jnp.int32)
        taken = jnp.take(pixels, jnp.where(active, global_row, 0).astype(jnp.int32), axis=0)
        target_pixels = jnp.where(active[:, None], taken, jnp.zeros((), pixels.dtype))
        same_image = (image_id[:, None] == image_id[None, :]) & active[:, None] & active[None, :]
        cot_rows = lax.dynamic_slice_in_dim(cotangent, (device_id * OUT_ROWS).astype(jnp.int32), OUT_ROWS, 0)
        attended, grad_embedded = forward_backward(target_pixels, active, same_image, quant_weight, embed_bias, ln_gain, ln_bias, qkv_weight, cot_rows, grad_factor)
        device_grad = jnp.dot(grad_embedded.T, target_pixels, preferred_element_type=jnp.float32)
        rounded = lax.optimization_barrier(device_grad.astype(jnp.bfloat16)).astype(jnp.float32)
        return (summed + rounded, attended)
    device_ids = jnp.arange(N_DP * N_BAL, dtype=jnp.int32)
    summed, attended = lax.scan(device_step, jnp.zeros((D, PIX), jnp.float32), device_ids)
    attended = attended.reshape(ROWS, HEADS * HEAD)
    grad_latent = jnp.where(inside, summed, 0.0)
    grad_scale = lsq_factor * lax.optimization_barrier(jnp.sum(summed * scale_slope, axis=1))
    return (attended, grad_latent, grad_scale)
```

```python
import functools
import math

import jax
import jax.numpy as jnp
from jax import lax
from jax.experimental import pallas as pl
from jax.experimental.pallas import tpu as pltpu
from jax.sharding import PartitionSpec as P

D = 1792
HEAD = 112
PIX = 588
HEADS = 8
MOVE_ROWS = 128


EPSILON = 1e-06


def quantize(latent, quant_scale):
    ratio = latent.astype(jnp.float32) / quant_scale[:, None]
    level = jnp.floor(ratio + 0.5)
    inside = (level >= -8.0) & (level <= 7.0)
    clipped = jnp.clip(level, -8.0, 7.0)
    quant_weight = (clipped * quant_scale[:, None]).astype(jnp.bfloat16)
    scale_slope = jnp.where(inside, level - ratio, clipped)
    return (quant_weight, inside, scale_slope)


def arrange(length, source, target, member, out_rows, move_rows):
    entries = length.shape[0]
    entry_index = jnp.arange(entries, dtype=jnp.int32)
    before = entry_index[:, None] > entry_index[None, :]
    moving = target != source

    def earlier_total(owner, amounts):
        matching = before & (owner[:, None] == owner[None, :])
        return jnp.sum(jnp.where(matching, amounts[None, :], 0), axis=1)

    target_start = earlier_total(target, length)
    source_start = earlier_total(source, length)
    outbox_start = earlier_total(source, jnp.where(moving, length, 0))
    row_index = jnp.arange(out_rows, dtype=jnp.int32)[:, None]
    covers = (
        (target[None, :] == member)
        & (row_index >= target_start[None, :])
        & (row_index < (target_start + length)[None, :])
    )

    def select_rows(values):
        return jnp.sum(jnp.where(covers, values[None, :], 0), axis=1)

    active = jnp.any(covers, axis=1)
    image_id = select_rows(entry_index)
    within = row_index[:, 0] - select_rows(target_start)
    from_device = select_rows(source)
    from_row = select_rows(source_start) + within
    outbox_row = select_rows(outbox_start) + within
    slot_index = jnp.arange(move_rows, dtype=jnp.int32)[:, None]
    leaving = (
        (source[None, :] == member)
        & moving[None, :]
        & (slot_index >= outbox_start[None, :])
        & (slot_index < (outbox_start + length)[None, :])
    )
    leaving_row = (
        jnp.sum(jnp.where(leaving, (source_start - outbox_start)[None, :], 0), axis=1)
        + slot_index[:, 0]
    )
    leaving_active = jnp.any(leaving, axis=1)
    return (active, image_id, from_device, from_row, outbox_row, leaving_active, leaving_row)


def forward_backward(
    target_pixels,
    active,
    same_image,
    quant_weight,
    embed_bias,
    ln_gain,
    ln_bias,
    project_forward,
    project_backward,
    cot_rows,
    grad_factor,
):
    proj_width = HEADS * HEAD
    score_scale = HEAD ** (-0.5)
    embedded = (
        lax.dot_general(
            target_pixels,
            quant_weight,
            (((1,), (1,)), ((), ())),
            preferred_element_type=jnp.float32,
        )
        + embed_bias
    ).astype(jnp.bfloat16)
    values_row = embedded.astype(jnp.float32)
    row_mean = jnp.mean(values_row, axis=1, keepdims=True)
    centered = values_row - row_mean
    variance = jnp.mean(centered * centered, axis=1, keepdims=True)
    inverse_std = lax.rsqrt(variance + EPSILON)
    centered_scaled = centered * inverse_std
    normed = (centered_scaled * ln_gain + ln_bias).astype(jnp.bfloat16)
    projected = project_forward(normed).astype(jnp.bfloat16)
    row_count = projected.shape[0]
    queries = projected[:, :proj_width].reshape(row_count, HEADS, HEAD)
    key_rows = projected[:, proj_width : 2 * proj_width].reshape(row_count, HEADS, HEAD)
    value_rows = projected[:, 2 * proj_width :].reshape(row_count, HEADS, HEAD)
    scores = (
        jnp.einsum("qhd,khd->hqk", queries, key_rows, preferred_element_type=jnp.float32)
        * score_scale
    )
    exponent = jnp.where(same_image[None], jnp.exp(scores), 0.0)
    denominator = jnp.sum(exponent, axis=2, keepdims=True)
    denominator = jnp.where(active[None, :, None], denominator, 1.0)
    attention = exponent / denominator
    attention_soft = attention.astype(jnp.bfloat16)
    attended = jnp.einsum(
        "hqk,khd->qhd", attention_soft, value_rows, preferred_element_type=jnp.float32
    ).reshape(row_count, proj_width)
    attended = jnp.where(active[:, None], attended, 0.0).astype(jnp.bfloat16)
    grad_out = jnp.where(active[:, None], cot_rows.astype(jnp.float32) * grad_factor, 0.0).astype(
        jnp.bfloat16
    )
    grad_out = grad_out.reshape(row_count, HEADS, HEAD)
    grad_values = jnp.einsum(
        "hqk,qhd->khd", attention_soft, grad_out, preferred_element_type=jnp.float32
    ).astype(jnp.bfloat16)
    grad_attention = jnp.einsum(
        "qhd,khd->hqk", grad_out, value_rows, preferred_element_type=jnp.float32
    )
    row_inner = jnp.sum(attention * grad_attention, axis=2, keepdims=True)
    grad_score = (attention * (grad_attention - row_inner) * score_scale).astype(jnp.bfloat16)
    grad_queries = jnp.einsum(
        "hqk,khd->qhd", grad_score, key_rows, preferred_element_type=jnp.float32
    ).astype(jnp.bfloat16)
    grad_keys = jnp.einsum(
        "hqk,qhd->khd", grad_score, queries, preferred_element_type=jnp.float32
    ).astype(jnp.bfloat16)
    grad_projected = jnp.concatenate(
        [
            grad_queries.reshape(row_count, proj_width),
            grad_keys.reshape(row_count, proj_width),
            grad_values.reshape(row_count, proj_width),
        ],
        axis=1,
    )
    grad_normed = project_backward(grad_projected)
    gained = grad_normed * ln_gain
    grad_rows = inverse_std * (
        gained
        - jnp.mean(gained, axis=1, keepdims=True)
        - centered_scaled * jnp.mean(gained * centered_scaled, axis=1, keepdims=True)
    )
    grad_embedded = jnp.where(active[:, None], grad_rows, 0.0).astype(jnp.bfloat16)
    return (attended, grad_embedded)


MESH = pl.DeviceIdType.MESH
SHARD = 168
CHIP_ROWS = 112
HALF_COLS = 8 * SHARD
PIX_PAD = 640
PIECES = 20
GROUP_ROWS = ((0, 64, 32), (64, 48, 32))


def place():
    z = lax.axis_index("dp")
    b = lax.axis_index("bal")
    core = lax.rem(b, 2)
    x = lax.rem(b // 2, 4)
    y = b // 8
    return z, b, x, y, core


def remote(src, dst, send, recv, device):
    copy = pltpu.make_async_remote_copy(
        src_ref=src, dst_ref=dst, send_sem=send, recv_sem=recv, device_id=device, device_id_type=MESH
    )
    return copy


def gather_kernel(
    w_ref,
    pieces_ref,
    source_ref,
    weight_ref,
    arrived_ref,
    ring,
    inbox,
    stage,
    ring_send,
    ring_recv,
    out_send,
    out_recv,
    back_send,
    back_recv,
    plane_send,
    plane_recv,
    pair_send,
    pair_recv,
):
    z, b, x, y, core = place()
    up = lax.rem(z + 1, 16)
    down = lax.rem(z + 15, 16)
    direction = 1 - 2 * core
    ring_to = lax.rem(z + direction + 16, 16)
    sibling = b + 1 - 2 * core
    chip = b // 2

    barrier = pltpu.get_barrier_semaphore()

    def greet(step, carry):
        pl.semaphore_signal(
            barrier, inc=1, device_id=(z, lax.rem(b + step, 32)), device_id_type=MESH
        )
        return carry

    lax.fori_loop(1, 32, greet, 0)
    for other in (up, down):
        pl.semaphore_signal(barrier, inc=1, device_id=(other, b), device_id_type=MESH)
    pl.semaphore_wait(barrier, 33)

    chip_rows = pl.ds(pl.multiple_of(chip * CHIP_ROWS, 16), CHIP_ROWS)
    ring[0] = w_ref[chip_rows, :]

    def ring_copy(step):
        return remote(
            ring.at[step],
            ring.at[step + 1],
            ring_send.at[step],
            ring_recv.at[step + 1],
            (ring_to, b),
        )

    def out_copy(target, slot):
        return remote(
            pieces_ref.at[target], inbox.at[slot], out_send.at[target], out_recv.at[slot], (z, target)
        )

    def back_copy(target, slot):
        return remote(
            stage.at[target],
            arrived_ref.at[slot],
            back_send.at[target],
            back_recv.at[slot],
            (z, target),
        )

    ring_copy(0).start()

    def send_out(step, carry):
        target = lax.rem(b + step, 32)

        @pl.when(target < PIECES)
        def _():
            out_copy(target, b).start()

        return carry

    lax.fori_loop(1, 32, send_out, 0)
    ring_copy(0).wait_recv()
    ring_copy(1).start()

    @pl.when(b < PIECES)
    def _():
        inbox[b] = pieces_ref[b]

        def take(step, carry):
            out_copy(b, lax.rem(b + step, 32)).wait_recv()
            return carry

        lax.fori_loop(1, 32, take, 0)

    ring_copy(1).wait_recv()
    ring_copy(2).start()

    @pl.when(b < PIECES)
    def _():
        arrived_ref[b] = inbox[source_ref[b]]

        def send_back(step, carry):
            target = lax.rem(b + step, 32)
            stage[target] = inbox[source_ref[target]]
            back_copy(target, b).start()
            return carry

        lax.fori_loop(1, 32, send_back, 0)

    for step in range(3, 7):
        ring_copy(step - 1).wait_recv()
        ring_copy(step).start()
    ring_copy(6).wait_recv()

    @pl.when(core == 0)
    def _():
        ring_copy(7).start()
        ring_copy(7).wait_recv()

    parts = []
    for j in range(8):
        below = lax.rem(z - j - 1 + 16, 8) + 1
        above = lax.rem(j - z + 16, 8)
        parts.append(ring[below * (1 - core) + above * core])
    weight_ref[core, chip_rows, :] = jnp.concatenate(parts, axis=1)

    def chip_at(group, first, second):
        swap = lax.rem(core + group, 2)
        dx = first * (1 - swap) + second * swap
        dy = first * swap + second * (1 - swap)
        return lax.rem(y + dy + 4, 4) * 4 + lax.rem(x + dx + 4, 4)

    def block(group, where, low=0, count=None):
        start, rows, _ = GROUP_ROWS[group]
        if count is None:
            count = rows - low
        first = pl.multiple_of(where * CHIP_ROWS + start + low, 16)
        return weight_ref.at[core, pl.ds(first, count), :]

    def plane_copy(group, index, sent, to, low=0, count=None):
        rows = block(group, sent, low, count)
        return remote(
            rows,
            rows,
            plane_send.at[group, index],
            plane_recv.at[group, index],
            (z, to * 2 + core),
        )

    offsets = (0, -1, 1, 2)

    def first_copy(group, kind, origin=0):
        lower = GROUP_ROWS[group][2]
        to = chip_at(group, 1 if kind in (0, 2) else -1, 0)
        sent = chip_at(group, (0, 0, -1, 1)[kind] + origin, 0)
        low, count = ((0, None), (0, None), (0, lower), (lower, None))[kind]
        return plane_copy(group, kind, sent, to, low, count)

    def first_wait(group, kind):
        lower = GROUP_ROWS[group][2]
        low, count = ((0, None), (0, None), (0, lower), (lower, None))[kind]
        sent = chip_at(group, (-1, 1, 2, 2)[kind], 0)
        plane_copy(group, kind, sent, 0, low, count).wait_recv()

    def second_copy(group, place_index, kind):
        lower = GROUP_ROWS[group][2]
        a = offsets[place_index]
        to = chip_at(group, 0, 1 if kind in (0, 2) else -1)
        sent = chip_at(group, a, (0, 0, -1, 1)[kind])
        low, count = ((0, None), (0, None), (0, lower), (lower, None))[kind]
        return plane_copy(group, 4 + 4 * place_index + kind, sent, to, low, count)

    def second_wait(group, place_index, kind):
        lower = GROUP_ROWS[group][2]
        a = offsets[place_index]
        low, count = ((0, None), (0, None), (0, lower), (lower, None))[kind]
        sent = chip_at(group, a, (-1, 1, 2, 2)[kind])
        plane_copy(group, 4 + 4 * place_index + kind, sent, 0, low, count).wait_recv()

    def pair_copy(group, place_index, second_index):
        rows = block(group, chip_at(group, offsets[place_index], offsets[second_index]))
        index = place_index * 4 + second_index
        return remote(
            rows, rows, pair_send.at[group, index], pair_recv.at[group, index], (z, sibling)
        )

    groups = (0, 1)
    for g in groups:
        first_copy(g, 0).start()
        first_copy(g, 1).start()
    for g in groups:
        second_copy(g, 0, 0).start()
        second_copy(g, 0, 1).start()
        pair_copy(g, 0, 0).start()
    for kind, index in ((0, 1), (1, 2)):
        for g in groups:
            first_wait(g, kind)
            first_copy(g, kind + 2).start()
            second_copy(g, index, 0).start()
            second_copy(g, index, 1).start()
            pair_copy(g, index, 0).start()
    for g in groups:
        first_wait(g, 2)
        first_wait(g, 3)
        second_copy(g, 3, 0).start()
        second_copy(g, 3, 1).start()
        pair_copy(g, 3, 0).start()
    for index in range(4):
        for kind in (0, 1):
            for g in groups:
                second_wait(g, index, kind)
                second_copy(g, index, kind + 2).start()
                pair_copy(g, index, kind + 1).start()
    for index in range(4):
        for g in groups:
            second_wait(g, index, 2)
            second_wait(g, index, 3)
            pair_copy(g, index, 3).start()

    for step in range(7):
        ring_copy(step).wait_send()

    @pl.when(core == 0)
    def _():
        ring_copy(7).wait_send()

    def sent_out(step, carry):
        target = lax.rem(b + step, 32)

        @pl.when(target < PIECES)
        def _():
            out_copy(target, b).wait_send()

        return carry

    lax.fori_loop(1, 32, sent_out, 0)

    @pl.when(b < PIECES)
    def _():
        def sent_back(step, carry):
            back_copy(lax.rem(b + step, 32), b).wait_send()
            return carry

        lax.fori_loop(1, 32, sent_back, 0)

    def arrive(step, carry):
        slot = lax.rem(b + step, 32)

        @pl.when(slot < PIECES)
        def _():
            back_copy(b, slot).wait_recv()

        return carry

    lax.fori_loop(1, 32, arrive, 0)
    for g in groups:
        for kind in range(4):
            first_copy(g, kind).wait_send()
            for index in range(4):
                second_copy(g, index, kind).wait_send()
        for index in range(4):
            for second in range(4):
                pair_copy(g, index, second).wait_send()
                start, rows, _ = GROUP_ROWS[g]
                swap = 1 - lax.rem(core + g, 2)
                dx = offsets[index] * (1 - swap) + offsets[second] * swap
                dy = offsets[index] * swap + offsets[second] * (1 - swap)
                where = lax.rem(y + dy + 4, 4) * 4 + lax.rem(x + dx + 4, 4)
                first = pl.multiple_of(where * CHIP_ROWS + start, 16)
                rows_ref = weight_ref.at[1 - core, pl.ds(first, rows), :]
                remote(
                    rows_ref,
                    rows_ref,
                    pair_send.at[g, index * 4 + second],
                    pair_recv.at[g, index * 4 + second],
                    (z, sibling),
                ).wait_recv()


def gather_weight(weight, pieces, source):
    vmem = pl.BlockSpec(memory_space=pltpu.VMEM)
    dma = pltpu.SemaphoreType.DMA
    return pl.pallas_call(
        gather_kernel,
        name="gather_weight",
        out_shape=(
            jax.ShapeDtypeStruct((2, D, HALF_COLS), jnp.bfloat16),
            jax.ShapeDtypeStruct((PIECES, 32, 128), jnp.bfloat16),
        ),
        in_specs=[vmem, vmem, pl.BlockSpec(memory_space=pltpu.SMEM)],
        out_specs=(vmem, vmem),
        scratch_shapes=[
            pltpu.VMEM((9, CHIP_ROWS, SHARD), jnp.bfloat16),
            pltpu.VMEM((32, 32, 128), jnp.bfloat16),
            pltpu.VMEM((32, 32, 128), jnp.bfloat16),
            dma((9,)),
            dma((9,)),
            dma((32,)),
            dma((32,)),
            dma((32,)),
            dma((32,)),
            dma((2, 20)),
            dma((2, 20)),
            dma((2, 16)),
            dma((2, 16)),
        ],
        compiler_params=pltpu.CompilerParams(
            collective_id=0, has_side_effects=True, vmem_limit_bytes=40 * 1024 * 1024
        ),
    )(weight, pieces, source)


def reduce_kernel(
    grad_ref,
    out_ref,
    twin,
    held,
    across,
    line,
    met,
    tiles,
    total,
    result,
    twin_send,
    twin_recv,
    across_send,
    across_recv,
    line_send,
    line_recv,
    tile_send,
    tile_recv,
    total_send,
    total_recv,
    last_send,
    last_recv,
):
    z, b, x, y, core = place()
    sibling = b + 1 - 2 * core
    first = x * (1 - core) + y * core
    second = y * (1 - core) + x * core

    def chip_of(which, f, s):
        return (s * 4 + f) * (1 - which) + (f * 4 + s) * which

    def target_chip(which, a, half):
        mine = x * (1 - which) + y * which
        f = lax.rem(mine + a, 4)
        return chip_of(which, f, 2 * half + lax.rem(f + which, 2))

    def at(f, s):
        return (z, chip_of(core, f, s) * 2 + core)

    barrier = pltpu.get_barrier_semaphore()
    pl.semaphore_signal(barrier, inc=1, device_id=(z, sibling), device_id_type=MESH)
    for a in range(1, 4):
        pl.semaphore_signal(
            barrier, inc=1, device_id=at(lax.rem(first + a, 4), second), device_id_type=MESH
        )
        pl.semaphore_signal(
            barrier, inc=1, device_id=at(first, lax.rem(second + a, 4)), device_id_type=MESH
        )

    def greet(step, carry):
        pl.semaphore_signal(
            barrier, inc=1, device_id=(lax.rem(z + step, 16), b), device_id_type=MESH
        )
        return carry

    lax.fori_loop(1, 16, greet, 0)
    pl.semaphore_wait(barrier, 22)

    def twin_copy(a, half):
        chip = target_chip(1 - core, a, half)
        return remote(
            grad_ref.at[chip], twin.at[a, half], twin_send.at[a, half], twin_recv.at[a, half], (z, sibling)
        )

    order = (2, 1, 3, 0)
    for a in order:
        for half in range(2):
            twin_copy(a, half).start()

    def across_copy(a):
        return remote(
            held.at[a],
            across.at[a],
            across_send.at[a],
            across_recv.at[a],
            at(lax.rem(first + a, 4), second),
        )

    for a in order:
        for half in range(2):
            twin_copy(a, half).wait_recv()
            chip = target_chip(core, a, half)
            held[a, half] = (
                grad_ref[chip].astype(jnp.float32) + twin[a, half].astype(jnp.float32)
            ).astype(jnp.bfloat16)
        if a > 0:
            across_copy(a).start()
    for a in (1, 3, 2):
        across_copy(a).wait_recv()
    for half in range(2):
        line[half] = (
            held[0, half].astype(jnp.float32)
            + across[1, half].astype(jnp.float32)
            + across[2, half].astype(jnp.float32)
            + across[3, half].astype(jnp.float32)
        ).astype(jnp.bfloat16)

    parity = lax.rem(first + core, 2)
    owner = lax.rem(first + second, 2) == core

    def line_copy(half):
        to = 2 * half + parity
        away = lax.rem(to - second + 4, 4)
        return remote(
            line.at[half],
            met.at[away],
            line_send.at[half],
            line_recv.at[away],
            at(first, to),
        )

    for a in range(1, 4):
        across_copy(a).wait_send()
    for half in range(2):
        to = 2 * half + parity

        @pl.when(to != second)
        def _():
            line_copy(half).start()

    tile = total.shape[1]

    def tile_copy(index):
        to = 2 * index
        return remote(
            result.at[pl.ds(16 * index, 16)],
            tiles.at[z],
            tile_send.at[index],
            tile_recv.at[z],
            (to, b),
        )

    def tile_wait(slot):
        remote(
            result.at[pl.ds(0, 16)], tiles.at[slot], tile_send.at[0], tile_recv.at[slot], (slot, b)
        ).wait_recv()

    def total_copy(to, index):
        return remote(
            total.at[index],
            total.at[index],
            total_send.at[to],
            total_recv.at[index],
            (to, b),
        )

    @pl.when(owner)
    def _():
        mine = line[second // 2].astype(jnp.float32)
        for away in (1, 3, 2):
            remote(
                line.at[0], met.at[away], line_send.at[0], line_recv.at[away], (z, sibling)
            ).wait_recv()
            mine = mine + met[away].astype(jnp.float32)
        result[...] = mine.astype(jnp.bfloat16)
        for index in range(7):

            @pl.when(z != 2 * index)
            def _():
                tile_copy(index).start()

        @pl.when((z < 14) & (lax.rem(z, 2) == 0))
        def _():
            index = z // 2
            tiles[z] = result[pl.ds(pl.multiple_of(16 * index, 16), 16), :]

            def take(step, carry):
                tile_wait(lax.rem(z + step, 16))
                return carry

            lax.fori_loop(1, 16, take, 0)
            value = tiles[0].astype(jnp.float32)
            for slot in range(1, 16):
                value = value + tiles[slot].astype(jnp.float32)
            total[index] = value.astype(jnp.bfloat16)

            def spread(step, carry):
                total_copy(lax.rem(z + step, 16), index).start()
                return carry

            lax.fori_loop(1, 16, spread, 0)

        for index in range(7):

            @pl.when(z != 2 * index)
            def _():
                total_copy(0, index).wait_recv()

        remote(total, total, last_send, last_recv, (z, sibling)).start()

        for index in range(7):

            @pl.when(z != 2 * index)
            def _():
                tile_copy(index).wait_send()

        @pl.when((z < 14) & (lax.rem(z, 2) == 0))
        def _():
            def spent(step, carry):
                total_copy(lax.rem(z + step, 16), z // 2).wait_send()
                return carry

            lax.fori_loop(1, 16, spent, 0)

        remote(total, total, last_send, last_recv, (z, sibling)).wait_send()

    @pl.when(jnp.logical_not(owner))
    def _():
        remote(total, total, last_send, last_recv, (z, sibling)).wait_recv()

    for a in range(4):
        for half in range(2):
            twin_copy(a, half).wait_send()
    for half in range(2):
        to = 2 * half + parity

        @pl.when(to != second)
        def _():
            line_copy(half).wait_send()

    out_ref[...] = total[...]


def reduce_grad(grad):
    vmem = pl.BlockSpec(memory_space=pltpu.VMEM)
    dma = pltpu.SemaphoreType.DMA
    block = (CHIP_ROWS, PIX_PAD)
    return pl.pallas_call(
        reduce_kernel,
        name="reduce_grad",
        out_shape=jax.ShapeDtypeStruct((7, 16, PIX_PAD), jnp.bfloat16),
        in_specs=[vmem],
        out_specs=vmem,
        scratch_shapes=[
            pltpu.VMEM((4, 2) + block, jnp.bfloat16),
            pltpu.VMEM((4, 2) + block, jnp.bfloat16),
            pltpu.VMEM((4, 2) + block, jnp.bfloat16),
            pltpu.VMEM((2,) + block, jnp.bfloat16),
            pltpu.VMEM((4,) + block, jnp.bfloat16),
            pltpu.VMEM((16, 16, PIX_PAD), jnp.bfloat16),
            pltpu.VMEM((7, 16, PIX_PAD), jnp.bfloat16),
            pltpu.VMEM(block, jnp.bfloat16),
            dma((4, 2)),
            dma((4, 2)),
            dma((4,)),
            dma((4,)),
            dma((2,)),
            dma((4,)),
            dma((7,)),
            dma((16,)),
            dma((16,)),
            dma((7,)),
            dma,
            dma,
        ],
        compiler_params=pltpu.CompilerParams(
            collective_id=1, has_side_effects=True, vmem_limit_bytes=40 * 1024 * 1024
        ),
    )(grad)


def per_device(
    pixels,
    latent,
    quant_scale,
    embed_bias,
    ln_gain,
    ln_bias,
    qkv_weight,
    cotangent,
    image_length,
    image_source,
    image_target,
):
    member = lax.axis_index("bal")
    members = lax.axis_size("bal")
    groups = lax.axis_size("dp")
    out_rows = cotangent.shape[0]
    length = image_length[0]
    source = image_source[0]
    target = image_target[0]
    active, image_id, from_device, from_row, outbox_row, leaving_active, leaving_row = arrange(
        length, source, target, member, out_rows, MOVE_ROWS
    )
    padded = jnp.pad(pixels, ((0, 0), (0, PIX_PAD - PIX)))
    rows_in = jnp.arange(pixels.shape[0], dtype=jnp.int32)[None, :]
    leaving = leaving_active[:, None] & (leaving_row[:, None] == rows_in)
    outgoing = jnp.dot(
        leaving.astype(jnp.bfloat16), padded, preferred_element_type=jnp.float32
    ).astype(jnp.bfloat16)
    pieces = outgoing.reshape(4, 32, 5, 128).transpose(0, 2, 1, 3).reshape(PIECES, 32, 128)
    moving = (target != source) & (length > 0)
    receivers = jnp.arange(members, dtype=jnp.int32)[:, None]
    sender = jnp.sum(
        jnp.where((target[None, :] == receivers) & moving[None, :], source[None, :], 0), axis=1
    )
    weight, arrived = gather_weight(qkv_weight, pieces, sender)
    arrived_rows = arrived.reshape(4, 5, 32, 128).transpose(0, 2, 1, 3).reshape(MOVE_ROWS, PIX_PAD)
    remote_row = from_device != member
    wanted = jnp.where(remote_row, pixels.shape[0] + outbox_row, from_row)
    columns = jnp.arange(pixels.shape[0] + MOVE_ROWS, dtype=jnp.int32)[None, :]
    selector = (active[:, None] & (wanted[:, None] == columns)).astype(jnp.bfloat16)
    target_pixels = jnp.dot(
        selector, jnp.concatenate([padded, arrived_rows], axis=0), preferred_element_type=jnp.float32
    ).astype(jnp.bfloat16)
    same_image = (image_id[:, None] == image_id[None, :]) & active[:, None] & active[None, :]
    quant_weight, inside, scale_slope = quantize(latent, quant_scale)
    grad_factor = 1.0 / math.sqrt(groups * members * out_rows)
    lsq_factor = 1.0 / math.sqrt(PIX * 7.0)
    slot = jnp.arange(HALF_COLS, dtype=jnp.int32)[None, :] // SHARD
    plane = lax.axis_index("dp")
    low_first = lax.rem(plane - slot + 15, 16) < 8

    def project_forward(normed):
        zero = jnp.dot(normed, weight[0], preferred_element_type=jnp.float32)
        one = jnp.dot(normed, weight[1], preferred_element_type=jnp.float32)
        return jnp.concatenate(
            [jnp.where(low_first, zero, one), jnp.where(low_first, one, zero)], axis=1
        )

    def project_backward(grad_projected):
        low, high = grad_projected[:, :HALF_COLS], grad_projected[:, HALF_COLS:]
        zero, one = jnp.where(low_first, low, high), jnp.where(low_first, high, low)
        contract = (((1,), (1,)), ((), ()))
        return lax.dot_general(
            zero, weight[0], contract, preferred_element_type=jnp.float32
        ) + lax.dot_general(one, weight[1], contract, preferred_element_type=jnp.float32)

    attended, grad_embedded = forward_backward(
        target_pixels[:, :PIX],
        active,
        same_image,
        quant_weight,
        embed_bias,
        ln_gain,
        ln_bias,
        project_forward,
        project_backward,
        cotangent,
        grad_factor,
    )
    row_share = D // members
    device_grad = lax.dot_general(
        grad_embedded, target_pixels, (((0,), (0,)), ((), ())), preferred_element_type=jnp.float32
    )
    blocks = device_grad.astype(jnp.bfloat16).reshape(D // CHIP_ROWS, CHIP_ROWS, PIX_PAD)
    reduced = reduce_grad(blocks).reshape(CHIP_ROWS, PIX_PAD)
    summed = lax.dynamic_slice_in_dim(reduced, lax.rem(member, 2) * row_share, row_share, 0)
    summed = summed[:, :PIX].astype(jnp.float32)
    row_start = member * row_share
    inside_rows = lax.dynamic_slice_in_dim(inside, row_start, row_share, 0)
    grad_latent = jnp.where(inside_rows, summed, 0.0)
    slope_rows = lax.dynamic_slice_in_dim(scale_slope, row_start, row_share, 0)
    grad_scale = lsq_factor * jnp.sum(summed * slope_rows, axis=1)
    return (attended, grad_latent, grad_scale)


def solution(mesh):
    placed = (
        P(("dp", "bal"), None),
        P(),
        P(),
        P(),
        P(),
        P(),
        P(None, "dp"),
        P(("dp", "bal"), None),
        P("dp", None),
        P("dp", None),
        P("dp", None),
    )
    return jax.shard_map(
        per_device,
        mesh=mesh,
        in_specs=placed,
        out_specs=(P(("dp", "bal"), None), P("bal", None), P("bal")),
        check_vma=False,
    )
```

```python
import math

import jax
import jax.numpy as jnp
from jax import lax
from jax.experimental import pallas as pl
from jax.experimental.pallas import tpu as pltpu
from jax.sharding import PartitionSpec as P

D = 1792
HEAD = 112
PIX = 588
HEADS = 8
MOVE_ROWS = 128
EPSILON = 1e-06
MESH = pl.DeviceIdType.MESH
SHARD = 168
MAIN = 128
REST_PAD = 48
CHIP_ROWS = 112
PIX_PAD = 640
PIECES = 20


def place():
    z = lax.axis_index("dp")
    b = lax.axis_index("bal")
    core = lax.rem(b, 2)
    x = lax.rem(b // 2, 4)
    y = b // 8
    return z, b, x, y, core


def remote(src, dst, send, recv, device):
    copy = pltpu.make_async_remote_copy(
        src_ref=src, dst_ref=dst, send_sem=send, recv_sem=recv, device_id=device, device_id_type=MESH
    )
    return copy


def gather_kernel(
    w_ref,
    latent_ref,
    scale_ref,
    bias_ref,
    gain_ref,
    shift_ref,
    pixels_ref,
    length_ref,
    source_ref,
    target_ref,
    sender_ref,
    main_out,
    rest_out,
    moved_ref,
    embedded_ref,
    projected_ref,
    column_id_ref,
    row_id_ref,
    main,
    rest,
    rows_in,
    pieces,
    inbox,
    stage,
    arrived,
    quant,
    normed,
    part_main,
    part_rest,
    z_send,
    z_recv,
    ring_send,
    ring_recv,
    hand_send,
    hand_recv,
    out_send,
    out_recv,
    back_send,
    back_recv,
    plane_send,
    plane_recv,
    pair_send,
    pair_recv,
    save_sem,
):
    z, b, x, y, core = place()
    sibling = b + 1 - 2 * core
    chip = b // 2
    quad = z // 4
    barrier = pltpu.get_barrier_semaphore()

    def greet_plane(step, carry):
        pl.semaphore_signal(
            barrier, inc=1, device_id=(z, lax.rem(b + step, 32)), device_id_type=MESH
        )
        return carry

    def greet_line(step, carry):
        pl.semaphore_signal(
            barrier, inc=1, device_id=(lax.rem(z + step, 16), b), device_id_type=MESH
        )
        return carry

    lax.fori_loop(1, 16, greet_line, 0)
    lax.fori_loop(1, 32, greet_plane, 0)

    def slice_rows(where):
        return pl.ds(pl.multiple_of((where // 2) * 16, 16), 16)

    def slice_lanes(where):
        return pl.ds(pl.multiple_of(lax.rem(where, 2) * 896, 128), 896)

    @pl.when(core == 0)
    def _():
        main[z, slice_rows(chip), slice_lanes(chip)] = w_ref[slice_rows(chip), slice_lanes(chip)]

    def rest_rows(plane):
        return pl.ds(pl.multiple_of(plane * REST_PAD, 16), REST_PAD)

    rest[rest_rows(z), :] = jnp.concatenate(
        [w_ref[pl.ds(MAIN, SHARD - MAIN), :], jnp.zeros((REST_PAD - SHARD + MAIN, D), jnp.bfloat16)],
        axis=0,
    )
    pl.semaphore_wait(barrier, 46)

    def z_copy(step):
        to = lax.rem(z + step, 16)
        return remote(
            w_ref.at[slice_rows(chip), slice_lanes(chip)],
            main.at[z, slice_rows(chip), slice_lanes(chip)],
            z_send.at[step],
            z_recv.at[z],
            (to, b),
        )

    def z_mine(step):
        return lax.rem(lax.rem(z + step, 16) // 4 + quad, 2) == core

    for step in (1, 15, 2, 14, 3, 13, 4, 12, 5, 11, 6, 10, 7, 9, 8):

        @pl.when(z_mine(step))
        def _():
            z_copy(step).start()

    def half_lanes(which, part):
        start, count = ((0, 512), (512, 384))[part]
        return pl.ds(pl.multiple_of(which * 896 + start, 128), count)

    def ring_copy(way, step, part):
        sign = 1 if way == 0 else -1
        origin = lax.rem(z - sign * (step - 1) + 16, 16)
        to = lax.rem(z + sign + 16, 16)
        block = rest.at[rest_rows(origin), half_lanes(core, part)]
        return remote(
            block, block, ring_send.at[way, step, part], ring_recv.at[way, step, part], (to, b)
        )

    def ring_wait(way, step, part):
        sign = 1 if way == 0 else -1
        origin = lax.rem(z - sign * step + 16, 16)
        block = rest.at[rest_rows(origin), half_lanes(core, part)]
        remote(
            block,
            block,
            ring_send.at[way, step, part],
            ring_recv.at[way, step, part],
            (lax.rem(z + 1, 16), b),
        ).wait_recv()

    def hand_copy(which, way, step):
        sign = 1 if way == 0 else -1
        origin = lax.rem(z - sign * step + 16, 16)
        block = rest.at[
            rest_rows(origin), pl.ds(pl.multiple_of(which * 896, 128), 896)
        ]
        return remote(
            block, block, hand_send.at[way, step], hand_recv.at[way, step], (z, sibling)
        )

    last = (8, 7)
    for part in range(2):
        for way in range(2):
            ring_copy(way, 1, part).start()

    def ring_step(step):
        for part in range(2):
            for way in range(2):
                if step <= last[way]:
                    ring_wait(way, step, part)
                    if step < last[way]:
                        ring_copy(way, step + 1, part).start()
        for way in range(2):
            if step <= last[way]:
                hand_copy(core, way, step).start()

    length_row = length_ref[...].astype(jnp.float32)
    source_row = source_ref[...].astype(jnp.float32)
    target_row = target_ref[...].astype(jnp.float32)
    entries = length_row.shape[1]

    def turned(row):
        return jnp.broadcast_to(row, (entries, entries)).T

    length_col, source_col, target_col = turned(length_row), turned(source_row), turned(target_row)
    down = lax.broadcasted_iota(jnp.int32, (entries, entries), 0)
    along = lax.broadcasted_iota(jnp.int32, (entries, entries), 1)
    member = b.astype(jnp.float32)

    def above(owner_col, owner_row, amount_col):
        match = (down < along) & (owner_col == owner_row)
        return jnp.sum(jnp.where(match, amount_col, 0.0), axis=0, keepdims=True)

    target_start = above(target_col, target_row, length_col)
    source_start = above(source_col, source_row, length_col)
    moving_col = jnp.where(target_col != source_col, length_col, 0.0)
    outbox_start = above(source_col, source_row, moving_col)
    before = (along < down) & (target_col == target_row)
    target_start_col = jnp.sum(jnp.where(before, length_row, 0.0), axis=1, keepdims=True)

    slots = lax.broadcasted_iota(jnp.int32, (MOVE_ROWS, entries), 0).astype(jnp.float32)
    leaving = (
        (source_row == member)
        & (target_row != source_row)
        & (slots >= outbox_start)
        & (slots < outbox_start + length_row)
    )
    leaving_row = jnp.sum(
        jnp.where(leaving, source_start - outbox_start + slots, 0.0), axis=1, keepdims=True
    )
    leaving_any = jnp.sum(jnp.where(leaving, 1.0, 0.0), axis=1, keepdims=True)
    leaving_row = jnp.where(leaving_any > 0.0, leaving_row, -1.0)
    count_in = pixels_ref.shape[0]
    rows_in[:, pl.ds(512, 128)] = jnp.zeros((rows_in.shape[0], 128), jnp.bfloat16)
    rows_in[pl.ds(0, count_in), pl.ds(0, PIX)] = pixels_ref[...]
    picks = lax.broadcasted_iota(jnp.int32, (MOVE_ROWS, count_in), 1).astype(jnp.float32)
    outgoing = jnp.dot(
        jnp.where(leaving_row == picks, 1.0, 0.0).astype(jnp.bfloat16),
        rows_in[pl.ds(0, count_in), :],
        preferred_element_type=jnp.float32,
    ).astype(jnp.bfloat16)
    for i in range(4):
        for j in range(5):
            pieces[5 * i + j] = outgoing[32 * i : 32 * i + 32, 128 * j : 128 * j + 128]

    def out_copy(target, slot):
        return remote(
            pieces.at[target], inbox.at[slot], out_send.at[target], out_recv.at[slot], (z, target)
        )

    def back_copy(target, slot):
        return remote(
            stage.at[target], arrived.at[slot], back_send.at[target], back_recv.at[slot], (z, target)
        )

    def send_out(step, carry):
        target = lax.rem(b + step, 32)

        @pl.when(target < PIECES)
        def _():
            out_copy(target, b).start()

        return carry

    lax.fori_loop(1, 32, send_out, 0)

    def quad_of(which, chunk):
        base = quad * (1 - which) + which * (quad + 3 + 2 * (lax.rem(z, 4) // 2))
        return lax.rem(base + 2 * chunk, 4)

    def chip_at(which, chunk, first, second):
        swap = lax.rem(which + chunk, 2)
        dx = first * (1 - swap) + second * swap
        dy = first * swap + second * (1 - swap)
        return lax.rem(y + dy + 4, 4) * 4 + lax.rem(x + dx + 4, 4)

    def piece(which, chunk, where, low=0, count=4):
        return main.at[
            pl.ds(4 * quad_of(which, chunk) + low, count), slice_rows(where), slice_lanes(where)
        ]

    offsets = (0, -1, 1, 2)
    spans = ((0, 4), (0, 4), (0, 2), (2, 2))

    def hop(chunk, index, axis, place_index, kind):
        low, count = spans[kind]
        sign = 1 if kind in (0, 2) else -1
        origin = (0, 0, -1, 1)[kind]
        a = offsets[place_index]
        if axis == 0:
            to, sent = chip_at(core, chunk, sign, 0), chip_at(core, chunk, origin, 0)
        else:
            to, sent = chip_at(core, chunk, 0, sign), chip_at(core, chunk, a, origin)
        rows = piece(core, chunk, sent, low, count)
        return remote(
            rows, rows, plane_send.at[chunk, index], plane_recv.at[chunk, index], (z, to * 2 + core)
        )

    def hop_wait(chunk, index, axis, place_index, kind):
        low, count = spans[kind]
        origin = (-1, 1, 2, 2)[kind]
        a = offsets[place_index]
        if axis == 0:
            sent = chip_at(core, chunk, origin, 0)
        else:
            sent = chip_at(core, chunk, a, origin)
        rows = piece(core, chunk, sent, low, count)
        remote(
            rows, rows, plane_send.at[chunk, index], plane_recv.at[chunk, index], (z, sibling)
        ).wait_recv()

    def first_copy(chunk, kind):
        return hop(chunk, kind, 0, 0, kind)

    def first_wait(chunk, kind):
        hop_wait(chunk, kind, 0, 0, kind)

    def second_copy(chunk, place_index, kind):
        return hop(chunk, 4 + 4 * place_index + kind, 1, place_index, kind)

    def second_wait(chunk, place_index, kind):
        hop_wait(chunk, 4 + 4 * place_index + kind, 1, place_index, kind)

    def pair_copy(which, chunk, place_index, second_index):
        rows = piece(
            which, chunk, chip_at(which, chunk, offsets[place_index], offsets[second_index])
        )
        index = place_index * 4 + second_index
        return remote(
            rows, rows, pair_send.at[chunk, index], pair_recv.at[chunk, index], (z, sibling)
        )

    def chunk_start(chunk):
        for j in range(4):
            origin = 4 * quad_of(core, chunk) + j

            @pl.when(origin != z)
            def _():
                rows = main.at[origin, slice_rows(chip), slice_lanes(chip)]
                remote(rows, rows, z_send.at[0], z_recv.at[origin], (z, sibling)).wait_recv()

        first_copy(chunk, 0).start()
        first_copy(chunk, 1).start()
        second_copy(chunk, 0, 0).start()
        second_copy(chunk, 0, 1).start()
        pair_copy(core, chunk, 0, 0).start()

    def chunk_first(chunk):
        for kind, index in ((0, 1), (1, 2)):
            first_wait(chunk, kind)
            first_copy(chunk, kind + 2).start()
            second_copy(chunk, index, 0).start()
            second_copy(chunk, index, 1).start()
            pair_copy(core, chunk, index, 0).start()

    def chunk_far(chunk):
        first_wait(chunk, 2)
        first_wait(chunk, 3)
        second_copy(chunk, 3, 0).start()
        second_copy(chunk, 3, 1).start()
        pair_copy(core, chunk, 3, 0).start()

    def chunk_second(chunk, index):
        for kind in (0, 1):
            second_wait(chunk, index, kind)
            second_copy(chunk, index, kind + 2).start()
            pair_copy(core, chunk, index, kind + 1).start()

    def chunk_last(chunk, index):
        second_wait(chunk, index, 2)
        second_wait(chunk, index, 3)
        pair_copy(core, chunk, index, 3).start()

    def quantize_part(part, carry):
        lanes = pl.ds(pl.multiple_of(part * 256, 128), 256)
        scale = scale_ref[:, lanes]
        level = jnp.floor(latent_ref[:, lanes].astype(jnp.float32) / scale + 0.5)
        quant[pl.ds(0, PIX), lanes] = (jnp.clip(level, -8.0, 7.0) * scale).astype(jnp.bfloat16)
        return carry

    def embed_part(part, carry):
        lanes = pl.ds(pl.multiple_of(part * 256, 128), 256)
        total = jnp.dot(moved_ref[...], quant[:, lanes], preferred_element_type=jnp.float32)
        embedded_ref[:, lanes] = (total + bias_ref[:, lanes]).astype(jnp.bfloat16)
        return carry

    def norm_part(part, carry):
        rows = pl.ds(pl.multiple_of(part * 32, 32), 32)
        values = embedded_ref[rows, :].astype(jnp.float32)
        centered = values - jnp.mean(values, axis=1, keepdims=True)
        variance = jnp.mean(centered * centered, axis=1, keepdims=True)
        hat = centered * lax.rsqrt(variance + EPSILON)
        normed[rows, :] = (hat * gain_ref[...] + shift_ref[...]).astype(jnp.bfloat16)
        return carry

    chunk_start(0)
    ring_step(1)

    @pl.when(b < PIECES)
    def _():
        inbox[b] = pieces[b]

        def take(step, carry):
            out_copy(b, lax.rem(b + step, 32)).wait_recv()
            return carry

        lax.fori_loop(1, 32, take, 0)
        arrived[b] = inbox[sender_ref[b]]

        def send_back(step, carry):
            target = lax.rem(b + step, 32)
            stage[target] = inbox[sender_ref[target]]
            back_copy(target, b).start()
            return carry

        lax.fori_loop(1, 32, send_back, 0)

    chunk_first(0)
    ring_step(2)
    quant[pl.ds(576, 64), :] = jnp.zeros((64, D), jnp.bfloat16)
    lax.fori_loop(0, 7, quantize_part, 0)
    chunk_far(0)
    chunk_second(0, 0)
    ring_step(3)

    row = lax.broadcasted_iota(jnp.int32, (moved_ref.shape[0], entries), 0).astype(jnp.float32)
    covers = (target_row == member) & (row >= target_start) & (row < target_start + length_row)
    take_from = (
        jnp.where(source_row == member, source_start, outbox_start + float(count_in)) - target_start
    )
    wanted = jnp.sum(jnp.where(covers, take_from + row, 0.0), axis=1, keepdims=True)
    entry = (lax.broadcasted_iota(jnp.int32, (1, entries), 1) + 1).astype(jnp.float32)
    image = jnp.sum(jnp.where(covers, entry, 0.0), axis=1, keepdims=True)
    wanted = jnp.where(image > 0.0, wanted, -1.0)
    column_id_ref[...] = image
    across = lax.broadcasted_iota(jnp.int32, (entries, moved_ref.shape[0]), 1).astype(jnp.float32)
    covers_turned = (
        (target_col[:, :1] == member)
        & (across >= target_start_col)
        & (across < target_start_col + length_col[:, :1])
    )
    entry_down = (lax.broadcasted_iota(jnp.int32, (entries, 1), 0) + 1).astype(jnp.float32)
    row_id_ref[...] = jnp.sum(jnp.where(covers_turned, entry_down, 0.0), axis=0, keepdims=True)

    def arrive(step, carry):
        slot = lax.rem(b + step, 32)

        @pl.when(slot < PIECES)
        def _():
            back_copy(b, slot).wait_recv()

        return carry

    lax.fori_loop(1, 32, arrive, 0)
    for i in range(4):
        for j in range(5):
            rows_in[pl.ds(count_in + 32 * i, 32), pl.ds(128 * j, 128)] = arrived[5 * i + j]
    choose = lax.broadcasted_iota(
        jnp.int32, (moved_ref.shape[0], count_in + MOVE_ROWS), 1
    ).astype(jnp.float32)
    moved_ref[...] = jnp.dot(
        jnp.where(wanted == choose, 1.0, 0.0).astype(jnp.bfloat16),
        rows_in[...],
        preferred_element_type=jnp.float32,
    ).astype(jnp.bfloat16)
    chunk_second(0, 1)
    chunk_start(1)
    ring_step(4)
    lax.fori_loop(0, 4, embed_part, 0)
    chunk_second(0, 2)
    chunk_first(1)
    ring_step(5)
    lax.fori_loop(4, 7, embed_part, 0)
    chunk_second(0, 3)
    chunk_far(1)
    chunk_second(1, 0)
    ring_step(6)
    lax.fori_loop(0, 4, norm_part, 0)
    chunk_second(1, 1)
    chunk_second(1, 2)
    ring_step(7)
    lax.fori_loop(4, 8, norm_part, 0)
    chunk_second(1, 3)
    for index in range(4):
        chunk_last(0, index)
    ring_step(8)
    for index in range(4):
        chunk_last(1, index)

    def project(which, chunk):
        q = quad_of(which, chunk)
        for pair in range(2):
            block = main[pl.ds(4 * q + 2 * pair, 2)].reshape(256, D)
            part_main[4 * q // 2 + pair] = lax.dot_general(
                normed[...], block, (((1,), (1,)), ((), ())), preferred_element_type=jnp.float32
            ).astype(jnp.bfloat16)

    def pair_wait(chunk):
        for index in range(4):
            for second in range(4):
                pair_copy(1 - core, chunk, index, second).wait_recv()

    project(core, 0)
    pair_wait(0)
    project(1 - core, 0)
    project(core, 1)
    pair_wait(1)
    save_main = pltpu.make_async_copy(main, main_out, save_sem.at[0])
    save_main.start()
    project(1 - core, 1)
    for way in range(2):
        for step in range(1, last[way] + 1):
            hand_copy(1 - core, way, step).wait_recv()
    save_rest = pltpu.make_async_copy(rest, rest_out, save_sem.at[1])
    save_rest.start()
    for part in range(3):
        part_rest[:, 256 * part : 256 * part + 256] = lax.dot_general(
            normed[...],
            rest[pl.ds(256 * part, 256), :],
            (((1,), (1,)), ((), ())),
            preferred_element_type=jnp.float32,
        ).astype(jnp.bfloat16)
    joined = []
    for plane in range(16):
        joined.append(part_main[plane // 2, :, 128 * (plane % 2) : 128 * (plane % 2) + 128])
        joined.append(part_rest[:, REST_PAD * plane : REST_PAD * plane + SHARD - MAIN])
    projected_ref[...] = jnp.concatenate(joined, axis=1)

    for step in range(1, 16):

        @pl.when(z_mine(step))
        def _():
            z_copy(step).wait_send()

    for way in range(2):
        for step in range(1, last[way] + 1):
            for part in range(2):
                ring_copy(way, step, part).wait_send()
            hand_copy(core, way, step).wait_send()

    def sent_out(step, carry):
        target = lax.rem(b + step, 32)

        @pl.when(target < PIECES)
        def _():
            out_copy(target, b).wait_send()

        return carry

    lax.fori_loop(1, 32, sent_out, 0)

    @pl.when(b < PIECES)
    def _():
        def sent_back(step, carry):
            back_copy(lax.rem(b + step, 32), b).wait_send()
            return carry

        lax.fori_loop(1, 32, sent_back, 0)

    for chunk in range(2):
        for kind in range(4):
            first_copy(chunk, kind).wait_send()
            for index in range(4):
                second_copy(chunk, index, kind).wait_send()
        for index in range(4):
            for second in range(4):
                pair_copy(core, chunk, index, second).wait_send()
    save_main.wait()
    save_rest.wait()


def gather_project(weight, latent, scale, bias, gain, shift, pixels, length, source, target, sender):
    vmem = pl.BlockSpec(memory_space=pltpu.VMEM)
    anywhere = pl.BlockSpec(memory_space=pl.ANY)
    dma = pltpu.SemaphoreType.DMA
    rows = 256
    shape = jax.ShapeDtypeStruct
    return pl.pallas_call(
        gather_kernel,
        name="gather_project",
        out_shape=(
            shape((16, MAIN, D), jnp.bfloat16),
            shape((16 * REST_PAD, D), jnp.bfloat16),
            shape((rows, PIX_PAD), jnp.bfloat16),
            shape((rows, D), jnp.bfloat16),
            shape((rows, 16 * SHARD), jnp.bfloat16),
            shape((rows, 1), jnp.float32),
            shape((1, rows), jnp.float32),
        ),
        in_specs=[vmem] * 10 + [pl.BlockSpec(memory_space=pltpu.SMEM)],
        out_specs=(anywhere, anywhere, vmem, vmem, vmem, vmem, vmem),
        scratch_shapes=[
            pltpu.VMEM((16, MAIN, D), jnp.bfloat16),
            pltpu.VMEM((16 * REST_PAD, D), jnp.bfloat16),
            pltpu.VMEM((pixels.shape[0] + MOVE_ROWS, PIX_PAD), jnp.bfloat16),
            pltpu.VMEM((PIECES, 32, 128), jnp.bfloat16),
            pltpu.VMEM((32, 32, 128), jnp.bfloat16),
            pltpu.VMEM((32, 32, 128), jnp.bfloat16),
            pltpu.VMEM((PIECES, 32, 128), jnp.bfloat16),
            pltpu.VMEM((PIX_PAD, D), jnp.bfloat16),
            pltpu.VMEM((rows, D), jnp.bfloat16),
            pltpu.VMEM((8, rows, 256), jnp.bfloat16),
            pltpu.VMEM((rows, 16 * REST_PAD), jnp.bfloat16),
            dma((16,)),
            dma((16,)),
            dma((2, 9, 2)),
            dma((2, 9, 2)),
            dma((2, 9)),
            dma((2, 9)),
            dma((32,)),
            dma((32,)),
            dma((32,)),
            dma((32,)),
            dma((2, 20)),
            dma((2, 20)),
            dma((2, 16)),
            dma((2, 16)),
            dma((2,)),
        ],
        compiler_params=pltpu.CompilerParams(
            collective_id=0, has_side_effects=True, vmem_limit_bytes=48 * 1024 * 1024
        ),
    )(weight, latent, scale, bias, gain, shift, pixels, length, source, target, sender)


def attention_kernel(
    projected_ref,
    column_id_ref,
    row_id_ref,
    cotangent_ref,
    embedded_ref,
    gain_ref,
    moved_ref,
    main_in,
    rest_in,
    attended_ref,
    grad_ref,
    main,
    rest,
    grad_out,
    attended,
    grad_projected,
    grad_main,
    grad_rest,
    grad_normed,
    grad_embedded,
    load_sem,
):
    load_main = pltpu.make_async_copy(main_in, main, load_sem.at[0])
    load_rest = pltpu.make_async_copy(rest_in, rest, load_sem.at[1])
    load_main.start()
    load_rest.start()
    width = HEADS * HEAD
    score_scale = HEAD ** (-0.5)
    grad_factor = 1.0 / math.sqrt(131072.0)
    column_id = column_id_ref[...]
    row_id = row_id_ref[...]
    active = column_id > 0.0
    same = (column_id == row_id) & active
    grad_out[...] = jnp.where(
        active, cotangent_ref[...].astype(jnp.float32) * grad_factor, 0.0
    ).astype(jnp.bfloat16)
    attended[...] = jnp.zeros_like(attended)
    grad_projected[...] = jnp.zeros_like(grad_projected)
    by_rows = (((1,), (1,)), ((), ()))
    by_columns = (((0,), (0,)), ((), ()))

    def dot(left, right, contract=(((1,), (0,)), ((), ()))):
        return lax.dot_general(left, right, contract, preferred_element_type=jnp.float32)

    for head in range(HEADS):
        start = HEAD * head // 128 * 128
        stop = -(-(HEAD * head + HEAD) // 128) * 128
        span = stop - start
        lane = lax.broadcasted_iota(jnp.int32, (1, span), 1) + start
        own = (lane >= HEAD * head) & (lane < HEAD * head + HEAD)

        def window(ref, base=0):
            return ref[:, base + start : base + stop]

        def masked(value):
            return jnp.where(own, value, jnp.zeros_like(value))

        queries, keys, values = (window(projected_ref, width * i) for i in range(3))
        out = window(grad_out)
        keys, values = masked(keys), masked(values)
        scores = dot(queries, keys, by_rows) * score_scale
        exponent = jnp.where(same, jnp.exp(scores), 0.0)
        total = jnp.sum(exponent, axis=1, keepdims=True)
        attention = exponent / jnp.where(active, total, 1.0)
        soft = attention.astype(jnp.bfloat16)
        attended[:, start:stop] += dot(soft, values)
        grad_attention = dot(out, values, by_rows)
        inner = jnp.sum(attention * grad_attention, axis=1, keepdims=True)
        grad_score = (attention * (grad_attention - inner) * score_scale).astype(jnp.bfloat16)
        grad_projected[:, start:stop] += dot(grad_score, keys)
        grad_projected[:, width + start : width + stop] += dot(
            grad_score, masked(queries), by_columns
        )
        grad_projected[:, 2 * width + start : 2 * width + stop] += dot(
            soft, masked(out), by_columns
        )
    attended_ref[...] = attended[...].astype(jnp.bfloat16)
    rounded = grad_projected[...].astype(jnp.bfloat16)
    pad = jnp.zeros((rounded.shape[0], REST_PAD - SHARD + MAIN), jnp.bfloat16)
    mains, rests = [], []
    for plane in range(16):
        base = SHARD * plane
        mains.append(rounded[:, base : base + MAIN])
        rests.append(rounded[:, base + MAIN : base + SHARD])
        rests.append(pad)
    grad_main[...] = jnp.concatenate(mains, axis=1)
    grad_rest[...] = jnp.concatenate(rests, axis=1)
    load_main.wait()
    load_rest.wait()

    def back_part(part, carry):
        lanes = pl.ds(pl.multiple_of(part * 256, 128), 256)
        grad_normed[:, lanes] = dot(
            grad_main[...], main[:, :, lanes].reshape(16 * MAIN, 256)
        ) + dot(grad_rest[...], rest[:, lanes])
        return carry

    lax.fori_loop(0, 7, back_part, 0)

    def norm_part(part, carry):
        rows = pl.ds(pl.multiple_of(part * 32, 32), 32)
        values = embedded_ref[rows, :].astype(jnp.float32)
        centered = values - jnp.mean(values, axis=1, keepdims=True)
        variance = jnp.mean(centered * centered, axis=1, keepdims=True)
        inverse = lax.rsqrt(variance + EPSILON)
        hat = centered * inverse
        gained = grad_normed[rows, :] * gain_ref[...]
        result = inverse * (
            gained
            - jnp.mean(gained, axis=1, keepdims=True)
            - hat * jnp.mean(gained * hat, axis=1, keepdims=True)
        )
        grad_embedded[rows, :] = jnp.where(column_id_ref[rows, :] > 0.0, result, 0.0).astype(
            jnp.bfloat16
        )
        return carry

    lax.fori_loop(0, 8, norm_part, 0)
    for part in range(2):
        block = dot(grad_embedded[:, 896 * part : 896 * part + 896], moved_ref[...], by_columns)
        grad_ref[8 * part : 8 * part + 8] = block.astype(jnp.bfloat16).reshape(
            8, CHIP_ROWS, PIX_PAD
        )


def attend(projected, column_id, row_id, cotangent, embedded, gain, moved, main, rest):
    vmem = pl.BlockSpec(memory_space=pltpu.VMEM)
    anywhere = pl.BlockSpec(memory_space=pl.ANY)
    rows = projected.shape[0]
    shape = jax.ShapeDtypeStruct
    return pl.pallas_call(
        attention_kernel,
        name="attend",
        out_shape=(
            shape((rows, HEADS * HEAD), jnp.bfloat16),
            shape((D // CHIP_ROWS, CHIP_ROWS, PIX_PAD), jnp.bfloat16),
        ),
        in_specs=[vmem] * 7 + [anywhere] * 2,
        out_specs=(vmem, vmem),
        scratch_shapes=[
            pltpu.VMEM((16, MAIN, D), jnp.bfloat16),
            pltpu.VMEM((16 * REST_PAD, D), jnp.bfloat16),
            pltpu.VMEM((rows, HEADS * HEAD), jnp.bfloat16),
            pltpu.VMEM((rows, HEADS * HEAD), jnp.float32),
            pltpu.VMEM((rows, 16 * SHARD), jnp.float32),
            pltpu.VMEM((rows, 16 * MAIN), jnp.bfloat16),
            pltpu.VMEM((rows, 16 * REST_PAD), jnp.bfloat16),
            pltpu.VMEM((rows, D), jnp.float32),
            pltpu.VMEM((rows, D), jnp.bfloat16),
            pltpu.SemaphoreType.DMA((2,)),
        ],
        compiler_params=pltpu.CompilerParams(vmem_limit_bytes=48 * 1024 * 1024),
    )(projected, column_id, row_id, cotangent, embedded, gain, moved, main, rest)


def reduce_kernel(
    grad_ref,
    out_ref,
    twin,
    held,
    across,
    line,
    met,
    tiles,
    total,
    result,
    twin_send,
    twin_recv,
    across_send,
    across_recv,
    line_send,
    line_recv,
    tile_send,
    tile_recv,
    total_send,
    total_recv,
    last_send,
    last_recv,
):
    z, b, x, y, core = place()
    sibling = b + 1 - 2 * core
    first = x * (1 - core) + y * core
    second = y * (1 - core) + x * core

    def chip_of(which, f, s):
        return (s * 4 + f) * (1 - which) + (f * 4 + s) * which

    def target_chip(which, a, half):
        mine = x * (1 - which) + y * which
        f = lax.rem(mine + a, 4)
        return chip_of(which, f, 2 * half + lax.rem(f + which, 2))

    def at(f, s):
        return (z, chip_of(core, f, s) * 2 + core)

    barrier = pltpu.get_barrier_semaphore()
    pl.semaphore_signal(barrier, inc=1, device_id=(z, sibling), device_id_type=MESH)
    for a in range(1, 4):
        pl.semaphore_signal(
            barrier, inc=1, device_id=at(lax.rem(first + a, 4), second), device_id_type=MESH
        )
        pl.semaphore_signal(
            barrier, inc=1, device_id=at(first, lax.rem(second + a, 4)), device_id_type=MESH
        )

    def greet(step, carry):
        pl.semaphore_signal(
            barrier, inc=1, device_id=(lax.rem(z + step, 16), b), device_id_type=MESH
        )
        return carry

    lax.fori_loop(1, 16, greet, 0)
    pl.semaphore_wait(barrier, 22)

    def twin_copy(a, half):
        chip = target_chip(1 - core, a, half)
        return remote(
            grad_ref.at[chip], twin.at[a, half], twin_send.at[a, half], twin_recv.at[a, half], (z, sibling)
        )

    order = (2, 1, 3, 0)
    for a in order:
        for half in range(2):
            twin_copy(a, half).start()

    def across_copy(a):
        return remote(
            held.at[a],
            across.at[a],
            across_send.at[a],
            across_recv.at[a],
            at(lax.rem(first + a, 4), second),
        )

    for a in order:
        for half in range(2):
            twin_copy(a, half).wait_recv()
            chip = target_chip(core, a, half)
            held[a, half] = (
                grad_ref[chip].astype(jnp.float32) + twin[a, half].astype(jnp.float32)
            ).astype(jnp.bfloat16)
        if a > 0:
            across_copy(a).start()
    for a in (1, 3, 2):
        across_copy(a).wait_recv()
    for half in range(2):
        line[half] = (
            held[0, half].astype(jnp.float32)
            + across[1, half].astype(jnp.float32)
            + across[2, half].astype(jnp.float32)
            + across[3, half].astype(jnp.float32)
        ).astype(jnp.bfloat16)

    parity = lax.rem(first + core, 2)
    owner = lax.rem(first + second, 2) == core

    def line_copy(half):
        to = 2 * half + parity
        away = lax.rem(to - second + 4, 4)
        return remote(
            line.at[half],
            met.at[away],
            line_send.at[half],
            line_recv.at[away],
            at(first, to),
        )

    for a in range(1, 4):
        across_copy(a).wait_send()
    for half in range(2):
        to = 2 * half + parity

        @pl.when(to != second)
        def _():
            line_copy(half).start()

    tile = total.shape[1]

    def tile_copy(index):
        to = 2 * index
        return remote(
            result.at[pl.ds(16 * index, 16)],
            tiles.at[z],
            tile_send.at[index],
            tile_recv.at[z],
            (to, b),
        )

    def tile_wait(slot):
        remote(
            result.at[pl.ds(0, 16)], tiles.at[slot], tile_send.at[0], tile_recv.at[slot], (slot, b)
        ).wait_recv()

    def total_copy(to, index):
        return remote(
            total.at[index],
            total.at[index],
            total_send.at[to],
            total_recv.at[index],
            (to, b),
        )

    @pl.when(owner)
    def _():
        mine = line[second // 2].astype(jnp.float32)
        for away in (1, 3, 2):
            remote(
                line.at[0], met.at[away], line_send.at[0], line_recv.at[away], (z, sibling)
            ).wait_recv()
            mine = mine + met[away].astype(jnp.float32)
        result[...] = mine.astype(jnp.bfloat16)
        for index in range(7):

            @pl.when(z != 2 * index)
            def _():
                tile_copy(index).start()

        @pl.when((z < 14) & (lax.rem(z, 2) == 0))
        def _():
            index = z // 2
            tiles[z] = result[pl.ds(pl.multiple_of(16 * index, 16), 16), :]

            def take(step, carry):
                tile_wait(lax.rem(z + step, 16))
                return carry

            lax.fori_loop(1, 16, take, 0)
            value = tiles[0].astype(jnp.float32)
            for slot in range(1, 16):
                value = value + tiles[slot].astype(jnp.float32)
            total[index] = value.astype(jnp.bfloat16)

            def spread(step, carry):
                total_copy(lax.rem(z + step, 16), index).start()
                return carry

            lax.fori_loop(1, 16, spread, 0)

        for index in range(7):

            @pl.when(z != 2 * index)
            def _():
                total_copy(0, index).wait_recv()

        remote(total, total, last_send, last_recv, (z, sibling)).start()

        for index in range(7):

            @pl.when(z != 2 * index)
            def _():
                tile_copy(index).wait_send()

        @pl.when((z < 14) & (lax.rem(z, 2) == 0))
        def _():
            def spent(step, carry):
                total_copy(lax.rem(z + step, 16), z // 2).wait_send()
                return carry

            lax.fori_loop(1, 16, spent, 0)

        remote(total, total, last_send, last_recv, (z, sibling)).wait_send()

    @pl.when(jnp.logical_not(owner))
    def _():
        remote(total, total, last_send, last_recv, (z, sibling)).wait_recv()

    for a in range(4):
        for half in range(2):
            twin_copy(a, half).wait_send()
    for half in range(2):
        to = 2 * half + parity

        @pl.when(to != second)
        def _():
            line_copy(half).wait_send()

    out_ref[...] = total[...]


def reduce_grad(grad):
    vmem = pl.BlockSpec(memory_space=pltpu.VMEM)
    dma = pltpu.SemaphoreType.DMA
    block = (CHIP_ROWS, PIX_PAD)
    return pl.pallas_call(
        reduce_kernel,
        name="reduce_grad",
        out_shape=jax.ShapeDtypeStruct((7, 16, PIX_PAD), jnp.bfloat16),
        in_specs=[vmem],
        out_specs=vmem,
        scratch_shapes=[
            pltpu.VMEM((4, 2) + block, jnp.bfloat16),
            pltpu.VMEM((4, 2) + block, jnp.bfloat16),
            pltpu.VMEM((4, 2) + block, jnp.bfloat16),
            pltpu.VMEM((2,) + block, jnp.bfloat16),
            pltpu.VMEM((4,) + block, jnp.bfloat16),
            pltpu.VMEM((16, 16, PIX_PAD), jnp.bfloat16),
            pltpu.VMEM((7, 16, PIX_PAD), jnp.bfloat16),
            pltpu.VMEM(block, jnp.bfloat16),
            dma((4, 2)),
            dma((4, 2)),
            dma((4,)),
            dma((4,)),
            dma((2,)),
            dma((4,)),
            dma((7,)),
            dma((16,)),
            dma((16,)),
            dma((7,)),
            dma,
            dma,
        ],
        compiler_params=pltpu.CompilerParams(
            collective_id=1, has_side_effects=True, vmem_limit_bytes=40 * 1024 * 1024
        ),
    )(grad)


def per_device(
    pixels,
    latent,
    quant_scale,
    embed_bias,
    ln_gain,
    ln_bias,
    qkv_weight,
    cotangent,
    image_length,
    image_source,
    image_target,
):
    member = lax.axis_index("bal")
    members = lax.axis_size("bal")
    length, source, target = image_length[0], image_source[0], image_target[0]
    moving = (target != source) & (length > 0)
    receivers = jnp.arange(members, dtype=jnp.int32)[:, None]
    sender = jnp.sum(
        jnp.where((target[None, :] == receivers) & moving[None, :], source[None, :], 0), axis=1
    )
    gain = ln_gain[None, :]
    main, rest, moved, embedded, projected, column_id, row_id = gather_project(
        qkv_weight.T,
        latent.T,
        quant_scale[None, :],
        embed_bias[None, :],
        gain,
        ln_bias[None, :],
        pixels,
        image_length,
        image_source,
        image_target,
        sender,
    )
    attended, grad = attend(
        projected, column_id, row_id, cotangent, embedded, gain, moved, main, rest
    )
    row_share = D // members
    row_start = member * row_share
    scale_rows = lax.dynamic_slice_in_dim(quant_scale, row_start, row_share, 0)[:, None]
    latent_rows = lax.dynamic_slice_in_dim(latent, row_start, row_share, 0)
    ratio = latent_rows.astype(jnp.float32) / scale_rows
    level = jnp.floor(ratio + 0.5)
    inside = (level >= -8.0) & (level <= 7.0)
    slope = jnp.where(inside, level - ratio, jnp.clip(level, -8.0, 7.0))
    reduced = reduce_grad(grad).reshape(CHIP_ROWS, PIX_PAD)
    summed = lax.dynamic_slice_in_dim(reduced, lax.rem(member, 2) * row_share, row_share, 0)
    summed = summed[:, :PIX].astype(jnp.float32)
    grad_latent = jnp.where(inside, summed, 0.0)
    grad_scale = (1.0 / math.sqrt(PIX * 7.0)) * jnp.sum(summed * slope, axis=1)
    return (attended, grad_latent, grad_scale)


def solution(mesh):
    placed = (
        P(("dp", "bal"), None),
        P(),
        P(),
        P(),
        P(),
        P(),
        P(None, "dp"),
        P(("dp", "bal"), None),
        P("dp", None),
        P("dp", None),
        P("dp", None),
    )
    return jax.shard_map(
        per_device,
        mesh=mesh,
        in_specs=placed,
        out_specs=(P(("dp", "bal"), None), P("bal", None), P("bal")),
        check_vma=False,
    )
```

```python
import math

import jax
import jax.numpy as jnp
from jax import lax
from jax.experimental import pallas as pl
from jax.experimental.pallas import tpu as pltpu
from jax.sharding import PartitionSpec as P

D = 1792
HEAD = 112
PIX = 588
HEADS = 8
MOVE_ROWS = 128
EPSILON = 1e-06
MESH = pl.DeviceIdType.MESH
SHARD = 168
MAIN = 128
REST_PAD = 48
CHIP_ROWS = 112
PIX_PAD = 640
PIECES = 20


def place():
    z = lax.axis_index("dp")
    b = lax.axis_index("bal")
    core = lax.rem(b, 2)
    x = lax.rem(b // 2, 4)
    y = b // 8
    return z, b, x, y, core


def remote(src, dst, send, recv, device):
    copy = pltpu.make_async_remote_copy(
        src_ref=src, dst_ref=dst, send_sem=send, recv_sem=recv, device_id=device, device_id_type=MESH
    )
    return copy


def whole_kernel(
    weight_in,
    latent_in,
    scale_in,
    bias_in,
    gain_in,
    shift_in,
    pixels_in,
    cotangent_in,
    length_ref,
    source_ref,
    target_ref,
    attended_ref,
    latent_out,
    scale_out,
    w_ref,
    latent_ref,
    vectors,
    pixels_ref,
    cotangent_ref,
    sender_vector,
    sender_ref,
    slope,
    within,
    moved_ref,
    embedded_ref,
    projected_ref,
    column_id_ref,
    row_id_ref,
    main,
    rest,
    rows_in,
    pieces,
    inbox,
    stage,
    arrived,
    quant,
    normed,
    part_main,
    part_rest,
    grad_out,
    attended,
    grad_projected,
    grad_main,
    grad_rest,
    grad_normed,
    grad_embedded,
    grad_ref,
    twin,
    held,
    across,
    line,
    met,
    tiles,
    total,
    summed,
    final,
    load_sem,
    z_send,
    z_recv,
    ring_send,
    ring_recv,
    hand_send,
    hand_recv,
    out_send,
    out_recv,
    back_send,
    back_recv,
    plane_send,
    plane_recv,
    pair_send,
    pair_recv,
    twin_send,
    twin_recv,
    across_send,
    across_recv,
    line_send,
    line_recv,
    tile_send,
    tile_recv,
    total_send,
    total_recv,
    last_send,
    last_recv,
):
    z, b, x, y, core = place()
    sibling = b + 1 - 2 * core
    chip = b // 2
    quad = z // 4
    barrier = pltpu.get_barrier_semaphore()

    def greet_plane(step, carry):
        pl.semaphore_signal(
            barrier, inc=1, device_id=(z, lax.rem(b + step, 32)), device_id_type=MESH
        )
        return carry

    def greet_line(step, carry):
        pl.semaphore_signal(
            barrier, inc=1, device_id=(lax.rem(z + step, 16), b), device_id_type=MESH
        )
        return carry

    loads = []
    for index, (source, held_at) in enumerate(
        (
            (weight_in, w_ref),
            (pixels_in, pixels_ref),
            (latent_in, latent_ref),
            (scale_in, vectors.at[0]),
            (bias_in, vectors.at[1]),
            (gain_in, vectors.at[2]),
            (shift_in, vectors.at[3]),
            (cotangent_in, cotangent_ref),
        )
    ):
        loads.append(pltpu.make_async_copy(source, held_at, load_sem.at[index]))
        loads[-1].start()
    scale_ref, bias_ref, gain_ref, shift_ref = (vectors.at[pl.ds(i, 1)] for i in range(4))
    lax.fori_loop(1, 16, greet_line, 0)
    lax.fori_loop(1, 32, greet_plane, 0)

    def slice_rows(where):
        return pl.ds(pl.multiple_of((where // 2) * 16, 16), 16)

    def slice_lanes(where):
        return pl.ds(pl.multiple_of(lax.rem(where, 2) * 896, 128), 896)

    loads[0].wait()

    @pl.when(core == 0)
    def _():
        main[z, slice_rows(chip), slice_lanes(chip)] = w_ref[slice_rows(chip), slice_lanes(chip)]

    def rest_rows(plane):
        return pl.ds(pl.multiple_of(plane * REST_PAD, 16), REST_PAD)

    rest[rest_rows(z), :] = jnp.concatenate(
        [w_ref[pl.ds(MAIN, SHARD - MAIN), :], jnp.zeros((REST_PAD - SHARD + MAIN, D), jnp.bfloat16)],
        axis=0,
    )
    pl.semaphore_wait(barrier, 46)

    def z_copy(step):
        to = lax.rem(z + step, 16)
        return remote(
            w_ref.at[slice_rows(chip), slice_lanes(chip)],
            main.at[z, slice_rows(chip), slice_lanes(chip)],
            z_send.at[step],
            z_recv.at[z],
            (to, b),
        )

    def z_mine(step):
        return lax.rem(lax.rem(z + step, 16) // 4 + quad, 2) == core

    for step in (1, 15, 2, 14, 3, 13, 4, 12, 5, 11, 6, 10, 7, 9, 8):

        @pl.when(z_mine(step))
        def _():
            z_copy(step).start()

    def half_lanes(which, part):
        start, count = ((0, 512), (512, 384))[part]
        return pl.ds(pl.multiple_of(which * 896 + start, 128), count)

    def ring_copy(way, step, part):
        sign = 1 if way == 0 else -1
        origin = lax.rem(z - sign * (step - 1) + 16, 16)
        to = lax.rem(z + sign + 16, 16)
        block = rest.at[rest_rows(origin), half_lanes(core, part)]
        return remote(
            block, block, ring_send.at[way, step, part], ring_recv.at[way, step, part], (to, b)
        )

    def ring_wait(way, step, part):
        sign = 1 if way == 0 else -1
        origin = lax.rem(z - sign * step + 16, 16)
        block = rest.at[rest_rows(origin), half_lanes(core, part)]
        remote(
            block,
            block,
            ring_send.at[way, step, part],
            ring_recv.at[way, step, part],
            (lax.rem(z + 1, 16), b),
        ).wait_recv()

    def hand_copy(which, way, step):
        sign = 1 if way == 0 else -1
        origin = lax.rem(z - sign * step + 16, 16)
        block = rest.at[
            rest_rows(origin), pl.ds(pl.multiple_of(which * 896, 128), 896)
        ]
        return remote(
            block, block, hand_send.at[way, step], hand_recv.at[way, step], (z, sibling)
        )

    last = (8, 7)
    for part in range(2):
        for way in range(2):
            ring_copy(way, 1, part).start()

    def ring_step(step):
        for part in range(2):
            for way in range(2):
                if step <= last[way]:
                    ring_wait(way, step, part)
                    if step < last[way]:
                        ring_copy(way, step + 1, part).start()
        for way in range(2):
            if step <= last[way]:
                hand_copy(core, way, step).start()

    length_row = length_ref[...].astype(jnp.float32)
    source_row = source_ref[...].astype(jnp.float32)
    target_row = target_ref[...].astype(jnp.float32)
    entries = length_row.shape[1]

    def turned(row):
        return jnp.broadcast_to(row, (entries, entries)).T

    length_col, source_col, target_col = turned(length_row), turned(source_row), turned(target_row)
    down = lax.broadcasted_iota(jnp.int32, (entries, entries), 0)
    along = lax.broadcasted_iota(jnp.int32, (entries, entries), 1)
    member = b.astype(jnp.float32)

    def above(owner_col, owner_row, amount_col):
        match = (down < along) & (owner_col == owner_row)
        return jnp.sum(jnp.where(match, amount_col, 0.0), axis=0, keepdims=True)

    target_start = above(target_col, target_row, length_col)
    source_start = above(source_col, source_row, length_col)
    moving_col = jnp.where(target_col != source_col, length_col, 0.0)
    outbox_start = above(source_col, source_row, moving_col)
    before = (along < down) & (target_col == target_row)
    target_start_col = jnp.sum(jnp.where(before, length_row, 0.0), axis=1, keepdims=True)

    slots = lax.broadcasted_iota(jnp.int32, (MOVE_ROWS, entries), 0).astype(jnp.float32)
    leaving = (
        (source_row == member)
        & (target_row != source_row)
        & (slots >= outbox_start)
        & (slots < outbox_start + length_row)
    )
    leaving_row = jnp.sum(
        jnp.where(leaving, source_start - outbox_start + slots, 0.0), axis=1, keepdims=True
    )
    leaving_any = jnp.sum(jnp.where(leaving, 1.0, 0.0), axis=1, keepdims=True)
    leaving_row = jnp.where(leaving_any > 0.0, leaving_row, -1.0)
    count_in = pixels_ref.shape[0]
    whole_col = [turned(ref[...]) for ref in (length_ref, source_ref, target_ref)]
    senders = jnp.where(
        (whole_col[2] == along) & (whole_col[2] != whole_col[1]) & (whole_col[0] > 0), whole_col[1], 0
    )
    sender_vector[...] = jnp.sum(senders, axis=0, keepdims=True)
    load_sender = pltpu.make_async_copy(sender_vector, sender_ref, load_sem.at[8])
    load_sender.start()
    loads[1].wait()
    rows_in[:, pl.ds(512, 128)] = jnp.zeros((rows_in.shape[0], 128), jnp.bfloat16)
    rows_in[pl.ds(0, count_in), pl.ds(0, PIX)] = pixels_ref[...]
    picks = lax.broadcasted_iota(jnp.int32, (MOVE_ROWS, count_in), 1).astype(jnp.float32)
    outgoing = jnp.dot(
        jnp.where(leaving_row == picks, 1.0, 0.0).astype(jnp.bfloat16),
        rows_in[pl.ds(0, count_in), :],
        preferred_element_type=jnp.float32,
    ).astype(jnp.bfloat16)
    for i in range(4):
        for j in range(5):
            pieces[5 * i + j] = outgoing[32 * i : 32 * i + 32, 128 * j : 128 * j + 128]

    def out_copy(target, slot):
        return remote(
            pieces.at[target], inbox.at[slot], out_send.at[target], out_recv.at[slot], (z, target)
        )

    def back_copy(target, slot):
        return remote(
            stage.at[target], arrived.at[slot], back_send.at[target], back_recv.at[slot], (z, target)
        )

    def send_out(step, carry):
        target = lax.rem(b + step, 32)

        @pl.when(target < PIECES)
        def _():
            out_copy(target, b).start()

        return carry

    lax.fori_loop(1, 32, send_out, 0)

    def quad_of(which, chunk):
        base = quad * (1 - which) + which * (quad + 3 + 2 * (lax.rem(z, 4) // 2))
        return lax.rem(base + 2 * chunk, 4)

    def chip_at(which, chunk, first, second):
        swap = lax.rem(which + chunk, 2)
        dx = first * (1 - swap) + second * swap
        dy = first * swap + second * (1 - swap)
        return lax.rem(y + dy + 4, 4) * 4 + lax.rem(x + dx + 4, 4)

    def piece(which, chunk, where, low=0, count=4):
        return main.at[
            pl.ds(4 * quad_of(which, chunk) + low, count), slice_rows(where), slice_lanes(where)
        ]

    offsets = (0, -1, 1, 2)
    spans = ((0, 4), (0, 4), (0, 2), (2, 2))

    def hop(chunk, index, axis, place_index, kind):
        low, count = spans[kind]
        sign = 1 if kind in (0, 2) else -1
        origin = (0, 0, -1, 1)[kind]
        a = offsets[place_index]
        if axis == 0:
            to, sent = chip_at(core, chunk, sign, 0), chip_at(core, chunk, origin, 0)
        else:
            to, sent = chip_at(core, chunk, 0, sign), chip_at(core, chunk, a, origin)
        rows = piece(core, chunk, sent, low, count)
        return remote(
            rows, rows, plane_send.at[chunk, index], plane_recv.at[chunk, index], (z, to * 2 + core)
        )

    def hop_wait(chunk, index, axis, place_index, kind):
        low, count = spans[kind]
        origin = (-1, 1, 2, 2)[kind]
        a = offsets[place_index]
        if axis == 0:
            sent = chip_at(core, chunk, origin, 0)
        else:
            sent = chip_at(core, chunk, a, origin)
        rows = piece(core, chunk, sent, low, count)
        remote(
            rows, rows, plane_send.at[chunk, index], plane_recv.at[chunk, index], (z, sibling)
        ).wait_recv()

    def first_copy(chunk, kind):
        return hop(chunk, kind, 0, 0, kind)

    def first_wait(chunk, kind):
        hop_wait(chunk, kind, 0, 0, kind)

    def second_copy(chunk, place_index, kind):
        return hop(chunk, 4 + 4 * place_index + kind, 1, place_index, kind)

    def second_wait(chunk, place_index, kind):
        hop_wait(chunk, 4 + 4 * place_index + kind, 1, place_index, kind)

    def pair_copy(which, chunk, place_index, second_index):
        rows = piece(
            which, chunk, chip_at(which, chunk, offsets[place_index], offsets[second_index])
        )
        index = place_index * 4 + second_index
        return remote(
            rows, rows, pair_send.at[chunk, index], pair_recv.at[chunk, index], (z, sibling)
        )

    def chunk_start(chunk):
        for j in range(4):
            origin = 4 * quad_of(core, chunk) + j

            @pl.when(origin != z)
            def _():
                rows = main.at[origin, slice_rows(chip), slice_lanes(chip)]
                remote(rows, rows, z_send.at[0], z_recv.at[origin], (z, sibling)).wait_recv()

        first_copy(chunk, 0).start()
        first_copy(chunk, 1).start()
        second_copy(chunk, 0, 0).start()
        second_copy(chunk, 0, 1).start()
        pair_copy(core, chunk, 0, 0).start()

    def chunk_first(chunk):
        for kind, index in ((0, 1), (1, 2)):
            first_wait(chunk, kind)
            first_copy(chunk, kind + 2).start()
            second_copy(chunk, index, 0).start()
            second_copy(chunk, index, 1).start()
            pair_copy(core, chunk, index, 0).start()

    def chunk_far(chunk):
        first_wait(chunk, 2)
        first_wait(chunk, 3)
        second_copy(chunk, 3, 0).start()
        second_copy(chunk, 3, 1).start()
        pair_copy(core, chunk, 3, 0).start()

    def chunk_second(chunk, index):
        for kind in (0, 1):
            second_wait(chunk, index, kind)
            second_copy(chunk, index, kind + 2).start()
            pair_copy(core, chunk, index, kind + 1).start()

    def chunk_last(chunk, index):
        second_wait(chunk, index, 2)
        second_wait(chunk, index, 3)
        pair_copy(core, chunk, index, 3).start()

    def quantize_part(part, carry):
        lanes = pl.ds(pl.multiple_of(part * 256, 128), 256)
        scale = scale_ref[:, lanes]
        level = jnp.floor(latent_ref[:, lanes].astype(jnp.float32) / scale + 0.5)
        quant[pl.ds(0, PIX), lanes] = (jnp.clip(level, -8.0, 7.0) * scale).astype(jnp.bfloat16)
        return carry

    def embed_part(part, carry):
        lanes = pl.ds(pl.multiple_of(part * 256, 128), 256)
        total = jnp.dot(moved_ref[...], quant[:, lanes], preferred_element_type=jnp.float32)
        embedded_ref[:, lanes] = (total + bias_ref[:, lanes]).astype(jnp.bfloat16)
        return carry

    def norm_part(part, carry):
        rows = pl.ds(pl.multiple_of(part * 32, 32), 32)
        values = embedded_ref[rows, :].astype(jnp.float32)
        centered = values - jnp.mean(values, axis=1, keepdims=True)
        variance = jnp.mean(centered * centered, axis=1, keepdims=True)
        hat = centered * lax.rsqrt(variance + EPSILON)
        normed[rows, :] = (hat * gain_ref[...] + shift_ref[...]).astype(jnp.bfloat16)
        return carry

    chunk_start(0)
    ring_step(1)
    load_sender.wait()

    @pl.when(b < PIECES)
    def _():
        inbox[b] = pieces[b]

        def take(step, carry):
            out_copy(b, lax.rem(b + step, 32)).wait_recv()
            return carry

        lax.fori_loop(1, 32, take, 0)
        arrived[b] = inbox[jnp.clip(sender_ref[0, b], 0, 31)]

        def send_back(step, carry):
            target = lax.rem(b + step, 32)
            stage[target] = inbox[jnp.clip(sender_ref[0, target], 0, 31)]
            back_copy(target, b).start()
            return carry

        lax.fori_loop(1, 32, send_back, 0)

    chunk_first(0)
    ring_step(2)
    quant[pl.ds(576, 64), :] = jnp.zeros((64, D), jnp.bfloat16)
    for index in range(2, 7):
        loads[index].wait()
    lax.fori_loop(0, 7, quantize_part, 0)
    share = D // 32
    window = jnp.minimum(chip * CHIP_ROWS // 128 * 128, D - 256)
    lanes = pl.ds(pl.multiple_of(window, 128), 256)
    ratio = latent_ref[:, lanes].astype(jnp.float32) / scale_ref[:, lanes]
    level = jnp.floor(ratio + 0.5)
    inside = (level >= -8.0) & (level <= 7.0)
    slope[...] = jnp.where(inside, level - ratio, jnp.clip(level, -8.0, 7.0)).T
    within[...] = jnp.where(inside, 1.0, 0.0).T
    share_rows = pl.ds(pl.multiple_of(chip * CHIP_ROWS - window + core * share, 8), share)
    chunk_far(0)
    chunk_second(0, 0)
    ring_step(3)

    row = lax.broadcasted_iota(jnp.int32, (moved_ref.shape[0], entries), 0).astype(jnp.float32)
    covers = (target_row == member) & (row >= target_start) & (row < target_start + length_row)
    take_from = (
        jnp.where(source_row == member, source_start, outbox_start + float(count_in)) - target_start
    )
    wanted = jnp.sum(jnp.where(covers, take_from + row, 0.0), axis=1, keepdims=True)
    entry = (lax.broadcasted_iota(jnp.int32, (1, entries), 1) + 1).astype(jnp.float32)
    image = jnp.sum(jnp.where(covers, entry, 0.0), axis=1, keepdims=True)
    wanted = jnp.where(image > 0.0, wanted, -1.0)
    column_id_ref[...] = image
    row_lane = lax.broadcasted_iota(jnp.int32, (entries, moved_ref.shape[0]), 1).astype(jnp.float32)
    covers_turned = (
        (target_col[:, :1] == member)
        & (row_lane >= target_start_col)
        & (row_lane < target_start_col + length_col[:, :1])
    )
    entry_down = (lax.broadcasted_iota(jnp.int32, (entries, 1), 0) + 1).astype(jnp.float32)
    row_id_ref[...] = jnp.sum(jnp.where(covers_turned, entry_down, 0.0), axis=0, keepdims=True)

    def arrive(step, carry):
        slot = lax.rem(b + step, 32)

        @pl.when(slot < PIECES)
        def _():
            back_copy(b, slot).wait_recv()

        return carry

    lax.fori_loop(1, 32, arrive, 0)
    for i in range(4):
        for j in range(5):
            rows_in[pl.ds(count_in + 32 * i, 32), pl.ds(128 * j, 128)] = arrived[5 * i + j]
    choose = lax.broadcasted_iota(
        jnp.int32, (moved_ref.shape[0], count_in + MOVE_ROWS), 1
    ).astype(jnp.float32)
    moved_ref[...] = jnp.dot(
        jnp.where(wanted == choose, 1.0, 0.0).astype(jnp.bfloat16),
        rows_in[...],
        preferred_element_type=jnp.float32,
    ).astype(jnp.bfloat16)
    chunk_second(0, 1)
    chunk_start(1)
    ring_step(4)
    lax.fori_loop(0, 4, embed_part, 0)
    chunk_second(0, 2)
    chunk_first(1)
    ring_step(5)
    lax.fori_loop(4, 7, embed_part, 0)
    chunk_second(0, 3)
    chunk_far(1)
    chunk_second(1, 0)
    ring_step(6)
    lax.fori_loop(0, 4, norm_part, 0)
    chunk_second(1, 1)
    chunk_second(1, 2)
    ring_step(7)
    lax.fori_loop(4, 8, norm_part, 0)
    chunk_second(1, 3)
    for index in range(4):
        chunk_last(0, index)
    ring_step(8)
    for index in range(4):
        chunk_last(1, index)

    def project(which, chunk):
        q = quad_of(which, chunk)
        for pair in range(2):
            block = main[pl.ds(4 * q + 2 * pair, 2)].reshape(256, D)
            part_main[4 * q // 2 + pair] = lax.dot_general(
                normed[...], block, (((1,), (1,)), ((), ())), preferred_element_type=jnp.float32
            ).astype(jnp.bfloat16)

    def pair_wait(chunk):
        for index in range(4):
            for second in range(4):
                pair_copy(1 - core, chunk, index, second).wait_recv()

    project(core, 0)
    pair_wait(0)
    project(1 - core, 0)
    project(core, 1)
    pair_wait(1)
    project(1 - core, 1)
    for way in range(2):
        for step in range(1, last[way] + 1):
            hand_copy(1 - core, way, step).wait_recv()
    for part in range(3):
        part_rest[:, 256 * part : 256 * part + 256] = lax.dot_general(
            normed[...],
            rest[pl.ds(256 * part, 256), :],
            (((1,), (1,)), ((), ())),
            preferred_element_type=jnp.float32,
        ).astype(jnp.bfloat16)
    joined = []
    for plane in range(16):
        joined.append(part_main[plane // 2, :, 128 * (plane % 2) : 128 * (plane % 2) + 128])
        joined.append(part_rest[:, REST_PAD * plane : REST_PAD * plane + SHARD - MAIN])
    projected_ref[...] = jnp.concatenate(joined, axis=1)

    loads[7].wait()
    width = HEADS * HEAD
    score_scale = HEAD ** (-0.5)
    grad_factor = 1.0 / math.sqrt(131072.0)
    column_id = column_id_ref[...]
    row_id = row_id_ref[...]
    active = column_id > 0.0
    same = (column_id == row_id) & active
    grad_out[...] = jnp.where(
        active, cotangent_ref[...].astype(jnp.float32) * grad_factor, 0.0
    ).astype(jnp.bfloat16)
    attended[...] = jnp.zeros_like(attended)
    grad_projected[...] = jnp.zeros_like(grad_projected)
    by_rows = (((1,), (1,)), ((), ()))
    by_columns = (((0,), (0,)), ((), ()))

    def dot(left, right, contract=(((1,), (0,)), ((), ()))):
        return lax.dot_general(left, right, contract, preferred_element_type=jnp.float32)

    for head in range(HEADS):
        start = HEAD * head // 128 * 128
        stop = -(-(HEAD * head + HEAD) // 128) * 128
        span = stop - start
        lane = lax.broadcasted_iota(jnp.int32, (1, span), 1) + start
        own = (lane >= HEAD * head) & (lane < HEAD * head + HEAD)

        def window(ref, base=0):
            return ref[:, base + start : base + stop]

        def masked(value):
            return jnp.where(own, value, jnp.zeros_like(value))

        queries, keys, values = (window(projected_ref, width * i) for i in range(3))
        out = window(grad_out)
        keys, values = masked(keys), masked(values)
        scores = dot(queries, keys, by_rows) * score_scale
        exponent = jnp.where(same, jnp.exp(scores), 0.0)
        denominator = jnp.sum(exponent, axis=1, keepdims=True)
        attention = exponent / jnp.where(active, denominator, 1.0)
        soft = attention.astype(jnp.bfloat16)
        attended[:, start:stop] += dot(soft, values)
        grad_attention = dot(out, values, by_rows)
        inner = jnp.sum(attention * grad_attention, axis=1, keepdims=True)
        grad_score = (attention * (grad_attention - inner) * score_scale).astype(jnp.bfloat16)
        grad_projected[:, start:stop] += dot(grad_score, keys)
        grad_projected[:, width + start : width + stop] += dot(
            grad_score, masked(queries), by_columns
        )
        grad_projected[:, 2 * width + start : 2 * width + stop] += dot(
            soft, masked(out), by_columns
        )
    attended_ref[...] = attended[...].astype(jnp.bfloat16)
    rounded = grad_projected[...].astype(jnp.bfloat16)
    pad = jnp.zeros((rounded.shape[0], REST_PAD - SHARD + MAIN), jnp.bfloat16)
    mains, rests = [], []
    for plane in range(16):
        base = SHARD * plane
        mains.append(rounded[:, base : base + MAIN])
        rests.append(rounded[:, base + MAIN : base + SHARD])
        rests.append(pad)
    grad_main[...] = jnp.concatenate(mains, axis=1)
    grad_rest[...] = jnp.concatenate(rests, axis=1)

    def back_part(part, carry):
        lanes = pl.ds(pl.multiple_of(part * 256, 128), 256)
        grad_normed[:, lanes] = dot(
            grad_main[...], main[:, :, lanes].reshape(16 * MAIN, 256)
        ) + dot(grad_rest[...], rest[:, lanes])
        return carry

    lax.fori_loop(0, 7, back_part, 0)

    def back_norm_part(part, carry):
        rows = pl.ds(pl.multiple_of(part * 32, 32), 32)
        values = embedded_ref[rows, :].astype(jnp.float32)
        centered = values - jnp.mean(values, axis=1, keepdims=True)
        variance = jnp.mean(centered * centered, axis=1, keepdims=True)
        inverse = lax.rsqrt(variance + EPSILON)
        hat = centered * inverse
        gained = grad_normed[rows, :] * gain_ref[...]
        result = inverse * (
            gained
            - jnp.mean(gained, axis=1, keepdims=True)
            - hat * jnp.mean(gained * hat, axis=1, keepdims=True)
        )
        grad_embedded[rows, :] = jnp.where(column_id_ref[rows, :] > 0.0, result, 0.0).astype(
            jnp.bfloat16
        )
        return carry

    lax.fori_loop(0, 8, back_norm_part, 0)
    for part in range(2):
        block = dot(grad_embedded[:, 896 * part : 896 * part + 896], moved_ref[...], by_columns)
        grad_ref[8 * part : 8 * part + 8] = block.astype(jnp.bfloat16).reshape(
            8, CHIP_ROWS, PIX_PAD
        )
    first = x * (1 - core) + y * core
    second = y * (1 - core) + x * core

    def chip_of(which, f, s):
        return (s * 4 + f) * (1 - which) + (f * 4 + s) * which

    def target_chip(which, a, half):
        mine = x * (1 - which) + y * which
        f = lax.rem(mine + a, 4)
        return chip_of(which, f, 2 * half + lax.rem(f + which, 2))

    def at(f, s):
        return (z, chip_of(core, f, s) * 2 + core)

    def twin_copy(a, half):
        chip = target_chip(1 - core, a, half)
        return remote(
            grad_ref.at[chip], twin.at[a, half], twin_send.at[a, half], twin_recv.at[a, half], (z, sibling)
        )

    order = (2, 1, 3, 0)
    for a in order:
        for half in range(2):
            twin_copy(a, half).start()

    def across_copy(a):
        return remote(
            held.at[a],
            across.at[a],
            across_send.at[a],
            across_recv.at[a],
            at(lax.rem(first + a, 4), second),
        )

    for a in order:
        for half in range(2):
            twin_copy(a, half).wait_recv()
            chip = target_chip(core, a, half)
            held[a, half] = (
                grad_ref[chip].astype(jnp.float32) + twin[a, half].astype(jnp.float32)
            ).astype(jnp.bfloat16)
        if a > 0:
            across_copy(a).start()
    for a in (1, 3, 2):
        across_copy(a).wait_recv()
    for half in range(2):
        line[half] = (
            held[0, half].astype(jnp.float32)
            + across[1, half].astype(jnp.float32)
            + across[2, half].astype(jnp.float32)
            + across[3, half].astype(jnp.float32)
        ).astype(jnp.bfloat16)

    parity = lax.rem(first + core, 2)
    owner = lax.rem(first + second, 2) == core

    def line_copy(half):
        to = 2 * half + parity
        away = lax.rem(to - second + 4, 4)
        return remote(
            line.at[half],
            met.at[away],
            line_send.at[half],
            line_recv.at[away],
            at(first, to),
        )

    for a in range(1, 4):
        across_copy(a).wait_send()
    for half in range(2):
        to = 2 * half + parity

        @pl.when(to != second)
        def _():
            line_copy(half).start()

    tile = total.shape[1]

    def tile_copy(index):
        to = 2 * index
        return remote(
            summed.at[pl.ds(16 * index, 16)],
            tiles.at[z],
            tile_send.at[index],
            tile_recv.at[z],
            (to, b),
        )

    def tile_wait(slot):
        remote(
            summed.at[pl.ds(0, 16)], tiles.at[slot], tile_send.at[0], tile_recv.at[slot], (slot, b)
        ).wait_recv()

    def total_copy(to, index):
        return remote(
            total.at[index],
            total.at[index],
            total_send.at[to],
            total_recv.at[index],
            (to, b),
        )

    @pl.when(owner)
    def _():
        mine = line[second // 2].astype(jnp.float32)
        for away in (1, 3, 2):
            remote(
                line.at[0], met.at[away], line_send.at[0], line_recv.at[away], (z, sibling)
            ).wait_recv()
            mine = mine + met[away].astype(jnp.float32)
        summed[...] = mine.astype(jnp.bfloat16)
        for index in range(7):

            @pl.when(z != 2 * index)
            def _():
                tile_copy(index).start()

        @pl.when((z < 14) & (lax.rem(z, 2) == 0))
        def _():
            index = z // 2
            tiles[z] = summed[pl.ds(pl.multiple_of(16 * index, 16), 16), :]

            def take(step, carry):
                tile_wait(lax.rem(z + step, 16))
                return carry

            lax.fori_loop(1, 16, take, 0)
            value = tiles[0].astype(jnp.float32)
            for slot in range(1, 16):
                value = value + tiles[slot].astype(jnp.float32)
            total[index] = value.astype(jnp.bfloat16)

            def spread(step, carry):
                total_copy(lax.rem(z + step, 16), index).start()
                return carry

            lax.fori_loop(1, 16, spread, 0)

        for index in range(7):

            @pl.when(z != 2 * index)
            def _():
                total_copy(0, index).wait_recv()

        remote(total, total, last_send, last_recv, (z, sibling)).start()

        for index in range(7):

            @pl.when(z != 2 * index)
            def _():
                tile_copy(index).wait_send()

        @pl.when((z < 14) & (lax.rem(z, 2) == 0))
        def _():
            def spent(step, carry):
                total_copy(lax.rem(z + step, 16), z // 2).wait_send()
                return carry

            lax.fori_loop(1, 16, spent, 0)

        remote(total, total, last_send, last_recv, (z, sibling)).wait_send()

    @pl.when(jnp.logical_not(owner))
    def _():
        remote(total, total, last_send, last_recv, (z, sibling)).wait_recv()

    for a in range(4):
        for half in range(2):
            twin_copy(a, half).wait_send()
    for half in range(2):
        to = 2 * half + parity

        @pl.when(to != second)
        def _():
            line_copy(half).wait_send()


    rows = total[...].astype(jnp.float32).reshape(CHIP_ROWS, PIX_PAD)
    final[...] = rows
    mine = final[pl.ds(pl.multiple_of(core * share, 8), share), pl.ds(0, PIX)]
    latent_out[...] = jnp.where(within[share_rows, :] > 0.0, mine, 0.0)
    scale_out[...] = (1.0 / math.sqrt(PIX * 7.0)) * jnp.sum(mine * slope[share_rows, :], axis=1)

    for step in range(1, 16):

        @pl.when(z_mine(step))
        def _():
            z_copy(step).wait_send()

    for way in range(2):
        for step in range(1, last[way] + 1):
            for part in range(2):
                ring_copy(way, step, part).wait_send()
            hand_copy(core, way, step).wait_send()

    def sent_out(step, carry):
        target = lax.rem(b + step, 32)

        @pl.when(target < PIECES)
        def _():
            out_copy(target, b).wait_send()

        return carry

    lax.fori_loop(1, 32, sent_out, 0)

    @pl.when(b < PIECES)
    def _():
        def sent_back(step, carry):
            back_copy(lax.rem(b + step, 32), b).wait_send()
            return carry

        lax.fori_loop(1, 32, sent_back, 0)

    for chunk in range(2):
        for kind in range(4):
            first_copy(chunk, kind).wait_send()
            for index in range(4):
                second_copy(chunk, index, kind).wait_send()
        for index in range(4):
            for second in range(4):
                pair_copy(core, chunk, index, second).wait_send()


def whole(weight, latent, scale, bias, gain, shift, pixels, cotangent, length, source, target):
    vmem = pl.BlockSpec(memory_space=pltpu.VMEM)
    anywhere = pl.BlockSpec(memory_space=pl.ANY)
    dma = pltpu.SemaphoreType.DMA
    rows = cotangent.shape[0]
    block = (CHIP_ROWS, PIX_PAD)
    shape = jax.ShapeDtypeStruct
    return pl.pallas_call(
        whole_kernel,
        name="whole",
        out_shape=(
            shape((rows, HEADS * HEAD), jnp.bfloat16),
            shape((D // 32, PIX), jnp.float32),
            shape((D // 32,), jnp.float32),
        ),
        in_specs=[anywhere] * 8 + [vmem] * 3,
        out_specs=(vmem, vmem, vmem),
        scratch_shapes=[
            pltpu.VMEM((SHARD, D), jnp.bfloat16),
            pltpu.VMEM((PIX, D), jnp.bfloat16),
            pltpu.VMEM((8, D), jnp.float32),
            pltpu.VMEM(pixels.shape, jnp.bfloat16),
            pltpu.VMEM(cotangent.shape, jnp.bfloat16),
            pltpu.VMEM((1, 128), jnp.int32),
            pltpu.SMEM((1, 128), jnp.int32),
            pltpu.VMEM((256, PIX), jnp.float32),
            pltpu.VMEM((256, PIX), jnp.float32),
            pltpu.VMEM((rows, PIX_PAD), jnp.bfloat16),
            pltpu.VMEM((rows, D), jnp.bfloat16),
            pltpu.VMEM((rows, 16 * SHARD), jnp.bfloat16),
            pltpu.VMEM((rows, 1), jnp.float32),
            pltpu.VMEM((1, rows), jnp.float32),
            pltpu.VMEM((16, MAIN, D), jnp.bfloat16),
            pltpu.VMEM((16 * REST_PAD, D), jnp.bfloat16),
            pltpu.VMEM((pixels.shape[0] + MOVE_ROWS, PIX_PAD), jnp.bfloat16),
            pltpu.VMEM((PIECES, 32, 128), jnp.bfloat16),
            pltpu.VMEM((32, 32, 128), jnp.bfloat16),
            pltpu.VMEM((32, 32, 128), jnp.bfloat16),
            pltpu.VMEM((PIECES, 32, 128), jnp.bfloat16),
            pltpu.VMEM((PIX_PAD, D), jnp.bfloat16),
            pltpu.VMEM((rows, D), jnp.bfloat16),
            pltpu.VMEM((8, rows, 256), jnp.bfloat16),
            pltpu.VMEM((rows, 16 * REST_PAD), jnp.bfloat16),
            pltpu.VMEM((rows, HEADS * HEAD), jnp.bfloat16),
            pltpu.VMEM((rows, HEADS * HEAD), jnp.float32),
            pltpu.VMEM((rows, 16 * SHARD), jnp.float32),
            pltpu.VMEM((rows, 16 * MAIN), jnp.bfloat16),
            pltpu.VMEM((rows, 16 * REST_PAD), jnp.bfloat16),
            pltpu.VMEM((rows, D), jnp.float32),
            pltpu.VMEM((rows, D), jnp.bfloat16),
            pltpu.VMEM((D // CHIP_ROWS,) + block, jnp.bfloat16),
            pltpu.VMEM((4, 2) + block, jnp.bfloat16),
            pltpu.VMEM((4, 2) + block, jnp.bfloat16),
            pltpu.VMEM((4, 2) + block, jnp.bfloat16),
            pltpu.VMEM((2,) + block, jnp.bfloat16),
            pltpu.VMEM((4,) + block, jnp.bfloat16),
            pltpu.VMEM((16, 16, PIX_PAD), jnp.bfloat16),
            pltpu.VMEM((7, 16, PIX_PAD), jnp.bfloat16),
            pltpu.VMEM(block, jnp.bfloat16),
            pltpu.VMEM(block, jnp.float32),
            dma((9,)),
            dma((16,)),
            dma((16,)),
            dma((2, 9, 2)),
            dma((2, 9, 2)),
            dma((2, 9)),
            dma((2, 9)),
            dma((32,)),
            dma((32,)),
            dma((32,)),
            dma((32,)),
            dma((2, 20)),
            dma((2, 20)),
            dma((2, 16)),
            dma((2, 16)),
            dma((4, 2)),
            dma((4, 2)),
            dma((4,)),
            dma((4,)),
            dma((2,)),
            dma((4,)),
            dma((7,)),
            dma((16,)),
            dma((16,)),
            dma((7,)),
            dma,
            dma,
        ],
        compiler_params=pltpu.CompilerParams(
            collective_id=0, has_side_effects=True, vmem_limit_bytes=58 * 1024 * 1024
        ),
    )(weight, latent, scale, bias, gain, shift, pixels, cotangent, length, source, target)


def per_device(
    pixels,
    latent,
    quant_scale,
    embed_bias,
    ln_gain,
    ln_bias,
    qkv_weight,
    cotangent,
    image_length,
    image_source,
    image_target,
):
    return whole(
        qkv_weight.T,
        latent.T,
        quant_scale,
        embed_bias,
        ln_gain,
        ln_bias,
        pixels,
        cotangent,
        image_length,
        image_source,
        image_target,
    )


def solution(mesh):
    placed = (
        P(("dp", "bal"), None),
        P(),
        P(),
        P(),
        P(),
        P(),
        P(None, "dp"),
        P(("dp", "bal"), None),
        P("dp", None),
        P("dp", None),
        P("dp", None),
    )
    return jax.shard_map(
        per_device,
        mesh=mesh,
        in_specs=placed,
        out_specs=(P(("dp", "bal"), None), P("bal", None), P("bal")),
        check_vma=False,
    )
```

```python
import math

import jax
import jax.numpy as jnp
from jax import lax
from jax.experimental import pallas as pl
from jax.experimental.pallas import tpu as pltpu
from jax.sharding import PartitionSpec as P

D = 1792
HEAD = 112
PIX = 588
HEADS = 8
MOVE_ROWS = 128
EPSILON = 1e-06
MESH = pl.DeviceIdType.MESH
SHARD = 168
MAIN = 128
REST_PAD = 48
CHIP_ROWS = 112
PIX_PAD = 640
PIECES = 20


def place():
    z = lax.axis_index("dp")
    b = lax.axis_index("bal")
    core = lax.rem(b, 2)
    x = lax.rem(b // 2, 4)
    y = b // 8
    return z, b, x, y, core


def remote(src, dst, send, recv, device):
    copy = pltpu.make_async_remote_copy(
        src_ref=src, dst_ref=dst, send_sem=send, recv_sem=recv, device_id=device, device_id_type=MESH
    )
    return copy


def whole_kernel(
    weight_in,
    latent_in,
    scale_in,
    bias_in,
    gain_in,
    shift_in,
    pixels_in,
    cotangent_in,
    length_ref,
    source_ref,
    target_ref,
    attended_ref,
    latent_out,
    scale_out,
    w_ref,
    latent_ref,
    vectors,
    pixels_ref,
    cotangent_ref,
    sender_vector,
    sender_ref,
    slope,
    within,
    moved_ref,
    embedded_ref,
    projected_ref,
    column_id_ref,
    row_id_ref,
    main,
    rest,
    rows_in,
    pieces,
    inbox,
    stage,
    arrived,
    quant,
    normed,
    part_main,
    part_rest,
    grad_out,
    attended,
    grad_projected,
    grad_main,
    grad_rest,
    grad_normed,
    grad_embedded,
    grad_ref,
    twin,
    held,
    across,
    line,
    met,
    tiles,
    total,
    summed,
    final,
    load_sem,
    z_send,
    z_recv,
    ring_send,
    ring_recv,
    hand_send,
    hand_recv,
    out_send,
    out_recv,
    back_send,
    back_recv,
    plane_send,
    plane_recv,
    pair_send,
    pair_recv,
    twin_send,
    twin_recv,
    across_send,
    across_recv,
    line_send,
    line_recv,
    tile_send,
    tile_recv,
    total_send,
    total_recv,
):
    z, b, x, y, core = place()
    sibling = b + 1 - 2 * core
    chip = b // 2
    quad = z // 4
    barrier = pltpu.get_barrier_semaphore()

    def greet_plane(step, carry):
        pl.semaphore_signal(
            barrier, inc=1, device_id=(z, lax.rem(b + step, 32)), device_id_type=MESH
        )
        return carry

    def greet_line(step, carry):
        pl.semaphore_signal(
            barrier, inc=1, device_id=(lax.rem(z + step, 16), b), device_id_type=MESH
        )
        return carry

    def greet_other(step, carry):
        pl.semaphore_signal(
            barrier, inc=1, device_id=(lax.rem(z + step, 16), sibling), device_id_type=MESH
        )
        return carry

    loads = []
    for index, (source, held_at) in enumerate(
        (
            (weight_in, w_ref),
            (pixels_in, pixels_ref),
            (latent_in, latent_ref),
            (scale_in, vectors.at[0]),
            (bias_in, vectors.at[1]),
            (gain_in, vectors.at[2]),
            (shift_in, vectors.at[3]),
            (cotangent_in, cotangent_ref),
        )
    ):
        loads.append(pltpu.make_async_copy(source, held_at, load_sem.at[index]))
        loads[-1].start()
    scale_ref, bias_ref, gain_ref, shift_ref = (vectors.at[pl.ds(i, 1)] for i in range(4))
    lax.fori_loop(1, 16, greet_line, 0)
    lax.fori_loop(1, 16, greet_other, 0)
    lax.fori_loop(1, 32, greet_plane, 0)

    def slice_rows(where):
        return pl.ds(pl.multiple_of((where // 2) * 16, 16), 16)

    def slice_lanes(where):
        return pl.ds(pl.multiple_of(lax.rem(where, 2) * 896, 128), 896)

    loads[0].wait()

    @pl.when(core == 0)
    def _():
        main[z, slice_rows(chip), slice_lanes(chip)] = w_ref[slice_rows(chip), slice_lanes(chip)]

    def rest_rows(plane):
        return pl.ds(pl.multiple_of(plane * REST_PAD, 16), REST_PAD)

    rest[rest_rows(z), :] = jnp.concatenate(
        [w_ref[pl.ds(MAIN, SHARD - MAIN), :], jnp.zeros((REST_PAD - SHARD + MAIN, D), jnp.bfloat16)],
        axis=0,
    )
    pl.semaphore_wait(barrier, 61)

    def z_copy(step):
        to = lax.rem(z + step, 16)
        return remote(
            w_ref.at[slice_rows(chip), slice_lanes(chip)],
            main.at[z, slice_rows(chip), slice_lanes(chip)],
            z_send.at[step],
            z_recv.at[z],
            (to, b),
        )

    def z_mine(step):
        return lax.rem(lax.rem(z + step, 16) // 4 + quad, 2) == core

    steps = (1, 15, 2, 14, 3, 13, 4, 12, 5, 11, 6, 10, 7, 9, 8)

    def z_early(step):
        to = lax.rem(z + step, 16)
        base = (to // 4) * (1 - core) + core * (to // 4 + 3 + 2 * (lax.rem(to, 4) // 2))
        return lax.rem(base, 4) == quad

    for step in steps:

        @pl.when(z_mine(step) & z_early(step))
        def _():
            z_copy(step).start()

    def half_lanes(which, part):
        start, count = ((0, 512), (512, 384))[part]
        return pl.ds(pl.multiple_of(which * 896 + start, 128), count)

    def ring_copy(way, step, part):
        sign = 1 if way == 0 else -1
        origin = lax.rem(z - sign * (step - 1) + 16, 16)
        to = lax.rem(z + sign + 16, 16)
        block = rest.at[rest_rows(origin), half_lanes(core, part)]
        return remote(
            block, block, ring_send.at[way, step, part], ring_recv.at[way, step, part], (to, b)
        )

    def ring_wait(way, step, part):
        sign = 1 if way == 0 else -1
        origin = lax.rem(z - sign * step + 16, 16)
        block = rest.at[rest_rows(origin), half_lanes(core, part)]
        remote(
            block,
            block,
            ring_send.at[way, step, part],
            ring_recv.at[way, step, part],
            (lax.rem(z + 1, 16), b),
        ).wait_recv()

    def hand_copy(which, way, step):
        sign = 1 if way == 0 else -1
        origin = lax.rem(z - sign * step + 16, 16)
        block = rest.at[
            rest_rows(origin), pl.ds(pl.multiple_of(which * 896, 128), 896)
        ]
        return remote(
            block, block, hand_send.at[way, step], hand_recv.at[way, step], (z, sibling)
        )

    last = (8, 7)
    for way in range(2):
        ring_copy(way, 1, 0).start()

    def ring_step(part, step):
        for way in range(2):
            if step <= last[way]:
                ring_wait(way, step, part)
                if step < last[way]:
                    ring_copy(way, step + 1, part).start()
        if part == 1:
            for way in range(2):
                if step <= last[way]:
                    hand_copy(core, way, step).start()

    length_row = length_ref[...].astype(jnp.float32)
    source_row = source_ref[...].astype(jnp.float32)
    target_row = target_ref[...].astype(jnp.float32)
    entries = length_row.shape[1]

    def turned(row):
        return jnp.broadcast_to(row, (entries, entries)).T

    length_col, source_col, target_col = turned(length_row), turned(source_row), turned(target_row)
    down = lax.broadcasted_iota(jnp.int32, (entries, entries), 0)
    along = lax.broadcasted_iota(jnp.int32, (entries, entries), 1)
    member = b.astype(jnp.float32)

    def above(owner_col, owner_row, amount_col):
        match = (down < along) & (owner_col == owner_row)
        return jnp.sum(jnp.where(match, amount_col, 0.0), axis=0, keepdims=True)

    target_start = above(target_col, target_row, length_col)
    source_start = above(source_col, source_row, length_col)
    moving_col = jnp.where(target_col != source_col, length_col, 0.0)
    outbox_start = above(source_col, source_row, moving_col)
    before = (along < down) & (target_col == target_row)
    target_start_col = jnp.sum(jnp.where(before, length_row, 0.0), axis=1, keepdims=True)

    slots = lax.broadcasted_iota(jnp.int32, (MOVE_ROWS, entries), 0).astype(jnp.float32)
    leaving = (
        (source_row == member)
        & (target_row != source_row)
        & (slots >= outbox_start)
        & (slots < outbox_start + length_row)
    )
    leaving_row = jnp.sum(
        jnp.where(leaving, source_start - outbox_start + slots, 0.0), axis=1, keepdims=True
    )
    leaving_any = jnp.sum(jnp.where(leaving, 1.0, 0.0), axis=1, keepdims=True)
    leaving_row = jnp.where(leaving_any > 0.0, leaving_row, -1.0)
    count_in = pixels_ref.shape[0]
    whole_col = [turned(ref[...]) for ref in (length_ref, source_ref, target_ref)]
    senders = jnp.where(
        (whole_col[2] == along) & (whole_col[2] != whole_col[1]) & (whole_col[0] > 0), whole_col[1], 0
    )
    sender_vector[...] = jnp.sum(senders, axis=0, keepdims=True)
    load_sender = pltpu.make_async_copy(sender_vector, sender_ref, load_sem.at[8])
    load_sender.start()
    loads[1].wait()
    rows_in[:, pl.ds(512, 128)] = jnp.zeros((rows_in.shape[0], 128), jnp.bfloat16)
    rows_in[pl.ds(0, count_in), pl.ds(0, PIX)] = pixels_ref[...]
    picks = lax.broadcasted_iota(jnp.int32, (MOVE_ROWS, count_in), 1).astype(jnp.float32)
    outgoing = jnp.dot(
        jnp.where(leaving_row == picks, 1.0, 0.0).astype(jnp.bfloat16),
        rows_in[pl.ds(0, count_in), :],
        preferred_element_type=jnp.float32,
    ).astype(jnp.bfloat16)
    for i in range(4):
        for j in range(5):
            pieces[5 * i + j] = outgoing[32 * i : 32 * i + 32, 128 * j : 128 * j + 128]

    def out_copy(target, slot):
        return remote(
            pieces.at[target], inbox.at[slot], out_send.at[target], out_recv.at[slot], (z, target)
        )

    def back_copy(target, slot):
        return remote(
            stage.at[target], arrived.at[slot], back_send.at[target], back_recv.at[slot], (z, target)
        )

    def send_out(step, carry):
        target = lax.rem(b + step, 32)

        @pl.when(target < PIECES)
        def _():
            out_copy(target, b).start()

        return carry

    lax.fori_loop(1, 32, send_out, 0)

    for step in steps:

        @pl.when(z_mine(step) & jnp.logical_not(z_early(step)))
        def _():
            z_copy(step).start()

    def quad_of(which, chunk):
        base = quad * (1 - which) + which * (quad + 3 + 2 * (lax.rem(z, 4) // 2))
        return lax.rem(base + 2 * chunk, 4)

    def chip_at(which, chunk, first, second):
        swap = lax.rem(which + chunk, 2)
        dx = first * (1 - swap) + second * swap
        dy = first * swap + second * (1 - swap)
        return lax.rem(y + dy + 4, 4) * 4 + lax.rem(x + dx + 4, 4)

    def piece(which, chunk, where, low=0, count=4):
        return main.at[
            pl.ds(4 * quad_of(which, chunk) + low, count), slice_rows(where), slice_lanes(where)
        ]

    offsets = (0, -1, 1, 2)
    spans = ((0, 4), (0, 4), (0, 2), (2, 2))

    def hop(chunk, index, axis, place_index, kind):
        low, count = spans[kind]
        sign = 1 if kind in (0, 2) else -1
        origin = (0, 0, -1, 1)[kind]
        a = offsets[place_index]
        if axis == 0:
            to, sent = chip_at(core, chunk, sign, 0), chip_at(core, chunk, origin, 0)
        else:
            to, sent = chip_at(core, chunk, 0, sign), chip_at(core, chunk, a, origin)
        rows = piece(core, chunk, sent, low, count)
        return remote(
            rows, rows, plane_send.at[chunk, index], plane_recv.at[chunk, index], (z, to * 2 + core)
        )

    def hop_wait(chunk, index, axis, place_index, kind):
        low, count = spans[kind]
        origin = (-1, 1, 2, 2)[kind]
        a = offsets[place_index]
        if axis == 0:
            sent = chip_at(core, chunk, origin, 0)
        else:
            sent = chip_at(core, chunk, a, origin)
        rows = piece(core, chunk, sent, low, count)
        remote(
            rows, rows, plane_send.at[chunk, index], plane_recv.at[chunk, index], (z, sibling)
        ).wait_recv()

    def first_copy(chunk, kind):
        return hop(chunk, kind, 0, 0, kind)

    def first_wait(chunk, kind):
        hop_wait(chunk, kind, 0, 0, kind)

    def second_copy(chunk, place_index, kind):
        return hop(chunk, 4 + 4 * place_index + kind, 1, place_index, kind)

    def second_wait(chunk, place_index, kind):
        hop_wait(chunk, 4 + 4 * place_index + kind, 1, place_index, kind)

    def pair_copy(which, chunk, place_index, second_index):
        rows = piece(
            which, chunk, chip_at(which, chunk, offsets[place_index], offsets[second_index])
        )
        index = place_index * 4 + second_index
        return remote(
            rows, rows, pair_send.at[chunk, index], pair_recv.at[chunk, index], (z, sibling)
        )

    def chunk_start(chunk):
        for j in range(4):
            origin = 4 * quad_of(core, chunk) + j

            @pl.when(origin != z)
            def _():
                rows = main.at[origin, slice_rows(chip), slice_lanes(chip)]
                remote(rows, rows, z_send.at[0], z_recv.at[origin], (z, sibling)).wait_recv()

        first_copy(chunk, 0).start()
        first_copy(chunk, 1).start()
        second_copy(chunk, 0, 0).start()
        second_copy(chunk, 0, 1).start()
        pair_copy(core, chunk, 0, 0).start()

    def chunk_first(chunk):
        for kind, index in ((0, 1), (1, 2)):
            first_wait(chunk, kind)
            first_copy(chunk, kind + 2).start()
            second_copy(chunk, index, 0).start()
            second_copy(chunk, index, 1).start()
            pair_copy(core, chunk, index, 0).start()

    def chunk_far(chunk):
        first_wait(chunk, 2)
        first_wait(chunk, 3)
        second_copy(chunk, 3, 0).start()
        second_copy(chunk, 3, 1).start()
        pair_copy(core, chunk, 3, 0).start()

    def chunk_second(chunk, index):
        for kind in (0, 1):
            second_wait(chunk, index, kind)
            second_copy(chunk, index, kind + 2).start()
            pair_copy(core, chunk, index, kind + 1).start()

    def chunk_last(chunk, index):
        second_wait(chunk, index, 2)
        second_wait(chunk, index, 3)
        pair_copy(core, chunk, index, 3).start()

    def quantize_part(part, carry):
        lanes = pl.ds(pl.multiple_of(part * 256, 128), 256)
        scale = scale_ref[:, lanes]
        level = jnp.floor(latent_ref[:, lanes].astype(jnp.float32) / scale + 0.5)
        quant[pl.ds(0, PIX), lanes] = (jnp.clip(level, -8.0, 7.0) * scale).astype(jnp.bfloat16)
        return carry

    def embed_part(part, carry):
        lanes = pl.ds(pl.multiple_of(part * 256, 128), 256)
        total = jnp.dot(moved_ref[...], quant[:, lanes], preferred_element_type=jnp.float32)
        embedded_ref[:, lanes] = (total + bias_ref[:, lanes]).astype(jnp.bfloat16)
        return carry

    def norm_part(part, carry):
        rows = pl.ds(pl.multiple_of(part * 32, 32), 32)
        values = embedded_ref[rows, :].astype(jnp.float32)
        centered = values - jnp.mean(values, axis=1, keepdims=True)
        variance = jnp.mean(centered * centered, axis=1, keepdims=True)
        hat = centered * lax.rsqrt(variance + EPSILON)
        normed[rows, :] = (hat * gain_ref[...] + shift_ref[...]).astype(jnp.bfloat16)
        return carry

    chunk_start(0)
    for way in range(2):
        ring_copy(way, 1, 1).start()
    ring_step(0, 1)
    load_sender.wait()

    @pl.when(b < PIECES)
    def _():
        inbox[b] = pieces[b]

        def take(step, carry):
            out_copy(b, lax.rem(b + step, 32)).wait_recv()
            return carry

        lax.fori_loop(1, 32, take, 0)
        arrived[b] = inbox[jnp.clip(sender_ref[0, b], 0, 31)]

        def send_back(step, carry):
            target = lax.rem(b + step, 32)
            stage[target] = inbox[jnp.clip(sender_ref[0, target], 0, 31)]
            back_copy(target, b).start()
            return carry

        lax.fori_loop(1, 32, send_back, 0)

    chunk_first(0)
    ring_step(1, 1)
    ring_step(0, 2)
    quant[pl.ds(576, 64), :] = jnp.zeros((64, D), jnp.bfloat16)
    for index in range(2, 7):
        loads[index].wait()
    lax.fori_loop(0, 7, quantize_part, 0)
    share = D // 32
    window = jnp.minimum(chip * CHIP_ROWS // 128 * 128, D - 256)
    lanes = pl.ds(pl.multiple_of(window, 128), 256)
    ratio = latent_ref[:, lanes].astype(jnp.float32) / scale_ref[:, lanes]
    level = jnp.floor(ratio + 0.5)
    inside = (level >= -8.0) & (level <= 7.0)
    slope[...] = jnp.where(inside, level - ratio, jnp.clip(level, -8.0, 7.0)).T
    within[...] = jnp.where(inside, 1.0, 0.0).T
    share_rows = pl.ds(pl.multiple_of(chip * CHIP_ROWS - window + core * share, 8), share)
    chunk_far(0)
    chunk_second(0, 0)
    ring_step(1, 2)
    ring_step(0, 3)

    row = lax.broadcasted_iota(jnp.int32, (moved_ref.shape[0], entries), 0).astype(jnp.float32)
    covers = (target_row == member) & (row >= target_start) & (row < target_start + length_row)
    take_from = (
        jnp.where(source_row == member, source_start, outbox_start + float(count_in)) - target_start
    )
    wanted = jnp.sum(jnp.where(covers, take_from + row, 0.0), axis=1, keepdims=True)
    entry = (lax.broadcasted_iota(jnp.int32, (1, entries), 1) + 1).astype(jnp.float32)
    image = jnp.sum(jnp.where(covers, entry, 0.0), axis=1, keepdims=True)
    wanted = jnp.where(image > 0.0, wanted, -1.0)
    column_id_ref[...] = image
    row_lane = lax.broadcasted_iota(jnp.int32, (entries, moved_ref.shape[0]), 1).astype(jnp.float32)
    covers_turned = (
        (target_col[:, :1] == member)
        & (row_lane >= target_start_col)
        & (row_lane < target_start_col + length_col[:, :1])
    )
    entry_down = (lax.broadcasted_iota(jnp.int32, (entries, 1), 0) + 1).astype(jnp.float32)
    row_id_ref[...] = jnp.sum(jnp.where(covers_turned, entry_down, 0.0), axis=0, keepdims=True)

    def arrive(step, carry):
        slot = lax.rem(b + step, 32)

        @pl.when(slot < PIECES)
        def _():
            back_copy(b, slot).wait_recv()

        return carry

    lax.fori_loop(1, 32, arrive, 0)
    for i in range(4):
        for j in range(5):
            rows_in[pl.ds(count_in + 32 * i, 32), pl.ds(128 * j, 128)] = arrived[5 * i + j]
    choose = lax.broadcasted_iota(
        jnp.int32, (moved_ref.shape[0], count_in + MOVE_ROWS), 1
    ).astype(jnp.float32)
    moved_ref[...] = jnp.dot(
        jnp.where(wanted == choose, 1.0, 0.0).astype(jnp.bfloat16),
        rows_in[...],
        preferred_element_type=jnp.float32,
    ).astype(jnp.bfloat16)
    chunk_second(0, 1)
    chunk_start(1)
    ring_step(1, 3)
    ring_step(0, 4)
    lax.fori_loop(0, 4, embed_part, 0)
    chunk_second(0, 2)
    chunk_first(1)
    ring_step(1, 4)
    ring_step(0, 5)
    lax.fori_loop(4, 7, embed_part, 0)
    chunk_second(0, 3)
    chunk_far(1)
    chunk_second(1, 0)
    ring_step(1, 5)
    ring_step(0, 6)
    lax.fori_loop(0, 4, norm_part, 0)
    chunk_second(1, 1)
    for index in range(4):
        chunk_last(0, index)
    ring_step(1, 6)
    ring_step(0, 7)
    lax.fori_loop(4, 8, norm_part, 0)
    chunk_second(1, 2)
    ring_step(1, 7)
    ring_step(0, 8)
    chunk_second(1, 3)
    ring_step(1, 8)
    for index in range(4):
        chunk_last(1, index)

    def project(which, chunk):
        q = quad_of(which, chunk)
        for pair in range(2):
            block = main[pl.ds(4 * q + 2 * pair, 2)].reshape(256, D)
            part_main[4 * q // 2 + pair] = lax.dot_general(
                normed[...], block, (((1,), (1,)), ((), ())), preferred_element_type=jnp.float32
            ).astype(jnp.bfloat16)

    def pair_wait(chunk):
        for index in range(4):
            for second in range(4):
                pair_copy(1 - core, chunk, index, second).wait_recv()

    project(core, 0)
    pair_wait(0)
    project(1 - core, 0)
    project(core, 1)
    pair_wait(1)
    project(1 - core, 1)
    for way in range(2):
        for step in range(1, last[way] + 1):
            hand_copy(1 - core, way, step).wait_recv()
    for part in range(3):
        part_rest[:, 256 * part : 256 * part + 256] = lax.dot_general(
            normed[...],
            rest[pl.ds(256 * part, 256), :],
            (((1,), (1,)), ((), ())),
            preferred_element_type=jnp.float32,
        ).astype(jnp.bfloat16)
    joined = []
    for plane in range(16):
        joined.append(part_main[plane // 2, :, 128 * (plane % 2) : 128 * (plane % 2) + 128])
        joined.append(part_rest[:, REST_PAD * plane : REST_PAD * plane + SHARD - MAIN])
    projected_ref[...] = jnp.concatenate(joined, axis=1)

    loads[7].wait()
    width = HEADS * HEAD
    score_scale = HEAD ** (-0.5)
    grad_factor = 1.0 / math.sqrt(131072.0)
    column_id = column_id_ref[...]
    row_id = row_id_ref[...]
    active = column_id > 0.0
    same = (column_id == row_id) & active
    grad_out[...] = jnp.where(
        active, cotangent_ref[...].astype(jnp.float32) * grad_factor, 0.0
    ).astype(jnp.bfloat16)
    attended[...] = jnp.zeros_like(attended)
    grad_projected[...] = jnp.zeros_like(grad_projected)
    by_rows = (((1,), (1,)), ((), ()))
    by_columns = (((0,), (0,)), ((), ()))

    def dot(left, right, contract=(((1,), (0,)), ((), ()))):
        return lax.dot_general(left, right, contract, preferred_element_type=jnp.float32)

    for head in range(HEADS):
        start = HEAD * head // 128 * 128
        stop = -(-(HEAD * head + HEAD) // 128) * 128
        span = stop - start
        lane = lax.broadcasted_iota(jnp.int32, (1, span), 1) + start
        own = (lane >= HEAD * head) & (lane < HEAD * head + HEAD)

        def window(ref, base=0):
            return ref[:, base + start : base + stop]

        def masked(value):
            return jnp.where(own, value, jnp.zeros_like(value))

        queries, keys, values = (window(projected_ref, width * i) for i in range(3))
        out = window(grad_out)
        keys, values = masked(keys), masked(values)
        scores = dot(queries, keys, by_rows) * score_scale
        exponent = jnp.where(same, jnp.exp(scores), 0.0)
        denominator = jnp.sum(exponent, axis=1, keepdims=True)
        attention = exponent / jnp.where(active, denominator, 1.0)
        soft = attention.astype(jnp.bfloat16)
        attended[:, start:stop] += dot(soft, values)
        grad_attention = dot(out, values, by_rows)
        inner = jnp.sum(attention * grad_attention, axis=1, keepdims=True)
        grad_score = (attention * (grad_attention - inner) * score_scale).astype(jnp.bfloat16)
        grad_projected[:, start:stop] += dot(grad_score, keys)
        grad_projected[:, width + start : width + stop] += dot(
            grad_score, masked(queries), by_columns
        )
        grad_projected[:, 2 * width + start : 2 * width + stop] += dot(
            soft, masked(out), by_columns
        )
    attended_ref[...] = attended[...].astype(jnp.bfloat16)
    rounded = grad_projected[...].astype(jnp.bfloat16)
    pad = jnp.zeros((rounded.shape[0], REST_PAD - SHARD + MAIN), jnp.bfloat16)
    mains, rests = [], []
    for plane in range(16):
        base = SHARD * plane
        mains.append(rounded[:, base : base + MAIN])
        rests.append(rounded[:, base + MAIN : base + SHARD])
        rests.append(pad)
    grad_main[...] = jnp.concatenate(mains, axis=1)
    grad_rest[...] = jnp.concatenate(rests, axis=1)

    def back_part(part, carry):
        lanes = pl.ds(pl.multiple_of(part * 256, 128), 256)
        grad_normed[:, lanes] = dot(
            grad_main[...], main[:, :, lanes].reshape(16 * MAIN, 256)
        ) + dot(grad_rest[...], rest[:, lanes])
        return carry

    lax.fori_loop(0, 7, back_part, 0)

    def back_norm_part(part, carry):
        rows = pl.ds(pl.multiple_of(part * 32, 32), 32)
        values = embedded_ref[rows, :].astype(jnp.float32)
        centered = values - jnp.mean(values, axis=1, keepdims=True)
        variance = jnp.mean(centered * centered, axis=1, keepdims=True)
        inverse = lax.rsqrt(variance + EPSILON)
        hat = centered * inverse
        gained = grad_normed[rows, :] * gain_ref[...]
        result = inverse * (
            gained
            - jnp.mean(gained, axis=1, keepdims=True)
            - hat * jnp.mean(gained * hat, axis=1, keepdims=True)
        )
        grad_embedded[rows, :] = jnp.where(column_id_ref[rows, :] > 0.0, result, 0.0).astype(
            jnp.bfloat16
        )
        return carry

    lax.fori_loop(0, 8, back_norm_part, 0)
    for part in range(2):
        block = dot(grad_embedded[:, 896 * part : 896 * part + 896], moved_ref[...], by_columns)
        grad_ref[8 * part : 8 * part + 8] = block.astype(jnp.bfloat16).reshape(
            8, CHIP_ROWS, PIX_PAD
        )
    first = x * (1 - core) + y * core
    second = y * (1 - core) + x * core
    parts = ((0, 256), (256, 256), (512, 128))

    def chip_of(which, f, s):
        return (s * 4 + f) * (1 - which) + (f * 4 + s) * which

    def target_chip(which, a, half):
        mine = x * (1 - which) + y * which
        f = lax.rem(mine + a, 4)
        return chip_of(which, f, 2 * half + lax.rem(f + which, 2))

    def at(f, s):
        return (z, chip_of(core, f, s) * 2 + core)

    def columns(k):
        return pl.ds(*parts[k])

    def wide(value):
        return value.astype(jnp.float32)

    def twin_copy(a, half, k):
        return remote(
            grad_ref.at[target_chip(1 - core, a, half), :, columns(k)],
            twin.at[a, half, :, columns(k)],
            twin_send.at[a, half, k],
            twin_recv.at[a, half, k],
            (z, sibling),
        )

    def across_copy(a, k):
        return remote(
            held.at[a, :, :, columns(k)],
            across.at[a, :, :, columns(k)],
            across_send.at[a, k],
            across_recv.at[a, k],
            at(lax.rem(first + a, 4), second),
        )

    order = (2, 1, 3, 0)
    spread = range(len(parts))
    for k in spread:
        for a in order:
            for half in range(2):
                twin_copy(a, half, k).start()
    for k in spread:
        for a in order:
            for half in range(2):
                twin_copy(a, half, k).wait_recv()
                chip_here = target_chip(core, a, half)
                held[a, half, :, columns(k)] = (
                    wide(grad_ref[chip_here, :, columns(k)]) + wide(twin[a, half, :, columns(k)])
                ).astype(jnp.bfloat16)
            if a > 0:
                across_copy(a, k).start()

    parity = lax.rem(first + core, 2)
    owner = lax.rem(first + second, 2) == core

    def line_copy(half, k):
        to = 2 * half + parity
        away = lax.rem(to - second + 4, 4)
        return remote(
            line.at[half, :, columns(k)],
            met.at[away, :, columns(k)],
            line_send.at[half, k],
            line_recv.at[away, k],
            at(first, to),
        )

    for k in spread:
        for a in (1, 3, 2):
            across_copy(a, k).wait_recv()
        for half in range(2):
            line[half, :, columns(k)] = (
                wide(held[0, half, :, columns(k)])
                + wide(across[1, half, :, columns(k)])
                + wide(across[2, half, :, columns(k)])
                + wide(across[3, half, :, columns(k)])
            ).astype(jnp.bfloat16)

            @pl.when(2 * half + parity != second)
            def _():
                line_copy(half, k).start()

    def tile_copy(index, k):
        return remote(
            summed.at[pl.ds(16 * index, 16), columns(k)],
            tiles.at[z, :, columns(k)],
            tile_send.at[index, k],
            tile_recv.at[z, k],
            (2 * index, b),
        )

    for k in spread:

        @pl.when(owner)
        def _():
            mine = wide(line[second // 2, :, columns(k)])
            for away in (1, 3, 2):
                remote(
                    line.at[0, :, columns(k)],
                    met.at[away, :, columns(k)],
                    line_send.at[0, k],
                    line_recv.at[away, k],
                    (z, sibling),
                ).wait_recv()
                mine = mine + wide(met[away, :, columns(k)])
            summed[:, columns(k)] = mine.astype(jnp.bfloat16)
            for index in range(7):

                @pl.when(z != 2 * index)
                def _():
                    tile_copy(index, k).start()

    collector = owner & (z < 14) & (lax.rem(z, 2) == 0)
    tile_index = jnp.minimum(z // 2, 6)

    def total_copy(step, which, k):
        return remote(
            total.at[tile_index, :, columns(k)],
            total.at[tile_index, :, columns(k)],
            total_send.at[step, which, k],
            total_recv.at[tile_index, k],
            (lax.rem(z + step, 16), chip * 2 + which),
        )

    def total_goes(step, which):
        wanted_there = (tile_index <= 3) if which == 0 else (tile_index >= 3)
        return wanted_there & ((step != 0) | (core != which))

    for k in spread:

        @pl.when(collector)
        def _():
            tile_rows = pl.ds(pl.multiple_of(16 * tile_index, 16), 16)
            tiles[z, :, columns(k)] = summed[tile_rows, columns(k)]

            def take(step, carry):
                slot = lax.rem(z + step, 16)
                remote(
                    summed.at[pl.ds(0, 16), columns(k)],
                    tiles.at[slot, :, columns(k)],
                    tile_send.at[0, k],
                    tile_recv.at[slot, k],
                    (slot, b),
                ).wait_recv()
                return carry

            lax.fori_loop(1, 16, take, 0)
            value = wide(tiles[0, :, columns(k)])
            for slot in range(1, 16):
                value = value + wide(tiles[slot, :, columns(k)])
            total[tile_index, :, columns(k)] = value.astype(jnp.bfloat16)

            def give(step, carry):
                for which in range(2):

                    @pl.when(total_goes(step, which))
                    def _():
                        total_copy(step, which, k).start()

                return carry

            lax.fori_loop(0, 16, give, 0)

    for k in spread:
        for j in range(4):
            index = 3 * core + j

            @pl.when(jnp.logical_not(owner & (z == 2 * index)))
            def _():
                remote(
                    total.at[index, :, columns(k)],
                    total.at[index, :, columns(k)],
                    total_send.at[0, 0, k],
                    total_recv.at[index, k],
                    (z, sibling),
                ).wait_recv()

    final[...] = wide(total[pl.ds(3 * core, 4)]).reshape(64, PIX_PAD)
    mine = final[pl.ds(pl.multiple_of(core * 8, 8), share), pl.ds(0, PIX)]
    latent_out[...] = jnp.where(within[share_rows, :] > 0.0, mine, 0.0)
    scale_out[...] = (1.0 / math.sqrt(PIX * 7.0)) * jnp.sum(mine * slope[share_rows, :], axis=1)

    for k in spread:
        for a in range(4):
            for half in range(2):
                twin_copy(a, half, k).wait_send()
            if a > 0:
                across_copy(a, k).wait_send()
        for half in range(2):

            @pl.when(2 * half + parity != second)
            def _():
                line_copy(half, k).wait_send()

        @pl.when(owner)
        def _():
            for index in range(7):

                @pl.when(z != 2 * index)
                def _():
                    tile_copy(index, k).wait_send()

        @pl.when(collector)
        def _():
            def given(step, carry):
                for which in range(2):

                    @pl.when(total_goes(step, which))
                    def _():
                        total_copy(step, which, k).wait_send()

                return carry

            lax.fori_loop(0, 16, given, 0)

    for step in range(1, 16):

        @pl.when(z_mine(step))
        def _():
            z_copy(step).wait_send()

    for way in range(2):
        for step in range(1, last[way] + 1):
            for part in range(2):
                ring_copy(way, step, part).wait_send()
            hand_copy(core, way, step).wait_send()

    def sent_out(step, carry):
        target = lax.rem(b + step, 32)

        @pl.when(target < PIECES)
        def _():
            out_copy(target, b).wait_send()

        return carry

    lax.fori_loop(1, 32, sent_out, 0)

    @pl.when(b < PIECES)
    def _():
        def sent_back(step, carry):
            back_copy(lax.rem(b + step, 32), b).wait_send()
            return carry

        lax.fori_loop(1, 32, sent_back, 0)

    for chunk in range(2):
        for kind in range(4):
            first_copy(chunk, kind).wait_send()
            for index in range(4):
                second_copy(chunk, index, kind).wait_send()
        for index in range(4):
            for second in range(4):
                pair_copy(core, chunk, index, second).wait_send()


def deliver_kernel(*refs):
    sems = refs[-1]
    copies = [pltpu.make_async_copy(refs[i], refs[3 + i], sems.at[i]) for i in range(3)]
    for copy in copies:
        copy.start()
    for copy in copies:
        copy.wait()


def deliver(*arrays):
    anywhere = pl.BlockSpec(memory_space=pl.ANY)
    return pl.pallas_call(
        deliver_kernel,
        name="deliver",
        out_shape=tuple(jax.ShapeDtypeStruct(a.shape, a.dtype) for a in arrays),
        in_specs=[anywhere] * 3,
        out_specs=(anywhere,) * 3,
        scratch_shapes=[pltpu.SemaphoreType.DMA((3,))],
    )(*arrays)


def whole(weight, latent, scale, bias, gain, shift, pixels, cotangent, length, source, target):
    vmem = pl.BlockSpec(memory_space=pltpu.VMEM)
    anywhere = pl.BlockSpec(memory_space=pl.ANY)
    dma = pltpu.SemaphoreType.DMA
    rows = cotangent.shape[0]
    block = (CHIP_ROWS, PIX_PAD)
    shape = jax.ShapeDtypeStruct
    return pl.pallas_call(
        whole_kernel,
        name="whole",
        out_shape=(
            shape((rows, HEADS * HEAD), jnp.bfloat16),
            shape((D // 32, PIX), jnp.float32),
            shape((D // 32,), jnp.float32),
        ),
        in_specs=[anywhere] * 8 + [vmem] * 3,
        out_specs=(vmem, vmem, vmem),
        scratch_shapes=[
            pltpu.VMEM((SHARD, D), jnp.bfloat16),
            pltpu.VMEM((PIX, D), jnp.bfloat16),
            pltpu.VMEM((8, D), jnp.float32),
            pltpu.VMEM(pixels.shape, jnp.bfloat16),
            pltpu.VMEM(cotangent.shape, jnp.bfloat16),
            pltpu.VMEM((1, 128), jnp.int32),
            pltpu.SMEM((1, 128), jnp.int32),
            pltpu.VMEM((256, PIX), jnp.float32),
            pltpu.VMEM((256, PIX), jnp.float32),
            pltpu.VMEM((rows, PIX_PAD), jnp.bfloat16),
            pltpu.VMEM((rows, D), jnp.bfloat16),
            pltpu.VMEM((rows, 16 * SHARD), jnp.bfloat16),
            pltpu.VMEM((rows, 1), jnp.float32),
            pltpu.VMEM((1, rows), jnp.float32),
            pltpu.VMEM((16, MAIN, D), jnp.bfloat16),
            pltpu.VMEM((16 * REST_PAD, D), jnp.bfloat16),
            pltpu.VMEM((pixels.shape[0] + MOVE_ROWS, PIX_PAD), jnp.bfloat16),
            pltpu.VMEM((PIECES, 32, 128), jnp.bfloat16),
            pltpu.VMEM((32, 32, 128), jnp.bfloat16),
            pltpu.VMEM((32, 32, 128), jnp.bfloat16),
            pltpu.VMEM((PIECES, 32, 128), jnp.bfloat16),
            pltpu.VMEM((PIX_PAD, D), jnp.bfloat16),
            pltpu.VMEM((rows, D), jnp.bfloat16),
            pltpu.VMEM((8, rows, 256), jnp.bfloat16),
            pltpu.VMEM((rows, 16 * REST_PAD), jnp.bfloat16),
            pltpu.VMEM((rows, HEADS * HEAD), jnp.bfloat16),
            pltpu.VMEM((rows, HEADS * HEAD), jnp.float32),
            pltpu.VMEM((rows, 16 * SHARD), jnp.float32),
            pltpu.VMEM((rows, 16 * MAIN), jnp.bfloat16),
            pltpu.VMEM((rows, 16 * REST_PAD), jnp.bfloat16),
            pltpu.VMEM((rows, D), jnp.float32),
            pltpu.VMEM((rows, D), jnp.bfloat16),
            pltpu.VMEM((D // CHIP_ROWS,) + block, jnp.bfloat16),
            pltpu.VMEM((4, 2) + block, jnp.bfloat16),
            pltpu.VMEM((4, 2) + block, jnp.bfloat16),
            pltpu.VMEM((4, 2) + block, jnp.bfloat16),
            pltpu.VMEM((2,) + block, jnp.bfloat16),
            pltpu.VMEM((4,) + block, jnp.bfloat16),
            pltpu.VMEM((16, 16, PIX_PAD), jnp.bfloat16),
            pltpu.VMEM((7, 16, PIX_PAD), jnp.bfloat16),
            pltpu.VMEM(block, jnp.bfloat16),
            pltpu.VMEM((64, PIX_PAD), jnp.float32),
            dma((9,)),
            dma((16,)),
            dma((16,)),
            dma((2, 9, 2)),
            dma((2, 9, 2)),
            dma((2, 9)),
            dma((2, 9)),
            dma((32,)),
            dma((32,)),
            dma((32,)),
            dma((32,)),
            dma((2, 20)),
            dma((2, 20)),
            dma((2, 16)),
            dma((2, 16)),
            dma((4, 2, 3)),
            dma((4, 2, 3)),
            dma((4, 3)),
            dma((4, 3)),
            dma((2, 3)),
            dma((4, 3)),
            dma((7, 3)),
            dma((16, 3)),
            dma((16, 2, 3)),
            dma((7, 3)),
        ],
        compiler_params=pltpu.CompilerParams(
            collective_id=0, has_side_effects=True, vmem_limit_bytes=58 * 1024 * 1024
        ),
    )(weight, latent, scale, bias, gain, shift, pixels, cotangent, length, source, target)


def per_device(
    pixels,
    latent,
    quant_scale,
    embed_bias,
    ln_gain,
    ln_bias,
    qkv_weight,
    cotangent,
    image_length,
    image_source,
    image_target,
):
    results = whole(
        qkv_weight.T,
        latent.T,
        quant_scale,
        embed_bias,
        ln_gain,
        ln_bias,
        pixels,
        cotangent,
        image_length,
        image_source,
        image_target,
    )
    return deliver(*results)


def solution(mesh):
    placed = (
        P(("dp", "bal"), None),
        P(),
        P(),
        P(),
        P(),
        P(),
        P(None, "dp"),
        P(("dp", "bal"), None),
        P("dp", None),
        P("dp", None),
        P("dp", None),
    )
    return jax.shard_map(
        per_device,
        mesh=mesh,
        in_specs=placed,
        out_specs=(P(("dp", "bal"), None), P("bal", None), P("bal")),
        check_vma=False,
    )
```

```python
import math

import jax
import jax.numpy as jnp
from jax import lax
from jax.experimental import pallas as pl
from jax.experimental.pallas import tpu as pltpu
from jax.sharding import PartitionSpec as P

D = 1792
HEAD = 112
PIX = 588
HEADS = 8
MOVE_ROWS = 128
EPSILON = 1e-06
MESH = pl.DeviceIdType.MESH
SHARD = 168
MAIN = 128
REST_PAD = 48
CHIP_ROWS = 112
PIX_PAD = 640
PIECES = 20


def place():
    z = lax.axis_index("dp")
    b = lax.axis_index("bal")
    core = lax.rem(b, 2)
    x = lax.rem(b // 2, 4)
    y = b // 8
    return z, b, x, y, core


def remote(src, dst, send, recv, device):
    copy = pltpu.make_async_remote_copy(
        src_ref=src, dst_ref=dst, send_sem=send, recv_sem=recv, device_id=device, device_id_type=MESH
    )
    return copy


def whole_kernel(
    weight_in,
    latent_in,
    scale_in,
    bias_in,
    gain_in,
    shift_in,
    pixels_in,
    cotangent_in,
    length_ref,
    source_ref,
    target_ref,
    attended_ref,
    latent_out,
    scale_out,
    w_ref,
    latent_ref,
    vectors,
    pixels_ref,
    cotangent_ref,
    sender_vector,
    sender_ref,
    slope,
    within,
    moved_ref,
    embedded_ref,
    projected_ref,
    column_id_ref,
    row_id_ref,
    main,
    rest,
    rows_in,
    pieces,
    inbox,
    stage,
    arrived,
    quant,
    normed,
    part_main,
    part_rest,
    grad_out,
    attended,
    grad_projected,
    grad_main,
    grad_rest,
    grad_normed,
    grad_embedded,
    grad_ref,
    twin,
    held,
    across,
    line,
    met,
    tiles,
    total,
    summed,
    final,
    load_sem,
    z_send,
    z_recv,
    ring_send,
    ring_recv,
    hand_send,
    hand_recv,
    out_send,
    out_recv,
    back_send,
    back_recv,
    plane_send,
    plane_recv,
    pair_send,
    pair_recv,
    twin_send,
    twin_recv,
    across_send,
    across_recv,
    line_send,
    line_recv,
    tile_send,
    tile_recv,
    total_send,
    total_recv,
):
    z, b, x, y, core = place()
    sibling = b + 1 - 2 * core
    chip = b // 2
    quad = z // 4
    barrier = pltpu.get_barrier_semaphore()

    def greet_plane(step, carry):
        pl.semaphore_signal(
            barrier, inc=1, device_id=(z, lax.rem(b + step, 32)), device_id_type=MESH
        )
        return carry

    def greet_line(step, carry):
        pl.semaphore_signal(
            barrier, inc=1, device_id=(lax.rem(z + step, 16), b), device_id_type=MESH
        )
        return carry

    def greet_other(step, carry):
        pl.semaphore_signal(
            barrier, inc=1, device_id=(lax.rem(z + step, 16), sibling), device_id_type=MESH
        )
        return carry

    loads = []
    for index, (source, held_at) in enumerate(
        (
            (weight_in, w_ref),
            (pixels_in, pixels_ref),
            (latent_in, latent_ref),
            (scale_in, vectors.at[0]),
            (bias_in, vectors.at[1]),
            (gain_in, vectors.at[2]),
            (shift_in, vectors.at[3]),
            (cotangent_in, cotangent_ref),
        )
    ):
        loads.append(pltpu.make_async_copy(source, held_at, load_sem.at[index]))
        loads[-1].start()
    scale_ref, bias_ref, gain_ref, shift_ref = (vectors.at[pl.ds(i, 1)] for i in range(4))
    lax.fori_loop(1, 16, greet_line, 0)
    lax.fori_loop(1, 16, greet_other, 0)
    lax.fori_loop(1, 32, greet_plane, 0)

    def slice_rows(where):
        return pl.ds(pl.multiple_of((where // 2) * 16, 16), 16)

    def slice_lanes(where):
        return pl.ds(pl.multiple_of(lax.rem(where, 2) * 896, 128), 896)

    loads[0].wait()

    @pl.when(core == 0)
    def _():
        main[z, slice_rows(chip), slice_lanes(chip)] = w_ref[slice_rows(chip), slice_lanes(chip)]

    def rest_rows(plane):
        return pl.ds(pl.multiple_of(plane * REST_PAD, 16), REST_PAD)

    rest[rest_rows(z), :] = jnp.concatenate(
        [w_ref[pl.ds(MAIN, SHARD - MAIN), :], jnp.zeros((REST_PAD - SHARD + MAIN, D), jnp.bfloat16)],
        axis=0,
    )
    pl.semaphore_wait(barrier, 61)

    def z_copy(step):
        to = lax.rem(z + step, 16)
        return remote(
            w_ref.at[slice_rows(chip), slice_lanes(chip)],
            main.at[z, slice_rows(chip), slice_lanes(chip)],
            z_send.at[step],
            z_recv.at[z],
            (to, b),
        )

    def z_mine(step):
        return lax.rem(lax.rem(z + step, 16) // 4 + quad, 2) == core

    steps = (1, 15, 2, 14, 3, 13, 4, 12, 5, 11, 6, 10, 7, 9, 8)

    def z_early(step):
        to = lax.rem(z + step, 16)
        base = (to // 4) * (1 - core) + core * (to // 4 + 3 + 2 * (lax.rem(to, 4) // 2))
        return lax.rem(base, 4) == quad

    for step in steps:

        @pl.when(z_mine(step) & z_early(step))
        def _():
            z_copy(step).start()

    def half_lanes(which, part):
        start, count = ((0, 512), (512, 384))[part]
        return pl.ds(pl.multiple_of(which * 896 + start, 128), count)

    def ring_copy(way, step, part):
        sign = 1 if way == 0 else -1
        origin = lax.rem(z - sign * (step - 1) + 16, 16)
        to = lax.rem(z + sign + 16, 16)
        block = rest.at[rest_rows(origin), half_lanes(core, part)]
        return remote(
            block, block, ring_send.at[way, step, part], ring_recv.at[way, step, part], (to, b)
        )

    def ring_wait(way, step, part):
        sign = 1 if way == 0 else -1
        origin = lax.rem(z - sign * step + 16, 16)
        block = rest.at[rest_rows(origin), half_lanes(core, part)]
        remote(
            block,
            block,
            ring_send.at[way, step, part],
            ring_recv.at[way, step, part],
            (lax.rem(z + 1, 16), b),
        ).wait_recv()

    def hand_copy(which, way, step):
        sign = 1 if way == 0 else -1
        origin = lax.rem(z - sign * step + 16, 16)
        block = rest.at[
            rest_rows(origin), pl.ds(pl.multiple_of(which * 896, 128), 896)
        ]
        return remote(
            block, block, hand_send.at[way, step], hand_recv.at[way, step], (z, sibling)
        )

    last = (8, 7)
    for way in range(2):
        ring_copy(way, 1, 0).start()

    def ring_step(part, step):
        for way in range(2):
            if step <= last[way]:
                ring_wait(way, step, part)
                if step < last[way]:
                    ring_copy(way, step + 1, part).start()
        if part == 1:
            for way in range(2):
                if step <= last[way]:
                    hand_copy(core, way, step).start()

    length_row = length_ref[...].astype(jnp.float32)
    source_row = source_ref[...].astype(jnp.float32)
    target_row = target_ref[...].astype(jnp.float32)
    entries = length_row.shape[1]

    def turned(row):
        return jnp.broadcast_to(row, (entries, entries)).T

    length_col, source_col, target_col = turned(length_row), turned(source_row), turned(target_row)
    down = lax.broadcasted_iota(jnp.int32, (entries, entries), 0)
    along = lax.broadcasted_iota(jnp.int32, (entries, entries), 1)
    member = b.astype(jnp.float32)

    def above(owner_col, owner_row, amount_col):
        match = (down < along) & (owner_col == owner_row)
        return jnp.sum(jnp.where(match, amount_col, 0.0), axis=0, keepdims=True)

    target_start = above(target_col, target_row, length_col)
    source_start = above(source_col, source_row, length_col)
    moving_col = jnp.where(target_col != source_col, length_col, 0.0)
    outbox_start = above(source_col, source_row, moving_col)
    before = (along < down) & (target_col == target_row)
    target_start_col = jnp.sum(jnp.where(before, length_row, 0.0), axis=1, keepdims=True)

    slots = lax.broadcasted_iota(jnp.int32, (MOVE_ROWS, entries), 0).astype(jnp.float32)
    leaving = (
        (source_row == member)
        & (target_row != source_row)
        & (slots >= outbox_start)
        & (slots < outbox_start + length_row)
    )
    leaving_row = jnp.sum(
        jnp.where(leaving, source_start - outbox_start + slots, 0.0), axis=1, keepdims=True
    )
    leaving_any = jnp.sum(jnp.where(leaving, 1.0, 0.0), axis=1, keepdims=True)
    leaving_row = jnp.where(leaving_any > 0.0, leaving_row, -1.0)
    count_in = pixels_ref.shape[0]
    whole_col = [turned(ref[...]) for ref in (length_ref, source_ref, target_ref)]
    senders = jnp.where(
        (whole_col[2] == along) & (whole_col[2] != whole_col[1]) & (whole_col[0] > 0), whole_col[1], 0
    )
    sender_vector[...] = jnp.sum(senders, axis=0, keepdims=True)
    load_sender = pltpu.make_async_copy(sender_vector, sender_ref, load_sem.at[8])
    load_sender.start()
    loads[1].wait()
    rows_in[:, pl.ds(512, 128)] = jnp.zeros((rows_in.shape[0], 128), jnp.bfloat16)
    rows_in[pl.ds(0, count_in), pl.ds(0, PIX)] = pixels_ref[...]
    picks = lax.broadcasted_iota(jnp.int32, (MOVE_ROWS, count_in), 1).astype(jnp.float32)
    outgoing = jnp.dot(
        jnp.where(leaving_row == picks, 1.0, 0.0).astype(jnp.bfloat16),
        rows_in[pl.ds(0, count_in), :],
        preferred_element_type=jnp.float32,
    ).astype(jnp.bfloat16)
    for i in range(4):
        for j in range(5):
            pieces[5 * i + j] = outgoing[32 * i : 32 * i + 32, 128 * j : 128 * j + 128]

    def out_copy(target, slot):
        return remote(
            pieces.at[target], inbox.at[slot], out_send.at[target], out_recv.at[slot], (z, target)
        )

    def back_copy(target, slot):
        return remote(
            stage.at[target], arrived.at[slot], back_send.at[target], back_recv.at[slot], (z, target)
        )

    def send_out(step, carry):
        target = lax.rem(b + step, 32)

        @pl.when(target < PIECES)
        def _():
            out_copy(target, b).start()

        return carry

    lax.fori_loop(1, 32, send_out, 0)

    for step in steps:

        @pl.when(z_mine(step) & jnp.logical_not(z_early(step)))
        def _():
            z_copy(step).start()

    def quad_of(which, chunk):
        base = quad * (1 - which) + which * (quad + 3 + 2 * (lax.rem(z, 4) // 2))
        return lax.rem(base + 2 * chunk, 4)

    def chip_at(which, chunk, first, second):
        swap = lax.rem(which + chunk, 2)
        dx = first * (1 - swap) + second * swap
        dy = first * swap + second * (1 - swap)
        return lax.rem(y + dy + 4, 4) * 4 + lax.rem(x + dx + 4, 4)

    def piece(which, chunk, where, low=0, count=4):
        return main.at[
            pl.ds(4 * quad_of(which, chunk) + low, count), slice_rows(where), slice_lanes(where)
        ]

    offsets = (0, -1, 1, 2)
    spans = ((0, 4), (0, 4), (0, 2), (2, 2))

    def hop(chunk, index, axis, place_index, kind):
        low, count = spans[kind]
        sign = 1 if kind in (0, 2) else -1
        origin = (0, 0, -1, 1)[kind]
        a = offsets[place_index]
        if axis == 0:
            to, sent = chip_at(core, chunk, sign, 0), chip_at(core, chunk, origin, 0)
        else:
            to, sent = chip_at(core, chunk, 0, sign), chip_at(core, chunk, a, origin)
        rows = piece(core, chunk, sent, low, count)
        return remote(
            rows, rows, plane_send.at[chunk, index], plane_recv.at[chunk, index], (z, to * 2 + core)
        )

    def hop_wait(chunk, index, axis, place_index, kind):
        low, count = spans[kind]
        origin = (-1, 1, 2, 2)[kind]
        a = offsets[place_index]
        if axis == 0:
            sent = chip_at(core, chunk, origin, 0)
        else:
            sent = chip_at(core, chunk, a, origin)
        rows = piece(core, chunk, sent, low, count)
        remote(
            rows, rows, plane_send.at[chunk, index], plane_recv.at[chunk, index], (z, sibling)
        ).wait_recv()

    def first_copy(chunk, kind):
        return hop(chunk, kind, 0, 0, kind)

    def first_wait(chunk, kind):
        hop_wait(chunk, kind, 0, 0, kind)

    def second_copy(chunk, place_index, kind):
        return hop(chunk, 4 + 4 * place_index + kind, 1, place_index, kind)

    def second_wait(chunk, place_index, kind):
        hop_wait(chunk, 4 + 4 * place_index + kind, 1, place_index, kind)

    def pair_copy(which, chunk, place_index, second_index):
        rows = piece(
            which, chunk, chip_at(which, chunk, offsets[place_index], offsets[second_index])
        )
        index = place_index * 4 + second_index
        return remote(
            rows, rows, pair_send.at[chunk, index], pair_recv.at[chunk, index], (z, sibling)
        )

    def chunk_start(chunk):
        for j in range(4):
            origin = 4 * quad_of(core, chunk) + j

            @pl.when(origin != z)
            def _():
                rows = main.at[origin, slice_rows(chip), slice_lanes(chip)]
                remote(rows, rows, z_send.at[0], z_recv.at[origin], (z, sibling)).wait_recv()

        first_copy(chunk, 0).start()
        first_copy(chunk, 1).start()
        second_copy(chunk, 0, 0).start()
        second_copy(chunk, 0, 1).start()
        pair_copy(core, chunk, 0, 0).start()

    def chunk_first(chunk):
        for kind, index in ((0, 1), (1, 2)):
            first_wait(chunk, kind)
            first_copy(chunk, kind + 2).start()
            second_copy(chunk, index, 0).start()
            second_copy(chunk, index, 1).start()
            pair_copy(core, chunk, index, 0).start()

    def chunk_far(chunk):
        first_wait(chunk, 2)
        first_wait(chunk, 3)
        second_copy(chunk, 3, 0).start()
        second_copy(chunk, 3, 1).start()
        pair_copy(core, chunk, 3, 0).start()

    def chunk_second(chunk, index):
        for kind in (0, 1):
            second_wait(chunk, index, kind)
            second_copy(chunk, index, kind + 2).start()
            pair_copy(core, chunk, index, kind + 1).start()

    def chunk_last(chunk, index):
        second_wait(chunk, index, 2)
        second_wait(chunk, index, 3)
        pair_copy(core, chunk, index, 3).start()

    def quantize_part(part, carry):
        lanes = pl.ds(pl.multiple_of(part * 256, 128), 256)
        scale = scale_ref[:, lanes]
        level = jnp.floor(latent_ref[:, lanes].astype(jnp.float32) / scale + 0.5)
        quant[pl.ds(0, PIX), lanes] = (jnp.clip(level, -8.0, 7.0) * scale).astype(jnp.bfloat16)
        return carry

    def embed_part(part, carry):
        lanes = pl.ds(pl.multiple_of(part * 256, 128), 256)
        total = jnp.dot(moved_ref[...], quant[:, lanes], preferred_element_type=jnp.float32)
        embedded_ref[:, lanes] = (total + bias_ref[:, lanes]).astype(jnp.bfloat16)
        return carry

    def norm_part(part, carry):
        rows = pl.ds(pl.multiple_of(part * 32, 32), 32)
        values = embedded_ref[rows, :].astype(jnp.float32)
        centered = values - jnp.mean(values, axis=1, keepdims=True)
        variance = jnp.mean(centered * centered, axis=1, keepdims=True)
        hat = centered * lax.rsqrt(variance + EPSILON)
        normed[rows, :] = (hat * gain_ref[...] + shift_ref[...]).astype(jnp.bfloat16)
        return carry

    chunk_start(0)
    for way in range(2):
        ring_copy(way, 1, 1).start()
    ring_step(0, 1)
    load_sender.wait()

    @pl.when(b < PIECES)
    def _():
        inbox[b] = pieces[b]

        def take(step, carry):
            out_copy(b, lax.rem(b + step, 32)).wait_recv()
            return carry

        lax.fori_loop(1, 32, take, 0)
        arrived[b] = inbox[jnp.clip(sender_ref[0, b], 0, 31)]

        def send_back(step, carry):
            target = lax.rem(b + step, 32)
            stage[target] = inbox[jnp.clip(sender_ref[0, target], 0, 31)]
            back_copy(target, b).start()
            return carry

        lax.fori_loop(1, 32, send_back, 0)

    chunk_first(0)
    ring_step(1, 1)
    ring_step(0, 2)
    quant[pl.ds(576, 64), :] = jnp.zeros((64, D), jnp.bfloat16)
    for index in range(2, 7):
        loads[index].wait()
    lax.fori_loop(0, 7, quantize_part, 0)
    share = D // 32
    window = jnp.minimum(chip * CHIP_ROWS // 128 * 128, D - 256)
    lanes = pl.ds(pl.multiple_of(window, 128), 256)
    ratio = latent_ref[:, lanes].astype(jnp.float32) / scale_ref[:, lanes]
    level = jnp.floor(ratio + 0.5)
    inside = (level >= -8.0) & (level <= 7.0)
    slope[...] = jnp.where(inside, level - ratio, jnp.clip(level, -8.0, 7.0)).T
    within[...] = jnp.where(inside, 1.0, 0.0).T
    share_rows = pl.ds(pl.multiple_of(chip * CHIP_ROWS - window + core * share, 8), share)
    chunk_far(0)
    chunk_second(0, 0)
    ring_step(1, 2)
    ring_step(0, 3)

    row = lax.broadcasted_iota(jnp.int32, (moved_ref.shape[0], entries), 0).astype(jnp.float32)
    covers = (target_row == member) & (row >= target_start) & (row < target_start + length_row)
    take_from = (
        jnp.where(source_row == member, source_start, outbox_start + float(count_in)) - target_start
    )
    wanted = jnp.sum(jnp.where(covers, take_from + row, 0.0), axis=1, keepdims=True)
    entry = (lax.broadcasted_iota(jnp.int32, (1, entries), 1) + 1).astype(jnp.float32)
    image = jnp.sum(jnp.where(covers, entry, 0.0), axis=1, keepdims=True)
    wanted = jnp.where(image > 0.0, wanted, -1.0)
    column_id_ref[...] = image
    row_lane = lax.broadcasted_iota(jnp.int32, (entries, moved_ref.shape[0]), 1).astype(jnp.float32)
    covers_turned = (
        (target_col[:, :1] == member)
        & (row_lane >= target_start_col)
        & (row_lane < target_start_col + length_col[:, :1])
    )
    entry_down = (lax.broadcasted_iota(jnp.int32, (entries, 1), 0) + 1).astype(jnp.float32)
    row_id_ref[...] = jnp.sum(jnp.where(covers_turned, entry_down, 0.0), axis=0, keepdims=True)

    def arrive(step, carry):
        slot = lax.rem(b + step, 32)

        @pl.when(slot < PIECES)
        def _():
            back_copy(b, slot).wait_recv()

        return carry

    lax.fori_loop(1, 32, arrive, 0)
    for i in range(4):
        for j in range(5):
            rows_in[pl.ds(count_in + 32 * i, 32), pl.ds(128 * j, 128)] = arrived[5 * i + j]
    choose = lax.broadcasted_iota(
        jnp.int32, (moved_ref.shape[0], count_in + MOVE_ROWS), 1
    ).astype(jnp.float32)
    moved_ref[...] = jnp.dot(
        jnp.where(wanted == choose, 1.0, 0.0).astype(jnp.bfloat16),
        rows_in[...],
        preferred_element_type=jnp.float32,
    ).astype(jnp.bfloat16)
    chunk_second(0, 1)
    chunk_start(1)
    ring_step(1, 3)
    ring_step(0, 4)
    lax.fori_loop(0, 4, embed_part, 0)
    chunk_second(0, 2)
    chunk_first(1)
    ring_step(1, 4)
    ring_step(0, 5)
    lax.fori_loop(4, 7, embed_part, 0)
    chunk_second(0, 3)
    chunk_far(1)
    chunk_second(1, 0)
    ring_step(1, 5)
    ring_step(0, 6)
    lax.fori_loop(0, 4, norm_part, 0)
    chunk_second(1, 1)
    for index in range(4):
        chunk_last(0, index)
    ring_step(1, 6)
    ring_step(0, 7)
    lax.fori_loop(4, 8, norm_part, 0)
    chunk_second(1, 2)
    ring_step(1, 7)
    ring_step(0, 8)
    chunk_second(1, 3)
    ring_step(1, 8)
    for index in range(4):
        chunk_last(1, index)

    def project(which, chunk):
        q = quad_of(which, chunk)
        for pair in range(2):
            block = main[pl.ds(4 * q + 2 * pair, 2)].reshape(256, D)
            part_main[4 * q // 2 + pair] = lax.dot_general(
                normed[...], block, (((1,), (1,)), ((), ())), preferred_element_type=jnp.float32
            ).astype(jnp.bfloat16)

    def pair_wait(chunk):
        for index in range(4):
            for second in range(4):
                pair_copy(1 - core, chunk, index, second).wait_recv()

    project(core, 0)
    pair_wait(0)
    project(1 - core, 0)
    project(core, 1)
    pair_wait(1)
    project(1 - core, 1)
    for way in range(2):
        for step in range(1, last[way] + 1):
            hand_copy(1 - core, way, step).wait_recv()
    for part in range(3):
        part_rest[:, 256 * part : 256 * part + 256] = lax.dot_general(
            normed[...],
            rest[pl.ds(256 * part, 256), :],
            (((1,), (1,)), ((), ())),
            preferred_element_type=jnp.float32,
        ).astype(jnp.bfloat16)
    joined = []
    for plane in range(16):
        joined.append(part_main[plane // 2, :, 128 * (plane % 2) : 128 * (plane % 2) + 128])
        joined.append(part_rest[:, REST_PAD * plane : REST_PAD * plane + SHARD - MAIN])
    projected_ref[...] = jnp.concatenate(joined, axis=1)

    loads[7].wait()
    width = HEADS * HEAD
    score_scale = HEAD ** (-0.5)
    grad_factor = 1.0 / math.sqrt(131072.0)
    column_id = column_id_ref[...]
    row_id = row_id_ref[...]
    active = column_id > 0.0
    same = (column_id == row_id) & active
    grad_out[...] = jnp.where(
        active, cotangent_ref[...].astype(jnp.float32) * grad_factor, 0.0
    ).astype(jnp.bfloat16)
    attended[...] = jnp.zeros_like(attended)
    grad_projected[...] = jnp.zeros_like(grad_projected)
    by_rows = (((1,), (1,)), ((), ()))
    by_columns = (((0,), (0,)), ((), ()))

    def dot(left, right, contract=(((1,), (0,)), ((), ()))):
        return lax.dot_general(left, right, contract, preferred_element_type=jnp.float32)

    for head in range(HEADS):
        start = HEAD * head // 128 * 128
        stop = -(-(HEAD * head + HEAD) // 128) * 128
        span = stop - start
        lane = lax.broadcasted_iota(jnp.int32, (1, span), 1) + start
        own = (lane >= HEAD * head) & (lane < HEAD * head + HEAD)

        def window(ref, base=0):
            return ref[:, base + start : base + stop]

        def masked(value):
            return jnp.where(own, value, jnp.zeros_like(value))

        queries, keys, values = (window(projected_ref, width * i) for i in range(3))
        out = window(grad_out)
        keys, values = masked(keys), masked(values)
        scores = dot(queries, keys, by_rows) * score_scale
        exponent = jnp.where(same, jnp.exp(scores), 0.0)
        denominator = jnp.sum(exponent, axis=1, keepdims=True)
        attention = exponent / jnp.where(active, denominator, 1.0)
        soft = attention.astype(jnp.bfloat16)
        attended[:, start:stop] += dot(soft, values)
        grad_attention = dot(out, values, by_rows)
        inner = jnp.sum(attention * grad_attention, axis=1, keepdims=True)
        grad_score = (attention * (grad_attention - inner) * score_scale).astype(jnp.bfloat16)
        grad_projected[:, start:stop] += dot(grad_score, keys)
        grad_projected[:, width + start : width + stop] += dot(
            grad_score, masked(queries), by_columns
        )
        grad_projected[:, 2 * width + start : 2 * width + stop] += dot(
            soft, masked(out), by_columns
        )
    attended_ref[...] = attended[...].astype(jnp.bfloat16)
    rounded = grad_projected[...].astype(jnp.bfloat16)
    pad = jnp.zeros((rounded.shape[0], REST_PAD - SHARD + MAIN), jnp.bfloat16)
    mains, rests = [], []
    for plane in range(16):
        base = SHARD * plane
        mains.append(rounded[:, base : base + MAIN])
        rests.append(rounded[:, base + MAIN : base + SHARD])
        rests.append(pad)
    grad_main[...] = jnp.concatenate(mains, axis=1)
    grad_rest[...] = jnp.concatenate(rests, axis=1)

    def back_part(part, carry):
        lanes = pl.ds(pl.multiple_of(part * 256, 128), 256)
        grad_normed[:, lanes] = dot(
            grad_main[...], main[:, :, lanes].reshape(16 * MAIN, 256)
        ) + dot(grad_rest[...], rest[:, lanes])
        return carry

    lax.fori_loop(0, 7, back_part, 0)

    def back_norm_part(part, carry):
        rows = pl.ds(pl.multiple_of(part * 32, 32), 32)
        values = embedded_ref[rows, :].astype(jnp.float32)
        centered = values - jnp.mean(values, axis=1, keepdims=True)
        variance = jnp.mean(centered * centered, axis=1, keepdims=True)
        inverse = lax.rsqrt(variance + EPSILON)
        hat = centered * inverse
        gained = grad_normed[rows, :] * gain_ref[...]
        result = inverse * (
            gained
            - jnp.mean(gained, axis=1, keepdims=True)
            - hat * jnp.mean(gained * hat, axis=1, keepdims=True)
        )
        grad_embedded[rows, :] = jnp.where(column_id_ref[rows, :] > 0.0, result, 0.0).astype(
            jnp.bfloat16
        )
        return carry

    lax.fori_loop(0, 8, back_norm_part, 0)
    for part in range(2):
        block = dot(grad_embedded[:, 896 * part : 896 * part + 896], moved_ref[...], by_columns)
        grad_ref[8 * part : 8 * part + 8] = block.astype(jnp.bfloat16).reshape(
            8, CHIP_ROWS, PIX_PAD
        )
    first = x * (1 - core) + y * core
    second = y * (1 - core) + x * core
    parts = ((0, 256), (256, 256), (512, 128))

    def chip_of(which, f, s):
        return (s * 4 + f) * (1 - which) + (f * 4 + s) * which

    def target_chip(which, a, half):
        mine = x * (1 - which) + y * which
        f = lax.rem(mine + a, 4)
        return chip_of(which, f, 2 * half + lax.rem(f + which, 2))

    def at(f, s):
        return (z, chip_of(core, f, s) * 2 + core)

    def columns(k):
        return pl.ds(*parts[k])

    def wide(value):
        return value.astype(jnp.float32)

    def twin_copy(a, half, k):
        return remote(
            grad_ref.at[target_chip(1 - core, a, half), :, columns(k)],
            twin.at[a, half, :, columns(k)],
            twin_send.at[a, half, k],
            twin_recv.at[a, half, k],
            (z, sibling),
        )

    def across_copy(a, k):
        return remote(
            held.at[a, :, :, columns(k)],
            across.at[a, :, :, columns(k)],
            across_send.at[a, k],
            across_recv.at[a, k],
            at(lax.rem(first + a, 4), second),
        )

    order = (2, 1, 3, 0)
    spread = range(len(parts))
    for k in spread:
        for a in order:
            for half in range(2):
                twin_copy(a, half, k).start()
    for k in spread:
        for a in order:
            for half in range(2):
                twin_copy(a, half, k).wait_recv()
                chip_here = target_chip(core, a, half)
                held[a, half, :, columns(k)] = (
                    wide(grad_ref[chip_here, :, columns(k)]) + wide(twin[a, half, :, columns(k)])
                ).astype(jnp.bfloat16)
            if a > 0 and k == 0:
                across_copy(a, k).start()

    parity = lax.rem(first + core, 2)
    owner = lax.rem(first + second, 2) == core

    def line_copy(half, k):
        to = 2 * half + parity
        away = lax.rem(to - second + 4, 4)
        return remote(
            line.at[half, :, columns(k)],
            met.at[away, :, columns(k)],
            line_send.at[half, k],
            line_recv.at[away, k],
            at(first, to),
        )

    for k in spread:
        for a in (2, 1, 3):
            across_copy(a, k).wait_send()
            if k + 1 < len(parts):
                across_copy(a, k + 1).start()
        for a in (1, 3, 2):
            across_copy(a, k).wait_recv()
        for half in range(2):
            line[half, :, columns(k)] = (
                wide(held[0, half, :, columns(k)])
                + wide(across[1, half, :, columns(k)])
                + wide(across[2, half, :, columns(k)])
                + wide(across[3, half, :, columns(k)])
            ).astype(jnp.bfloat16)

            @pl.when(2 * half + parity != second)
            def _():
                line_copy(half, k).start()

    def tile_copy(index, k):
        return remote(
            summed.at[pl.ds(16 * index, 16), columns(k)],
            tiles.at[z, :, columns(k)],
            tile_send.at[index, k],
            tile_recv.at[z, k],
            (2 * index, b),
        )

    for k in spread:

        @pl.when(owner)
        def _():
            mine = wide(line[second // 2, :, columns(k)])
            for away in (1, 3, 2):
                remote(
                    line.at[0, :, columns(k)],
                    met.at[away, :, columns(k)],
                    line_send.at[0, k],
                    line_recv.at[away, k],
                    (z, sibling),
                ).wait_recv()
                mine = mine + wide(met[away, :, columns(k)])
            summed[:, columns(k)] = mine.astype(jnp.bfloat16)
            for index in range(7):

                @pl.when(z != 2 * index)
                def _():
                    tile_copy(index, k).start()

    collector = owner & (z < 14) & (lax.rem(z, 2) == 0)
    tile_index = jnp.minimum(z // 2, 6)

    def total_copy(step, which, k):
        return remote(
            total.at[tile_index, :, columns(k)],
            total.at[tile_index, :, columns(k)],
            total_send.at[step, which, k],
            total_recv.at[tile_index, k],
            (lax.rem(z + step, 16), chip * 2 + which),
        )

    def total_goes(step, which):
        wanted_there = (tile_index <= 3) if which == 0 else (tile_index >= 3)
        return wanted_there & ((step != 0) | (core != which))

    for k in spread:

        @pl.when(collector)
        def _():
            tile_rows = pl.ds(pl.multiple_of(16 * tile_index, 16), 16)
            tiles[z, :, columns(k)] = summed[tile_rows, columns(k)]

            def take(step, carry):
                slot = lax.rem(z + step, 16)
                remote(
                    summed.at[pl.ds(0, 16), columns(k)],
                    tiles.at[slot, :, columns(k)],
                    tile_send.at[0, k],
                    tile_recv.at[slot, k],
                    (slot, b),
                ).wait_recv()
                return carry

            lax.fori_loop(1, 16, take, 0)
            value = wide(tiles[0, :, columns(k)])
            for slot in range(1, 16):
                value = value + wide(tiles[slot, :, columns(k)])
            total[tile_index, :, columns(k)] = value.astype(jnp.bfloat16)

            def give(step, carry):
                for which in range(2):

                    @pl.when(total_goes(step, which))
                    def _():
                        total_copy(step, which, k).start()

                return carry

            lax.fori_loop(0, 16, give, 0)

    for k in spread:
        for j in range(4):
            index = 3 * core + j

            @pl.when(jnp.logical_not(owner & (z == 2 * index)))
            def _():
                remote(
                    total.at[index, :, columns(k)],
                    total.at[index, :, columns(k)],
                    total_send.at[0, 0, k],
                    total_recv.at[index, k],
                    (z, sibling),
                ).wait_recv()

    final[...] = wide(total[pl.ds(3 * core, 4)]).reshape(64, PIX_PAD)
    mine = final[pl.ds(pl.multiple_of(core * 8, 8), share), pl.ds(0, PIX)]
    latent_out[...] = jnp.where(within[share_rows, :] > 0.0, mine, 0.0)
    scale_out[...] = (1.0 / math.sqrt(PIX * 7.0)) * jnp.sum(mine * slope[share_rows, :], axis=1)

    for k in spread:
        for a in range(4):
            for half in range(2):
                twin_copy(a, half, k).wait_send()
        for half in range(2):

            @pl.when(2 * half + parity != second)
            def _():
                line_copy(half, k).wait_send()

        @pl.when(owner)
        def _():
            for index in range(7):

                @pl.when(z != 2 * index)
                def _():
                    tile_copy(index, k).wait_send()

        @pl.when(collector)
        def _():
            def given(step, carry):
                for which in range(2):

                    @pl.when(total_goes(step, which))
                    def _():
                        total_copy(step, which, k).wait_send()

                return carry

            lax.fori_loop(0, 16, given, 0)

    for step in range(1, 16):

        @pl.when(z_mine(step))
        def _():
            z_copy(step).wait_send()

    for way in range(2):
        for step in range(1, last[way] + 1):
            for part in range(2):
                ring_copy(way, step, part).wait_send()
            hand_copy(core, way, step).wait_send()

    def sent_out(step, carry):
        target = lax.rem(b + step, 32)

        @pl.when(target < PIECES)
        def _():
            out_copy(target, b).wait_send()

        return carry

    lax.fori_loop(1, 32, sent_out, 0)

    @pl.when(b < PIECES)
    def _():
        def sent_back(step, carry):
            back_copy(lax.rem(b + step, 32), b).wait_send()
            return carry

        lax.fori_loop(1, 32, sent_back, 0)

    for chunk in range(2):
        for kind in range(4):
            first_copy(chunk, kind).wait_send()
            for index in range(4):
                second_copy(chunk, index, kind).wait_send()
        for index in range(4):
            for second in range(4):
                pair_copy(core, chunk, index, second).wait_send()


def deliver_kernel(attended, latent, scale, attended_out, latent_out, scale_out):
    attended_out[...] = attended[...]
    latent_out[...] = latent[...]
    scale_out[...] = scale[...]


def deliver(*arrays):
    vmem = pl.BlockSpec(memory_space=pltpu.VMEM)
    return pl.pallas_call(
        deliver_kernel,
        name="deliver",
        out_shape=tuple(jax.ShapeDtypeStruct(a.shape, a.dtype) for a in arrays),
        in_specs=[vmem] * 3,
        out_specs=(vmem,) * 3,
    )(*arrays)


def whole(weight, latent, scale, bias, gain, shift, pixels, cotangent, length, source, target):
    vmem = pl.BlockSpec(memory_space=pltpu.VMEM)
    anywhere = pl.BlockSpec(memory_space=pl.ANY)
    dma = pltpu.SemaphoreType.DMA
    rows = cotangent.shape[0]
    block = (CHIP_ROWS, PIX_PAD)
    shape = jax.ShapeDtypeStruct
    return pl.pallas_call(
        whole_kernel,
        name="whole",
        out_shape=(
            shape((rows, HEADS * HEAD), jnp.bfloat16),
            shape((D // 32, PIX), jnp.float32),
            shape((D // 32,), jnp.float32),
        ),
        in_specs=[anywhere] * 8 + [vmem] * 3,
        out_specs=(vmem, vmem, vmem),
        scratch_shapes=[
            pltpu.VMEM((SHARD, D), jnp.bfloat16),
            pltpu.VMEM((PIX, D), jnp.bfloat16),
            pltpu.VMEM((8, D), jnp.float32),
            pltpu.VMEM(pixels.shape, jnp.bfloat16),
            pltpu.VMEM(cotangent.shape, jnp.bfloat16),
            pltpu.VMEM((1, 128), jnp.int32),
            pltpu.SMEM((1, 128), jnp.int32),
            pltpu.VMEM((256, PIX), jnp.float32),
            pltpu.VMEM((256, PIX), jnp.float32),
            pltpu.VMEM((rows, PIX_PAD), jnp.bfloat16),
            pltpu.VMEM((rows, D), jnp.bfloat16),
            pltpu.VMEM((rows, 16 * SHARD), jnp.bfloat16),
            pltpu.VMEM((rows, 1), jnp.float32),
            pltpu.VMEM((1, rows), jnp.float32),
            pltpu.VMEM((16, MAIN, D), jnp.bfloat16),
            pltpu.VMEM((16 * REST_PAD, D), jnp.bfloat16),
            pltpu.VMEM((pixels.shape[0] + MOVE_ROWS, PIX_PAD), jnp.bfloat16),
            pltpu.VMEM((PIECES, 32, 128), jnp.bfloat16),
            pltpu.VMEM((32, 32, 128), jnp.bfloat16),
            pltpu.VMEM((32, 32, 128), jnp.bfloat16),
            pltpu.VMEM((PIECES, 32, 128), jnp.bfloat16),
            pltpu.VMEM((PIX_PAD, D), jnp.bfloat16),
            pltpu.VMEM((rows, D), jnp.bfloat16),
            pltpu.VMEM((8, rows, 256), jnp.bfloat16),
            pltpu.VMEM((rows, 16 * REST_PAD), jnp.bfloat16),
            pltpu.VMEM((rows, HEADS * HEAD), jnp.bfloat16),
            pltpu.VMEM((rows, HEADS * HEAD), jnp.float32),
            pltpu.VMEM((rows, 16 * SHARD), jnp.float32),
            pltpu.VMEM((rows, 16 * MAIN), jnp.bfloat16),
            pltpu.VMEM((rows, 16 * REST_PAD), jnp.bfloat16),
            pltpu.VMEM((rows, D), jnp.float32),
            pltpu.VMEM((rows, D), jnp.bfloat16),
            pltpu.VMEM((D // CHIP_ROWS,) + block, jnp.bfloat16),
            pltpu.VMEM((4, 2) + block, jnp.bfloat16),
            pltpu.VMEM((4, 2) + block, jnp.bfloat16),
            pltpu.VMEM((4, 2) + block, jnp.bfloat16),
            pltpu.VMEM((2,) + block, jnp.bfloat16),
            pltpu.VMEM((4,) + block, jnp.bfloat16),
            pltpu.VMEM((16, 16, PIX_PAD), jnp.bfloat16),
            pltpu.VMEM((7, 16, PIX_PAD), jnp.bfloat16),
            pltpu.VMEM(block, jnp.bfloat16),
            pltpu.VMEM((64, PIX_PAD), jnp.float32),
            dma((9,)),
            dma((16,)),
            dma((16,)),
            dma((2, 9, 2)),
            dma((2, 9, 2)),
            dma((2, 9)),
            dma((2, 9)),
            dma((32,)),
            dma((32,)),
            dma((32,)),
            dma((32,)),
            dma((2, 20)),
            dma((2, 20)),
            dma((2, 16)),
            dma((2, 16)),
            dma((4, 2, 3)),
            dma((4, 2, 3)),
            dma((4, 3)),
            dma((4, 3)),
            dma((2, 3)),
            dma((4, 3)),
            dma((7, 3)),
            dma((16, 3)),
            dma((16, 2, 3)),
            dma((7, 3)),
        ],
        compiler_params=pltpu.CompilerParams(
            collective_id=0, has_side_effects=True, vmem_limit_bytes=58 * 1024 * 1024
        ),
    )(weight, latent, scale, bias, gain, shift, pixels, cotangent, length, source, target)


def per_device(
    pixels,
    latent,
    quant_scale,
    embed_bias,
    ln_gain,
    ln_bias,
    qkv_weight,
    cotangent,
    image_length,
    image_source,
    image_target,
):
    results = whole(
        qkv_weight.T,
        latent.T,
        quant_scale,
        embed_bias,
        ln_gain,
        ln_bias,
        pixels,
        cotangent,
        image_length,
        image_source,
        image_target,
    )
    return deliver(*results)


def solution(mesh):
    placed = (
        P(("dp", "bal"), None),
        P(),
        P(),
        P(),
        P(),
        P(),
        P(None, "dp"),
        P(("dp", "bal"), None),
        P("dp", None),
        P("dp", None),
        P("dp", None),
    )
    return jax.shard_map(
        per_device,
        mesh=mesh,
        in_specs=placed,
        out_specs=(P(("dp", "bal"), None), P("bal", None), P("bal")),
        check_vma=False,
    )
```

```python
import math

import jax
import jax.numpy as jnp
from jax import lax
from jax.experimental import pallas as pl
from jax.experimental.pallas import tpu as pltpu
from jax.sharding import PartitionSpec as P

D = 1792
HEAD = 112
PIX = 588
HEADS = 8
MOVE_ROWS = 128
EPSILON = 1e-06
MESH = pl.DeviceIdType.MESH
SHARD = 168
MAIN = 128
REST_PAD = 48
CHIP_ROWS = 112
PIX_PAD = 640
PIECES = 20


def place():
    z = lax.axis_index("dp")
    b = lax.axis_index("bal")
    core = lax.rem(b, 2)
    x = lax.rem(b // 2, 4)
    y = b // 8
    return z, b, x, y, core


def remote(src, dst, send, recv, device):
    copy = pltpu.make_async_remote_copy(
        src_ref=src, dst_ref=dst, send_sem=send, recv_sem=recv, device_id=device, device_id_type=MESH
    )
    return copy


def whole_kernel(
    weight_in,
    latent_in,
    scale_in,
    bias_in,
    gain_in,
    shift_in,
    pixels_in,
    cotangent_in,
    length_ref,
    source_ref,
    target_ref,
    attended_ref,
    latent_out,
    scale_out,
    w_ref,
    latent_ref,
    vectors,
    pixels_ref,
    cotangent_ref,
    sender_vector,
    sender_ref,
    slope,
    within,
    moved_ref,
    embedded_ref,
    projected_ref,
    column_id_ref,
    row_id_ref,
    main,
    rest,
    rows_in,
    pieces,
    inbox,
    stage,
    arrived,
    quant,
    normed,
    part_main,
    part_rest,
    grad_out,
    attended,
    grad_projected,
    grad_main,
    grad_rest,
    grad_normed,
    grad_embedded,
    grad_ref,
    twin,
    held,
    across,
    line,
    met,
    tiles,
    total,
    summed,
    final,
    load_sem,
    z_send,
    z_recv,
    ring_send,
    ring_recv,
    hand_send,
    hand_recv,
    out_send,
    out_recv,
    back_send,
    back_recv,
    plane_send,
    plane_recv,
    pair_send,
    pair_recv,
    twin_send,
    twin_recv,
    across_send,
    across_recv,
    line_send,
    line_recv,
    tile_send,
    tile_recv,
    total_send,
    total_recv,
):
    z, b, x, y, core = place()
    sibling = b + 1 - 2 * core
    chip = b // 2
    quad = z // 4
    barrier = pltpu.get_barrier_semaphore()

    def greet_plane(step, carry):
        pl.semaphore_signal(
            barrier, inc=1, device_id=(z, lax.rem(b + step, 32)), device_id_type=MESH
        )
        return carry

    def greet_line(step, carry):
        pl.semaphore_signal(
            barrier, inc=1, device_id=(lax.rem(z + step, 16), b), device_id_type=MESH
        )
        return carry

    def greet_other(step, carry):
        pl.semaphore_signal(
            barrier, inc=1, device_id=(lax.rem(z + step, 16), sibling), device_id_type=MESH
        )
        return carry

    loads = []
    for index, (source, held_at) in enumerate(
        (
            (weight_in, w_ref),
            (pixels_in, pixels_ref),
            (latent_in, latent_ref),
            (scale_in, vectors.at[0]),
            (bias_in, vectors.at[1]),
            (gain_in, vectors.at[2]),
            (shift_in, vectors.at[3]),
            (cotangent_in, cotangent_ref),
        )
    ):
        loads.append(pltpu.make_async_copy(source, held_at, load_sem.at[index]))
        loads[-1].start()
    scale_ref, bias_ref, gain_ref, shift_ref = (vectors.at[pl.ds(i, 1)] for i in range(4))
    lax.fori_loop(1, 16, greet_line, 0)
    lax.fori_loop(1, 16, greet_other, 0)
    lax.fori_loop(1, 32, greet_plane, 0)

    def slice_rows(where):
        return pl.ds(pl.multiple_of((where // 2) * 16, 16), 16)

    def slice_lanes(where):
        return pl.ds(pl.multiple_of(lax.rem(where, 2) * 896, 128), 896)

    loads[0].wait()

    @pl.when(core == 0)
    def _():
        main[z, slice_rows(chip), slice_lanes(chip)] = w_ref[slice_rows(chip), slice_lanes(chip)]

    def rest_rows(plane):
        return pl.ds(pl.multiple_of(plane * REST_PAD, 16), REST_PAD)

    rest[rest_rows(z), :] = jnp.concatenate(
        [w_ref[pl.ds(MAIN, SHARD - MAIN), :], jnp.zeros((REST_PAD - SHARD + MAIN, D), jnp.bfloat16)],
        axis=0,
    )
    pl.semaphore_wait(barrier, 61)

    def z_copy(step):
        to = lax.rem(z + step, 16)
        return remote(
            w_ref.at[slice_rows(chip), slice_lanes(chip)],
            main.at[z, slice_rows(chip), slice_lanes(chip)],
            z_send.at[step],
            z_recv.at[z],
            (to, b),
        )

    def z_mine(step):
        return lax.rem(lax.rem(z + step, 16) // 4 + quad, 2) == core

    steps = (1, 15, 2, 14, 3, 13, 4, 12, 5, 11, 6, 10, 7, 9, 8)

    def z_early(step):
        to = lax.rem(z + step, 16)
        base = (to // 4) * (1 - core) + core * (to // 4 + 3 + 2 * (lax.rem(to, 4) // 2))
        return lax.rem(base, 4) == quad

    for step in steps:

        @pl.when(z_mine(step) & z_early(step))
        def _():
            z_copy(step).start()

    def half_lanes(which, part):
        start, count = ((0, 512), (512, 384))[part]
        return pl.ds(pl.multiple_of(which * 896 + start, 128), count)

    def ring_copy(way, step, part):
        sign = 1 if way == 0 else -1
        origin = lax.rem(z - sign * (step - 1) + 16, 16)
        to = lax.rem(z + sign + 16, 16)
        block = rest.at[rest_rows(origin), half_lanes(core, part)]
        return remote(
            block, block, ring_send.at[way, step, part], ring_recv.at[way, step, part], (to, b)
        )

    def ring_wait(way, step, part):
        sign = 1 if way == 0 else -1
        origin = lax.rem(z - sign * step + 16, 16)
        block = rest.at[rest_rows(origin), half_lanes(core, part)]
        remote(
            block,
            block,
            ring_send.at[way, step, part],
            ring_recv.at[way, step, part],
            (lax.rem(z + 1, 16), b),
        ).wait_recv()

    def hand_copy(which, way, step):
        sign = 1 if way == 0 else -1
        origin = lax.rem(z - sign * step + 16, 16)
        block = rest.at[
            rest_rows(origin), pl.ds(pl.multiple_of(which * 896, 128), 896)
        ]
        return remote(
            block, block, hand_send.at[way, step], hand_recv.at[way, step], (z, sibling)
        )

    last = (8, 7)
    for way in range(2):
        ring_copy(way, 1, 0).start()

    def ring_step(part, step):
        for way in range(2):
            if step <= last[way]:
                ring_wait(way, step, part)
                if step < last[way]:
                    ring_copy(way, step + 1, part).start()
        if part == 1:
            for way in range(2):
                if step <= last[way]:
                    hand_copy(core, way, step).start()

    length_row = length_ref[...].astype(jnp.float32)
    source_row = source_ref[...].astype(jnp.float32)
    target_row = target_ref[...].astype(jnp.float32)
    entries = length_row.shape[1]

    def turned(row):
        return jnp.broadcast_to(row, (entries, entries)).T

    length_col, source_col, target_col = turned(length_row), turned(source_row), turned(target_row)
    down = lax.broadcasted_iota(jnp.int32, (entries, entries), 0)
    along = lax.broadcasted_iota(jnp.int32, (entries, entries), 1)
    member = b.astype(jnp.float32)

    def above(owner_col, owner_row, amount_col):
        match = (down < along) & (owner_col == owner_row)
        return jnp.sum(jnp.where(match, amount_col, 0.0), axis=0, keepdims=True)

    target_start = above(target_col, target_row, length_col)
    source_start = above(source_col, source_row, length_col)
    moving_col = jnp.where(target_col != source_col, length_col, 0.0)
    outbox_start = above(source_col, source_row, moving_col)
    before = (along < down) & (target_col == target_row)
    target_start_col = jnp.sum(jnp.where(before, length_row, 0.0), axis=1, keepdims=True)

    slots = lax.broadcasted_iota(jnp.int32, (MOVE_ROWS, entries), 0).astype(jnp.float32)
    leaving = (
        (source_row == member)
        & (target_row != source_row)
        & (slots >= outbox_start)
        & (slots < outbox_start + length_row)
    )
    leaving_row = jnp.sum(
        jnp.where(leaving, source_start - outbox_start + slots, 0.0), axis=1, keepdims=True
    )
    leaving_any = jnp.sum(jnp.where(leaving, 1.0, 0.0), axis=1, keepdims=True)
    leaving_row = jnp.where(leaving_any > 0.0, leaving_row, -1.0)
    count_in = pixels_ref.shape[0]
    whole_col = [turned(ref[...]) for ref in (length_ref, source_ref, target_ref)]
    senders = jnp.where(
        (whole_col[2] == along) & (whole_col[2] != whole_col[1]) & (whole_col[0] > 0), whole_col[1], 0
    )
    sender_vector[...] = jnp.sum(senders, axis=0, keepdims=True)
    load_sender = pltpu.make_async_copy(sender_vector, sender_ref, load_sem.at[8])
    load_sender.start()
    loads[1].wait()
    rows_in[:, pl.ds(512, 128)] = jnp.zeros((rows_in.shape[0], 128), jnp.bfloat16)
    rows_in[pl.ds(0, count_in), pl.ds(0, PIX)] = pixels_ref[...]
    picks = lax.broadcasted_iota(jnp.int32, (MOVE_ROWS, count_in), 1).astype(jnp.float32)
    outgoing = jnp.dot(
        jnp.where(leaving_row == picks, 1.0, 0.0).astype(jnp.bfloat16),
        rows_in[pl.ds(0, count_in), :],
        preferred_element_type=jnp.float32,
    ).astype(jnp.bfloat16)
    for i in range(4):
        for j in range(5):
            pieces[5 * i + j] = outgoing[32 * i : 32 * i + 32, 128 * j : 128 * j + 128]

    def out_copy(target, slot):
        return remote(
            pieces.at[target], inbox.at[slot], out_send.at[target], out_recv.at[slot], (z, target)
        )

    def back_copy(target, slot):
        return remote(
            stage.at[target], arrived.at[slot], back_send.at[target], back_recv.at[slot], (z, target)
        )

    def send_out(step, carry):
        target = lax.rem(b + step, 32)

        @pl.when(target < PIECES)
        def _():
            out_copy(target, b).start()

        return carry

    lax.fori_loop(1, 32, send_out, 0)

    for step in steps:

        @pl.when(z_mine(step) & jnp.logical_not(z_early(step)))
        def _():
            z_copy(step).start()

    def quad_of(which, chunk):
        base = quad * (1 - which) + which * (quad + 3 + 2 * (lax.rem(z, 4) // 2))
        return lax.rem(base + 2 * chunk, 4)

    def chip_at(which, chunk, first, second):
        swap = lax.rem(which + chunk, 2)
        dx = first * (1 - swap) + second * swap
        dy = first * swap + second * (1 - swap)
        return lax.rem(y + dy + 4, 4) * 4 + lax.rem(x + dx + 4, 4)

    def piece(which, chunk, where, low=0, count=4):
        return main.at[
            pl.ds(4 * quad_of(which, chunk) + low, count), slice_rows(where), slice_lanes(where)
        ]

    offsets = (0, -1, 1, 2)
    spans = ((0, 4), (0, 4), (0, 2), (2, 2))

    def hop(chunk, index, axis, place_index, kind):
        low, count = spans[kind]
        sign = 1 if kind in (0, 2) else -1
        origin = (0, 0, -1, 1)[kind]
        a = offsets[place_index]
        if axis == 0:
            to, sent = chip_at(core, chunk, sign, 0), chip_at(core, chunk, origin, 0)
        else:
            to, sent = chip_at(core, chunk, 0, sign), chip_at(core, chunk, a, origin)
        rows = piece(core, chunk, sent, low, count)
        return remote(
            rows, rows, plane_send.at[chunk, index], plane_recv.at[chunk, index], (z, to * 2 + core)
        )

    def hop_wait(chunk, index, axis, place_index, kind):
        low, count = spans[kind]
        origin = (-1, 1, 2, 2)[kind]
        a = offsets[place_index]
        if axis == 0:
            sent = chip_at(core, chunk, origin, 0)
        else:
            sent = chip_at(core, chunk, a, origin)
        rows = piece(core, chunk, sent, low, count)
        remote(
            rows, rows, plane_send.at[chunk, index], plane_recv.at[chunk, index], (z, sibling)
        ).wait_recv()

    def first_copy(chunk, kind):
        return hop(chunk, kind, 0, 0, kind)

    def first_wait(chunk, kind):
        hop_wait(chunk, kind, 0, 0, kind)

    def second_copy(chunk, place_index, kind):
        return hop(chunk, 4 + 4 * place_index + kind, 1, place_index, kind)

    def second_wait(chunk, place_index, kind):
        hop_wait(chunk, 4 + 4 * place_index + kind, 1, place_index, kind)

    def pair_copy(which, chunk, place_index, second_index):
        rows = piece(
            which, chunk, chip_at(which, chunk, offsets[place_index], offsets[second_index])
        )
        index = place_index * 4 + second_index
        return remote(
            rows, rows, pair_send.at[chunk, index], pair_recv.at[chunk, index], (z, sibling)
        )

    def chunk_start(chunk):
        for j in range(4):
            origin = 4 * quad_of(core, chunk) + j

            @pl.when(origin != z)
            def _():
                rows = main.at[origin, slice_rows(chip), slice_lanes(chip)]
                remote(rows, rows, z_send.at[0], z_recv.at[origin], (z, sibling)).wait_recv()

        first_copy(chunk, 0).start()
        first_copy(chunk, 1).start()
        second_copy(chunk, 0, 0).start()
        second_copy(chunk, 0, 1).start()
        pair_copy(core, chunk, 0, 0).start()

    def chunk_first(chunk):
        for kind, index in ((0, 1), (1, 2)):
            first_wait(chunk, kind)
            first_copy(chunk, kind + 2).start()
            second_copy(chunk, index, 0).start()
            second_copy(chunk, index, 1).start()
            pair_copy(core, chunk, index, 0).start()

    def chunk_far(chunk):
        first_wait(chunk, 2)
        first_wait(chunk, 3)
        second_copy(chunk, 3, 0).start()
        second_copy(chunk, 3, 1).start()
        pair_copy(core, chunk, 3, 0).start()

    def chunk_second(chunk, index):
        for kind in (0, 1):
            second_wait(chunk, index, kind)
            second_copy(chunk, index, kind + 2).start()
            pair_copy(core, chunk, index, kind + 1).start()

    def chunk_last(chunk, index):
        second_wait(chunk, index, 2)
        second_wait(chunk, index, 3)
        pair_copy(core, chunk, index, 3).start()

    def quantize_part(part, carry):
        lanes = pl.ds(pl.multiple_of(part * 256, 128), 256)
        scale = scale_ref[:, lanes]
        level = jnp.floor(latent_ref[:, lanes].astype(jnp.float32) / scale + 0.5)
        quant[pl.ds(0, PIX), lanes] = (jnp.clip(level, -8.0, 7.0) * scale).astype(jnp.bfloat16)
        return carry

    def embed_part(part, carry):
        lanes = pl.ds(pl.multiple_of(part * 256, 128), 256)
        total = jnp.dot(moved_ref[...], quant[:, lanes], preferred_element_type=jnp.float32)
        embedded_ref[:, lanes] = (total + bias_ref[:, lanes]).astype(jnp.bfloat16)
        return carry

    def norm_part(part, carry):
        rows = pl.ds(pl.multiple_of(part * 32, 32), 32)
        values = embedded_ref[rows, :].astype(jnp.float32)
        centered = values - jnp.mean(values, axis=1, keepdims=True)
        variance = jnp.mean(centered * centered, axis=1, keepdims=True)
        hat = centered * lax.rsqrt(variance + EPSILON)
        normed[rows, :] = (hat * gain_ref[...] + shift_ref[...]).astype(jnp.bfloat16)
        return carry

    chunk_start(0)
    for way in range(2):
        ring_copy(way, 1, 1).start()
    ring_step(0, 1)
    load_sender.wait()

    @pl.when(b < PIECES)
    def _():
        inbox[b] = pieces[b]

        def take(step, carry):
            out_copy(b, lax.rem(b + step, 32)).wait_recv()
            return carry

        lax.fori_loop(1, 32, take, 0)
        arrived[b] = inbox[jnp.clip(sender_ref[0, b], 0, 31)]

        def send_back(step, carry):
            target = lax.rem(b + step, 32)
            stage[target] = inbox[jnp.clip(sender_ref[0, target], 0, 31)]
            back_copy(target, b).start()
            return carry

        lax.fori_loop(1, 32, send_back, 0)

    chunk_first(0)
    ring_step(1, 1)
    ring_step(0, 2)
    quant[pl.ds(576, 64), :] = jnp.zeros((64, D), jnp.bfloat16)
    for index in range(2, 7):
        loads[index].wait()
    lax.fori_loop(0, 7, quantize_part, 0)
    share = D // 32
    window = jnp.minimum(chip * CHIP_ROWS // 128 * 128, D - 256)
    lanes = pl.ds(pl.multiple_of(window, 128), 256)
    ratio = latent_ref[:, lanes].astype(jnp.float32) / scale_ref[:, lanes]
    level = jnp.floor(ratio + 0.5)
    inside = (level >= -8.0) & (level <= 7.0)
    slope[...] = jnp.where(inside, level - ratio, jnp.clip(level, -8.0, 7.0)).T
    within[...] = jnp.where(inside, 1.0, 0.0).T
    share_rows = pl.ds(pl.multiple_of(chip * CHIP_ROWS - window + core * share, 8), share)
    chunk_far(0)
    chunk_second(0, 0)
    ring_step(1, 2)
    ring_step(0, 3)

    row = lax.broadcasted_iota(jnp.int32, (moved_ref.shape[0], entries), 0).astype(jnp.float32)
    covers = (target_row == member) & (row >= target_start) & (row < target_start + length_row)
    take_from = (
        jnp.where(source_row == member, source_start, outbox_start + float(count_in)) - target_start
    )
    wanted = jnp.sum(jnp.where(covers, take_from + row, 0.0), axis=1, keepdims=True)
    entry = (lax.broadcasted_iota(jnp.int32, (1, entries), 1) + 1).astype(jnp.float32)
    image = jnp.sum(jnp.where(covers, entry, 0.0), axis=1, keepdims=True)
    wanted = jnp.where(image > 0.0, wanted, -1.0)
    column_id_ref[...] = image
    row_lane = lax.broadcasted_iota(jnp.int32, (entries, moved_ref.shape[0]), 1).astype(jnp.float32)
    covers_turned = (
        (target_col[:, :1] == member)
        & (row_lane >= target_start_col)
        & (row_lane < target_start_col + length_col[:, :1])
    )
    entry_down = (lax.broadcasted_iota(jnp.int32, (entries, 1), 0) + 1).astype(jnp.float32)
    row_id_ref[...] = jnp.sum(jnp.where(covers_turned, entry_down, 0.0), axis=0, keepdims=True)

    def arrive(step, carry):
        slot = lax.rem(b + step, 32)

        @pl.when(slot < PIECES)
        def _():
            back_copy(b, slot).wait_recv()

        return carry

    lax.fori_loop(1, 32, arrive, 0)
    for i in range(4):
        for j in range(5):
            rows_in[pl.ds(count_in + 32 * i, 32), pl.ds(128 * j, 128)] = arrived[5 * i + j]
    choose = lax.broadcasted_iota(
        jnp.int32, (moved_ref.shape[0], count_in + MOVE_ROWS), 1
    ).astype(jnp.float32)
    moved_ref[...] = jnp.dot(
        jnp.where(wanted == choose, 1.0, 0.0).astype(jnp.bfloat16),
        rows_in[...],
        preferred_element_type=jnp.float32,
    ).astype(jnp.bfloat16)
    chunk_second(0, 1)
    chunk_start(1)
    ring_step(1, 3)
    ring_step(0, 4)
    lax.fori_loop(0, 4, embed_part, 0)
    chunk_second(0, 2)
    chunk_first(1)
    ring_step(1, 4)
    ring_step(0, 5)
    lax.fori_loop(4, 7, embed_part, 0)
    chunk_second(0, 3)
    chunk_far(1)
    chunk_second(1, 0)
    ring_step(1, 5)
    ring_step(0, 6)
    lax.fori_loop(0, 4, norm_part, 0)
    chunk_second(1, 1)
    for index in range(4):
        chunk_last(0, index)
    ring_step(1, 6)
    ring_step(0, 7)
    lax.fori_loop(4, 8, norm_part, 0)
    chunk_second(1, 2)
    ring_step(1, 7)
    ring_step(0, 8)
    chunk_second(1, 3)
    ring_step(1, 8)
    for index in range(4):
        chunk_last(1, index)

    def project(which, chunk):
        q = quad_of(which, chunk)
        for pair in range(2):
            block = main[pl.ds(4 * q + 2 * pair, 2)].reshape(256, D)
            part_main[4 * q // 2 + pair] = lax.dot_general(
                normed[...], block, (((1,), (1,)), ((), ())), preferred_element_type=jnp.float32
            ).astype(jnp.bfloat16)

    def pair_wait(chunk):
        for index in range(4):
            for second in range(4):
                pair_copy(1 - core, chunk, index, second).wait_recv()

    project(core, 0)
    pair_wait(0)
    project(1 - core, 0)
    project(core, 1)
    pair_wait(1)
    project(1 - core, 1)
    for way in range(2):
        for step in range(1, last[way] + 1):
            hand_copy(1 - core, way, step).wait_recv()
    for part in range(3):
        part_rest[:, 256 * part : 256 * part + 256] = lax.dot_general(
            normed[...],
            rest[pl.ds(256 * part, 256), :],
            (((1,), (1,)), ((), ())),
            preferred_element_type=jnp.float32,
        ).astype(jnp.bfloat16)
    joined = []
    for plane in range(16):
        joined.append(part_main[plane // 2, :, 128 * (plane % 2) : 128 * (plane % 2) + 128])
        joined.append(part_rest[:, REST_PAD * plane : REST_PAD * plane + SHARD - MAIN])
    projected_ref[...] = jnp.concatenate(joined, axis=1)

    loads[7].wait()
    width = HEADS * HEAD
    score_scale = HEAD ** (-0.5)
    grad_factor = 1.0 / math.sqrt(131072.0)
    column_id = column_id_ref[...]
    row_id = row_id_ref[...]
    active = column_id > 0.0
    same = (column_id == row_id) & active
    grad_out[...] = jnp.where(
        active, cotangent_ref[...].astype(jnp.float32) * grad_factor, 0.0
    ).astype(jnp.bfloat16)
    attended[...] = jnp.zeros_like(attended)
    grad_projected[...] = jnp.zeros_like(grad_projected)
    by_rows = (((1,), (1,)), ((), ()))
    by_columns = (((0,), (0,)), ((), ()))

    def dot(left, right, contract=(((1,), (0,)), ((), ()))):
        return lax.dot_general(left, right, contract, preferred_element_type=jnp.float32)

    for head in range(HEADS):
        start = HEAD * head // 128 * 128
        stop = -(-(HEAD * head + HEAD) // 128) * 128
        span = stop - start
        lane = lax.broadcasted_iota(jnp.int32, (1, span), 1) + start
        own = (lane >= HEAD * head) & (lane < HEAD * head + HEAD)

        def window(ref, base=0):
            return ref[:, base + start : base + stop]

        def masked(value):
            return jnp.where(own, value, jnp.zeros_like(value))

        queries, keys, values = (window(projected_ref, width * i) for i in range(3))
        out = window(grad_out)
        keys, values = masked(keys), masked(values)
        scores = dot(queries, keys, by_rows) * score_scale
        exponent = jnp.where(same, jnp.exp(scores), 0.0)
        denominator = jnp.sum(exponent, axis=1, keepdims=True)
        attention = exponent / jnp.where(active, denominator, 1.0)
        soft = attention.astype(jnp.bfloat16)
        attended[:, start:stop] += dot(soft, values)
        grad_attention = dot(out, values, by_rows)
        inner = jnp.sum(attention * grad_attention, axis=1, keepdims=True)
        grad_score = (attention * (grad_attention - inner) * score_scale).astype(jnp.bfloat16)
        grad_projected[:, start:stop] += dot(grad_score, keys)
        grad_projected[:, width + start : width + stop] += dot(
            grad_score, masked(queries), by_columns
        )
        grad_projected[:, 2 * width + start : 2 * width + stop] += dot(
            soft, masked(out), by_columns
        )
    attended_ref[...] = attended[...].astype(jnp.bfloat16)
    rounded = grad_projected[...].astype(jnp.bfloat16)
    pad = jnp.zeros((rounded.shape[0], REST_PAD - SHARD + MAIN), jnp.bfloat16)
    mains, rests = [], []
    for plane in range(16):
        base = SHARD * plane
        mains.append(rounded[:, base : base + MAIN])
        rests.append(rounded[:, base + MAIN : base + SHARD])
        rests.append(pad)
    grad_main[...] = jnp.concatenate(mains, axis=1)
    grad_rest[...] = jnp.concatenate(rests, axis=1)

    def back_part(part, carry):
        lanes = pl.ds(pl.multiple_of(part * 256, 128), 256)
        grad_normed[:, lanes] = dot(
            grad_main[...], main[:, :, lanes].reshape(16 * MAIN, 256)
        ) + dot(grad_rest[...], rest[:, lanes])
        return carry

    lax.fori_loop(0, 7, back_part, 0)

    def back_norm_part(part, carry):
        rows = pl.ds(pl.multiple_of(part * 32, 32), 32)
        values = embedded_ref[rows, :].astype(jnp.float32)
        centered = values - jnp.mean(values, axis=1, keepdims=True)
        variance = jnp.mean(centered * centered, axis=1, keepdims=True)
        inverse = lax.rsqrt(variance + EPSILON)
        hat = centered * inverse
        gained = grad_normed[rows, :] * gain_ref[...]
        result = inverse * (
            gained
            - jnp.mean(gained, axis=1, keepdims=True)
            - hat * jnp.mean(gained * hat, axis=1, keepdims=True)
        )
        grad_embedded[rows, :] = jnp.where(column_id_ref[rows, :] > 0.0, result, 0.0).astype(
            jnp.bfloat16
        )
        return carry

    lax.fori_loop(0, 8, back_norm_part, 0)
    first = x * (1 - core) + y * core
    second = y * (1 - core) + x * core
    parts = ((0, 256), (256, 256), (512, 128))

    def chip_of(which, f, s):
        return (s * 4 + f) * (1 - which) + (f * 4 + s) * which

    def target_chip(which, a, half):
        mine = x * (1 - which) + y * which
        f = lax.rem(mine + a, 4)
        return chip_of(which, f, 2 * half + lax.rem(f + which, 2))

    def at(f, s):
        return (z, chip_of(core, f, s) * 2 + core)

    def columns(k):
        return pl.ds(*parts[k])

    def wide(value):
        return value.astype(jnp.float32)

    def twin_copy(a, half, k):
        return remote(
            grad_ref.at[target_chip(1 - core, a, half), :, columns(k)],
            twin.at[a, half, :, columns(k)],
            twin_send.at[a, half, k],
            twin_recv.at[a, half, k],
            (z, sibling),
        )

    def across_copy(a, k):
        return remote(
            held.at[a, :, :, columns(k)],
            across.at[a, :, :, columns(k)],
            across_send.at[a, k],
            across_recv.at[a, k],
            at(lax.rem(first + a, 4), second),
        )

    order = (2, 1, 3, 0)
    spread = range(len(parts))
    for k in spread:
        for part in range(2):
            block = dot(
                grad_embedded[:, 896 * part : 896 * part + 896], moved_ref[:, columns(k)], by_columns
            )
            grad_ref[8 * part : 8 * part + 8, :, columns(k)] = block.astype(jnp.bfloat16).reshape(
                8, CHIP_ROWS, parts[k][1]
            )
        for a in order:
            for half in range(2):
                twin_copy(a, half, k).start()
    for k in spread:
        for a in order:
            for half in range(2):
                twin_copy(a, half, k).wait_recv()
                chip_here = target_chip(core, a, half)
                held[a, half, :, columns(k)] = (
                    wide(grad_ref[chip_here, :, columns(k)]) + wide(twin[a, half, :, columns(k)])
                ).astype(jnp.bfloat16)
            if a > 0 and k == 0:
                across_copy(a, k).start()

    parity = lax.rem(first + core, 2)
    owner = lax.rem(first + second, 2) == core

    def line_copy(half, k):
        to = 2 * half + parity
        away = lax.rem(to - second + 4, 4)
        return remote(
            line.at[half, :, columns(k)],
            met.at[away, :, columns(k)],
            line_send.at[half, k],
            line_recv.at[away, k],
            at(first, to),
        )

    for k in spread:
        for a in (2, 1, 3):
            across_copy(a, k).wait_send()
            if k + 1 < len(parts):
                across_copy(a, k + 1).start()
        for a in (1, 3, 2):
            across_copy(a, k).wait_recv()
        for half in range(2):
            line[half, :, columns(k)] = (
                wide(held[0, half, :, columns(k)])
                + wide(across[1, half, :, columns(k)])
                + wide(across[2, half, :, columns(k)])
                + wide(across[3, half, :, columns(k)])
            ).astype(jnp.bfloat16)

            @pl.when(2 * half + parity != second)
            def _():
                line_copy(half, k).start()

    def tile_copy(index, k):
        return remote(
            summed.at[pl.ds(16 * index, 16), columns(k)],
            tiles.at[z, :, columns(k)],
            tile_send.at[index, k],
            tile_recv.at[z, k],
            (2 * index, b),
        )

    for k in spread:

        @pl.when(owner)
        def _():
            mine = wide(line[second // 2, :, columns(k)])
            for away in (1, 3, 2):
                remote(
                    line.at[0, :, columns(k)],
                    met.at[away, :, columns(k)],
                    line_send.at[0, k],
                    line_recv.at[away, k],
                    (z, sibling),
                ).wait_recv()
                mine = mine + wide(met[away, :, columns(k)])
            summed[:, columns(k)] = mine.astype(jnp.bfloat16)
            for index in range(7):

                @pl.when(z != 2 * index)
                def _():
                    tile_copy(index, k).start()

    collector = owner & (z < 14) & (lax.rem(z, 2) == 0)
    tile_index = jnp.minimum(z // 2, 6)

    def total_copy(step, which, k):
        return remote(
            total.at[tile_index, :, columns(k)],
            total.at[tile_index, :, columns(k)],
            total_send.at[step, which, k],
            total_recv.at[tile_index, k],
            (lax.rem(z + step, 16), chip * 2 + which),
        )

    def total_goes(step, which):
        wanted_there = (tile_index <= 3) if which == 0 else (tile_index >= 3)
        return wanted_there & ((step != 0) | (core != which))

    for k in spread:

        @pl.when(collector)
        def _():
            tile_rows = pl.ds(pl.multiple_of(16 * tile_index, 16), 16)
            tiles[z, :, columns(k)] = summed[tile_rows, columns(k)]

            def take(step, carry):
                slot = lax.rem(z + step, 16)
                remote(
                    summed.at[pl.ds(0, 16), columns(k)],
                    tiles.at[slot, :, columns(k)],
                    tile_send.at[0, k],
                    tile_recv.at[slot, k],
                    (slot, b),
                ).wait_recv()
                return carry

            lax.fori_loop(1, 16, take, 0)
            value = wide(tiles[0, :, columns(k)])
            for slot in range(1, 16):
                value = value + wide(tiles[slot, :, columns(k)])
            total[tile_index, :, columns(k)] = value.astype(jnp.bfloat16)

            def give(step, carry):
                for which in range(2):

                    @pl.when(total_goes(step, which))
                    def _():
                        total_copy(step, which, k).start()

                return carry

            lax.fori_loop(0, 16, give, 0)

    for k in spread:
        for j in range(4):
            index = 3 * core + j

            @pl.when(jnp.logical_not(owner & (z == 2 * index)))
            def _():
                remote(
                    total.at[index, :, columns(k)],
                    total.at[index, :, columns(k)],
                    total_send.at[0, 0, k],
                    total_recv.at[index, k],
                    (z, sibling),
                ).wait_recv()

    final[...] = wide(total[pl.ds(3 * core, 4)]).reshape(64, PIX_PAD)
    mine = final[pl.ds(pl.multiple_of(core * 8, 8), share), pl.ds(0, PIX)]
    latent_out[...] = jnp.where(within[share_rows, :] > 0.0, mine, 0.0)
    scale_out[...] = (1.0 / math.sqrt(PIX * 7.0)) * jnp.sum(mine * slope[share_rows, :], axis=1)

    for k in spread:
        for a in range(4):
            for half in range(2):
                twin_copy(a, half, k).wait_send()
        for half in range(2):

            @pl.when(2 * half + parity != second)
            def _():
                line_copy(half, k).wait_send()

        @pl.when(owner)
        def _():
            for index in range(7):

                @pl.when(z != 2 * index)
                def _():
                    tile_copy(index, k).wait_send()

        @pl.when(collector)
        def _():
            def given(step, carry):
                for which in range(2):

                    @pl.when(total_goes(step, which))
                    def _():
                        total_copy(step, which, k).wait_send()

                return carry

            lax.fori_loop(0, 16, given, 0)

    for step in range(1, 16):

        @pl.when(z_mine(step))
        def _():
            z_copy(step).wait_send()

    for way in range(2):
        for step in range(1, last[way] + 1):
            for part in range(2):
                ring_copy(way, step, part).wait_send()
            hand_copy(core, way, step).wait_send()

    def sent_out(step, carry):
        target = lax.rem(b + step, 32)

        @pl.when(target < PIECES)
        def _():
            out_copy(target, b).wait_send()

        return carry

    lax.fori_loop(1, 32, sent_out, 0)

    @pl.when(b < PIECES)
    def _():
        def sent_back(step, carry):
            back_copy(lax.rem(b + step, 32), b).wait_send()
            return carry

        lax.fori_loop(1, 32, sent_back, 0)

    for chunk in range(2):
        for kind in range(4):
            first_copy(chunk, kind).wait_send()
            for index in range(4):
                second_copy(chunk, index, kind).wait_send()
        for index in range(4):
            for second in range(4):
                pair_copy(core, chunk, index, second).wait_send()


def deliver_kernel(attended, latent, scale, attended_out, latent_out, scale_out):
    attended_out[...] = attended[...]
    latent_out[...] = latent[...]
    scale_out[...] = scale[...]


def deliver(*arrays):
    vmem = pl.BlockSpec(memory_space=pltpu.VMEM)
    return pl.pallas_call(
        deliver_kernel,
        name="deliver",
        out_shape=tuple(jax.ShapeDtypeStruct(a.shape, a.dtype) for a in arrays),
        in_specs=[vmem] * 3,
        out_specs=(vmem,) * 3,
    )(*arrays)


def whole(weight, latent, scale, bias, gain, shift, pixels, cotangent, length, source, target):
    vmem = pl.BlockSpec(memory_space=pltpu.VMEM)
    anywhere = pl.BlockSpec(memory_space=pl.ANY)
    dma = pltpu.SemaphoreType.DMA
    rows = cotangent.shape[0]
    block = (CHIP_ROWS, PIX_PAD)
    shape = jax.ShapeDtypeStruct
    return pl.pallas_call(
        whole_kernel,
        name="whole",
        out_shape=(
            shape((rows, HEADS * HEAD), jnp.bfloat16),
            shape((D // 32, PIX), jnp.float32),
            shape((D // 32,), jnp.float32),
        ),
        in_specs=[anywhere] * 8 + [vmem] * 3,
        out_specs=(vmem, vmem, vmem),
        scratch_shapes=[
            pltpu.VMEM((SHARD, D), jnp.bfloat16),
            pltpu.VMEM((PIX, D), jnp.bfloat16),
            pltpu.VMEM((8, D), jnp.float32),
            pltpu.VMEM(pixels.shape, jnp.bfloat16),
            pltpu.VMEM(cotangent.shape, jnp.bfloat16),
            pltpu.VMEM((1, 128), jnp.int32),
            pltpu.SMEM((1, 128), jnp.int32),
            pltpu.VMEM((256, PIX), jnp.float32),
            pltpu.VMEM((256, PIX), jnp.float32),
            pltpu.VMEM((rows, PIX_PAD), jnp.bfloat16),
            pltpu.VMEM((rows, D), jnp.bfloat16),
            pltpu.VMEM((rows, 16 * SHARD), jnp.bfloat16),
            pltpu.VMEM((rows, 1), jnp.float32),
            pltpu.VMEM((1, rows), jnp.float32),
            pltpu.VMEM((16, MAIN, D), jnp.bfloat16),
            pltpu.VMEM((16 * REST_PAD, D), jnp.bfloat16),
            pltpu.VMEM((pixels.shape[0] + MOVE_ROWS, PIX_PAD), jnp.bfloat16),
            pltpu.VMEM((PIECES, 32, 128), jnp.bfloat16),
            pltpu.VMEM((32, 32, 128), jnp.bfloat16),
            pltpu.VMEM((32, 32, 128), jnp.bfloat16),
            pltpu.VMEM((PIECES, 32, 128), jnp.bfloat16),
            pltpu.VMEM((PIX_PAD, D), jnp.bfloat16),
            pltpu.VMEM((rows, D), jnp.bfloat16),
            pltpu.VMEM((8, rows, 256), jnp.bfloat16),
            pltpu.VMEM((rows, 16 * REST_PAD), jnp.bfloat16),
            pltpu.VMEM((rows, HEADS * HEAD), jnp.bfloat16),
            pltpu.VMEM((rows, HEADS * HEAD), jnp.float32),
            pltpu.VMEM((rows, 16 * SHARD), jnp.float32),
            pltpu.VMEM((rows, 16 * MAIN), jnp.bfloat16),
            pltpu.VMEM((rows, 16 * REST_PAD), jnp.bfloat16),
            pltpu.VMEM((rows, D), jnp.float32),
            pltpu.VMEM((rows, D), jnp.bfloat16),
            pltpu.VMEM((D // CHIP_ROWS,) + block, jnp.bfloat16),
            pltpu.VMEM((4, 2) + block, jnp.bfloat16),
            pltpu.VMEM((4, 2) + block, jnp.bfloat16),
            pltpu.VMEM((4, 2) + block, jnp.bfloat16),
            pltpu.VMEM((2,) + block, jnp.bfloat16),
            pltpu.VMEM((4,) + block, jnp.bfloat16),
            pltpu.VMEM((16, 16, PIX_PAD), jnp.bfloat16),
            pltpu.VMEM((7, 16, PIX_PAD), jnp.bfloat16),
            pltpu.VMEM(block, jnp.bfloat16),
            pltpu.VMEM((64, PIX_PAD), jnp.float32),
            dma((9,)),
            dma((16,)),
            dma((16,)),
            dma((2, 9, 2)),
            dma((2, 9, 2)),
            dma((2, 9)),
            dma((2, 9)),
            dma((32,)),
            dma((32,)),
            dma((32,)),
            dma((32,)),
            dma((2, 20)),
            dma((2, 20)),
            dma((2, 16)),
            dma((2, 16)),
            dma((4, 2, 3)),
            dma((4, 2, 3)),
            dma((4, 3)),
            dma((4, 3)),
            dma((2, 3)),
            dma((4, 3)),
            dma((7, 3)),
            dma((16, 3)),
            dma((16, 2, 3)),
            dma((7, 3)),
        ],
        compiler_params=pltpu.CompilerParams(
            collective_id=0, has_side_effects=True, vmem_limit_bytes=58 * 1024 * 1024
        ),
    )(weight, latent, scale, bias, gain, shift, pixels, cotangent, length, source, target)


def per_device(
    pixels,
    latent,
    quant_scale,
    embed_bias,
    ln_gain,
    ln_bias,
    qkv_weight,
    cotangent,
    image_length,
    image_source,
    image_target,
):
    results = whole(
        qkv_weight.T,
        latent.T,
        quant_scale,
        embed_bias,
        ln_gain,
        ln_bias,
        pixels,
        cotangent,
        image_length,
        image_source,
        image_target,
    )
    return deliver(*results)


def solution(mesh):
    placed = (
        P(("dp", "bal"), None),
        P(),
        P(),
        P(),
        P(),
        P(),
        P(None, "dp"),
        P(("dp", "bal"), None),
        P("dp", None),
        P("dp", None),
        P("dp", None),
    )
    return jax.shard_map(
        per_device,
        mesh=mesh,
        in_specs=placed,
        out_specs=(P(("dp", "bal"), None), P("bal", None), P("bal")),
        check_vma=False,
    )
```
